32 devices in a mesh: clip: 4 (over y, x), space: 8 (over z, core).
Axes of the slice: x: 2, y: 2, z: 4, core: 2. Of those that a mesh axis runs over, the one named last changes fastest.
Arguments:
- clip_input: bfloat16 [16, 16, 14, 14, 1024], P('clip', 'space'), may hold values from -6 to 6
- frame_counts: int32 [16], P('clip'), may hold values from 2 to 16, as said below
- third_down: bfloat16 [1024, 256], replicated, may hold values from -0.1875 to 0.1875
- third_depth: float32 [256, 27], replicated, may hold values from -1.25 to 1.25
- third_up: bfloat16 [256, 1024], replicated, may hold values from -0.375 to 0.375
- third_gain: float32 [1024], replicated, may hold values from 0.25 to 1.75
- third_shift: float32 [1024], replicated, may hold values from -3 to 3
- fourth_down: bfloat16 [1024, 512], replicated, may hold values from -0.1875 to 0.1875
- fourth_skip: bfloat16 [1024, 2048], replicated, may hold values from -0.1875 to 0.1875
- fourth_depth: float32 [512, 27], replicated, may hold values from -1.25 to 1.25
- fourth_up: bfloat16 [512, 2048], replicated, may hold values from -0.25 to 0.25
- fourth_gain: float32 [2048], replicated, may hold values from 0.25 to 1.75
- fourth_shift: float32 [2048], replicated, may hold values from -3 to 3
- classifier: bfloat16 [2048, 400], replicated, may hold values from -0.125 to 0.125
- class_bias: float32 [400], replicated, may hold values from -3 to 3
- logit_grad: float32 [16, 400], replicated, may hold values from -6 to 6
Outputs:
- logits: float32 [16, 400], P('clip')
- clip_grad: bfloat16 [16, 16, 14, 14, 1024], P('clip', 'space')
- third_down_grad: float32 [1024, 256], P(('clip', 'space'))
- third_depth_grad: float32 [256, 27], P(('clip', 'space'))
- third_up_grad: float32 [256, 1024], P(('clip', 'space'))
- third_gain_grad: float32 [1024], P(('clip', 'space'))
- third_shift_grad: float32 [1024], P(('clip', 'space'))
- fourth_down_grad: float32 [1024, 512], P(('clip', 'space'))
- fourth_skip_grad: float32 [1024, 2048], P(('clip', 'space'))
- fourth_depth_grad: float32 [512, 27], P(('clip', 'space'))
- fourth_up_grad: float32 [512, 2048], P(('clip', 'space'))
- fourth_gain_grad: float32 [2048], P(('clip', 'space'))
- fourth_shift_grad: float32 [2048], P(('clip', 'space'))
- classifier_grad: float32 [2048, 400], P(('clip', 'space'))
- class_bias_grad: float32 [400], replicated
The draws below stay inside these ranges and needn't reach their ends.
Inputs may be any that keep to these rules, and one draw needn't show every extreme that they name: `frame_counts`: in each group of 4 clips one clip has exactly 16 frames.
All inputs are finite; a program needn't handle non-finite values.
Results may differ from the reference program's by a relative error of at most 0.014.
Values may be sent and summed in bfloat16 or wider, within the bound.
No kernel may reach another device: no remote copies, remote signals or barrier semaphores. Data moves between devices by JAX's collectives and lax.ppermute only.
A program may use at most 128 MiB of HBM per device.

```python
import jax
import jax.numpy as jnp
from jax import lax

C3 = 1024
B3 = 256
C4 = 2048
B4 = 512
NCLS = 400
H = 14
CLIPS = 4
FRAMES = 16
CLIPS_ALL = 16
N_CLIP = 4


def draw_frame_counts(key, part):
    low_count = max(FRAMES // 8, 2)
    groups = CLIPS_ALL // CLIPS
    counts = jax.random.randint(jax.random.fold_in(key, 11), (groups, CLIPS), low_count, FRAMES + 1)
    chosen = jax.random.randint(jax.random.fold_in(key, 12), (groups, 1), 0, CLIPS)
    longest = jnp.arange(CLIPS, dtype=jnp.int32)[None, :] == chosen
    counts = jnp.where(longest, FRAMES, counts)
    return counts.reshape(CLIPS_ALL).astype(jnp.int32)


def block_scale(rng, dims, pieces, least, top_value):
    loudness = 1.0
    for axis_at, parts in pieces:
        steps = jax.random.uniform(jax.random.fold_in(jax.random.fold_in(rng, 6), axis_at), (parts,), jnp.float32, least / len(pieces), top_value / len(pieces))
        loudness = loudness * jnp.repeat(jnp.exp(steps), dims[axis_at] // parts).reshape((-1,) + (1,) * (len(dims) - 1 - axis_at))
    return loudness


def gaussian(stream_key, dims, deviation, bound, split=(), held_as=jnp.bfloat16):
    result = deviation * jax.random.normal(stream_key, dims, jnp.float32)
    if split:
        result = result * block_scale(stream_key, dims, split, -0.22, 0.18)
    return jnp.clip(result, -bound, bound).astype(held_as)


def setup_inputs(seed: int = 0) -> dict:
    key_list = jax.random.split(jax.random.key(seed), 17)
    clip_input = gaussian(key_list[0], (CLIPS_ALL, FRAMES, H, H, C3), 1.0, 6.0, ((0, 4), (1, 8)))
    frame_counts = draw_frame_counts(jax.random.fold_in(key_list[16], 71), 0)
    third_down = gaussian(key_list[2], (C3, B3), C3 ** -0.5, 0.1875)
    third_depth = gaussian(key_list[3], (B3, 27), 27 ** -0.5, 1.25, (), jnp.float32)
    third_up = gaussian(key_list[4], (B3, C3), B3 ** -0.5, 0.375)
    third_gain = jnp.clip(1.0 + 0.15 * jax.random.normal(key_list[5], (C3,), jnp.float32), 0.25, 1.75)
    third_shift = gaussian(key_list[6], (C3,), 0.5, 3.0, (), jnp.float32)
    fourth_down = gaussian(key_list[7], (C3, B4), C3 ** -0.5, 0.1875)
    fourth_skip = gaussian(key_list[8], (C3, C4), C3 ** -0.5, 0.1875)
    fourth_depth = gaussian(key_list[9], (B4, 27), 27 ** -0.5, 1.25, (), jnp.float32)
    fourth_up = gaussian(key_list[10], (B4, C4), B4 ** -0.5, 0.25)
    fourth_gain = jnp.clip(1.0 + 0.15 * jax.random.normal(key_list[11], (C4,), jnp.float32), 0.25, 1.75)
    fourth_shift = gaussian(key_list[12], (C4,), 0.5, 3.0, (), jnp.float32)
    classifier = gaussian(key_list[13], (C4, NCLS), C4 ** -0.5, 0.125)
    class_bias = gaussian(key_list[14], (NCLS,), 0.5, 3.0, (), jnp.float32)
    logit_grad = gaussian(key_list[15], (CLIPS_ALL, NCLS), 1.0, 6.0, (), jnp.float32)
    return {"clip_input": clip_input, "frame_counts": frame_counts, "third_down": third_down, "third_depth": third_depth, "third_up": third_up, "third_gain": third_gain, "third_shift": third_shift, "fourth_down": fourth_down, "fourth_skip": fourth_skip, "fourth_depth": fourth_depth, "fourth_up": fourth_up, "fourth_gain": fourth_gain, "fourth_shift": fourth_shift, "classifier": classifier, "class_bias": class_bias, "logit_grad": logit_grad}


eps = 1e-05

@jax.custom_vjp
def low(v):
    return lax.optimization_barrier(v.astype(jnp.bfloat16)).astype(jnp.float32)

@jax.custom_vjp
def low_back(v):
    return v

def low_keep(v):
    return (low(v), None)

def low_pass(kept, grad):
    return (grad,)

def back_keep(v):
    return (v, None)

def back_low(kept, grad):
    return (low(grad),)
low.defvjp(low_keep, low_pass)
low_back.defvjp(back_keep, back_low)

def depthwise(source, kernel):
    frames, height, breadth = (source.shape[1], source.shape[2], source.shape[3])
    padded = jnp.pad(source, ((0, 0), (1, 1), (1, 1), (1, 1), (0, 0)))
    running = jnp.zeros(source.shape, jnp.float32)
    for lag_t in range(3):
        for lag_h in range(3):
            for lag_w in range(3):
                running = running + padded[:, lag_t:lag_t + frames, lag_h:lag_h + height, lag_w:lag_w + breadth, :] * kernel[:, lag_t * 9 + lag_h * 3 + lag_w]
    return running

def project(source, weight):
    return jnp.einsum('kfhwc,cd->kfhwd', source, weight, precision=lax.Precision.HIGHEST)

def batch_norm(values, masks, gain, shift):
    voxel_count = jnp.sum(masks) * values.shape[2] * values.shape[3]
    center = lax.optimization_barrier(jnp.sum(values * masks, axis=(0, 1, 2, 3))) / voxel_count
    spread = lax.optimization_barrier(jnp.sum(values * values * masks, axis=(0, 1, 2, 3))) / voxel_count - center * center
    return (values - center) * lax.rsqrt(spread + eps) * gain + shift

def group_pool(source, counts, params):
    third_down, third_depth, third_up, third_gain, third_shift, fourth_down, fourth_skip, fourth_depth, fourth_up, fourth_gain, fourth_shift = params
    frames = source.shape[1]
    frame_mask = (jnp.arange(frames, dtype=jnp.int32)[None, :] < counts[:, None]).astype(jnp.float32)[:, :, None, None, None]
    first_pre = low_back(project(source, third_down))
    first_act = low(jax.nn.gelu(first_pre) * frame_mask)
    mid_pre = low_back(depthwise(first_act, third_depth))
    mid_act = low(jax.nn.gelu(mid_pre))
    third_sum = low_back(project(mid_act, third_up))
    third_out = source + batch_norm(third_sum, frame_mask, third_gain, third_shift)
    late_entry = low(third_out[:, ::2, ::2, ::2, :])
    late_mask = (2 * jnp.arange(frames // 2, dtype=jnp.int32)[None, :] < counts[:, None]).astype(jnp.float32)[:, :, None, None, None]
    late_first = low_back(project(late_entry, fourth_down))
    late_act = low(jax.nn.gelu(late_first) * late_mask)
    late_mid = low_back(depthwise(late_act, fourth_depth))
    late_mid_act = low(jax.nn.gelu(late_mid))
    late_sum = low(low_back(project(late_mid_act, fourth_up)))
    skipped = low(low_back(project(late_entry, fourth_skip)))
    late_post = jax.nn.gelu(batch_norm(late_sum, late_mask, fourth_gain, fourth_shift) + skipped)
    pool_count = lax.optimization_barrier(jnp.sum(late_mask, axis=(1, 2, 3, 4))) * late_entry.shape[2] * late_entry.shape[3]
    pooled = lax.optimization_barrier(jnp.sum(late_post * late_mask, axis=(1, 2, 3))) / pool_count[:, None]
    return low(low_back(pooled))

def reference(clip_input, frame_counts, third_down, third_depth, third_up, third_gain, third_shift, fourth_down, fourth_skip, fourth_depth, fourth_up, fourth_gain, fourth_shift, classifier, class_bias, logit_grad):
    params = tuple((member.astype(jnp.float32) for member in (third_down, third_depth, third_up, third_gain, third_shift, fourth_down, fourth_skip, fourth_depth, fourth_up, fourth_gain, fourth_shift)))
    head = classifier.astype(jnp.float32)

    def forward(clip_values, params_in, head_in, bias_in):
        groups = clip_values.reshape((N_CLIP, CLIPS) + clip_values.shape[1:])
        counts = frame_counts.reshape(N_CLIP, CLIPS)

        def one_group(members):
            return group_pool(members[0].astype(jnp.float32), members[1], params_in)
        pooled = lax.map(jax.checkpoint(one_group), (groups, counts))
        pooled = pooled.reshape(CLIPS_ALL, pooled.shape[-1])
        return jnp.dot(pooled, head_in, precision=lax.Precision.HIGHEST) + bias_in
    logits, pullback = jax.vjp(forward, clip_input, params, head, class_bias)
    clip_grad, param_grads, head_grad, bias_grad = pullback(logit_grad)
    return (logits, clip_grad, param_grads[0], param_grads[1], param_grads[2], param_grads[3], param_grads[4], param_grads[5], param_grads[6], param_grads[7], param_grads[8], param_grads[9], param_grads[10], head_grad, bias_grad)
```

```python
import jax
import jax.numpy as jnp
from jax import lax
from jax.sharding import PartitionSpec as P

eps = 1e-05


def extended(array, sides, width):
    for axis, dim in sides:
        size, length = (lax.axis_size(axis), array.shape[dim])
        up = [(i, (i + 1) % size) for i in range(size - 1)]
        down = [(j, i) for i, j in up]
        last = lax.slice_in_dim(array, length - width, length, axis=dim)
        first = lax.slice_in_dim(array, 0, width, axis=dim)
        before = lax.ppermute(last, axis, up)
        after = lax.ppermute(first, axis, down)
        array = jnp.concatenate([before, array, after], axis=dim)
    return array


def gelu_pair(values):
    result, pullback = jax.vjp(jax.nn.gelu, values)
    return (result, pullback(jnp.ones_like(values))[0])


def spread_rows(source):
    return jnp.pad(source, ((0, 0), (0, 0), (1, 1), (1, 1), (0, 0)))


def depth_conv(padded, kernel):
    channels = kernel.shape[0]
    filters = jnp.transpose(kernel).reshape(3, 3, 3, 1, channels)
    return lax.conv_general_dilated(
        padded,
        filters,
        (1, 1, 1),
        "VALID",
        dimension_numbers=("NDHWC", "DHWIO", "NDHWC"),
        feature_group_count=channels,
        precision=lax.Precision.HIGHEST,
    )


def depthwise(padded, kernel):
    return depth_conv(padded.astype(jnp.float32), kernel)


def depthwise_back(padded, kernel):
    return depth_conv(padded.astype(jnp.float32), kernel[:, ::-1])


def kernel_grad(padded, gradient, kernel):
    padded_wide = padded.astype(jnp.float32)
    _, pullback = jax.vjp(lambda weights: depth_conv(padded_wide, weights), kernel)
    return pullback(gradient.astype(jnp.float32))[0]


def contract_rows(left, right):
    return lax.dot_general(
        left, right, (((0, 1, 2, 3), (0, 1, 2, 3)), ((), ())), preferred_element_type=jnp.float32
    )


def back_project(gradient, weight):
    return lax.dot_general(
        gradient, weight, (((4,), (1,)), ((), ())), preferred_element_type=jnp.float32
    )


def place_even(sparse, frames):
    clip_count, _, half_rows, _, channels = sparse.shape
    even_grid = sparse.reshape(clip_count, 1, half_rows, 1, half_rows, 1, channels)
    even_grid = jnp.pad(even_grid, ((0, 0), (0, 0), (0, 0), (0, 1), (0, 0), (0, 1), (0, 0)))
    even_grid = even_grid.reshape(clip_count, 1, 2 * half_rows, 2 * half_rows, channels)
    return jnp.pad(even_grid, ((0, 0), (0, frames - 1), (0, 0), (0, 0), (0, 0)))


def group_total(values):
    size = lax.axis_size("space")
    copies = jnp.broadcast_to(values[None], (size,) + values.shape)
    received = lax.all_to_all(copies, "space", split_axis=0, concat_axis=0, tiled=True)
    return jnp.sum(received, axis=0)


def reduce_rows(term, axes=("clip", "space")):
    parts = 1
    for axis in axes:
        parts *= lax.axis_size(axis)
    pieces = term.astype(jnp.bfloat16).reshape((parts, term.shape[0] // parts) + term.shape[1:])
    received = lax.all_to_all(pieces, axes, split_axis=0, concat_axis=0, tiled=True)
    return jnp.sum(received.astype(jnp.float32), axis=0)


def per_device(
    clip_input,
    frame_counts,
    third_down,
    third_depth,
    third_up,
    third_gain,
    third_shift,
    fourth_down,
    fourth_skip,
    fourth_depth,
    fourth_up,
    fourth_gain,
    fourth_shift,
    classifier,
    class_bias,
    logit_grad,
):
    clip_count, local_frames, grid_rows = (
        clip_input.shape[0],
        clip_input.shape[1],
        clip_input.shape[2],
    )
    half_rows = grid_rows // 2
    slab_index = lax.axis_index("space")
    late_width = fourth_up.shape[1]
    frame_ids = 2 * slab_index + jnp.arange(local_frames, dtype=jnp.int32)
    frame_mask = (frame_ids[None, :] < frame_counts[:, None]).astype(jnp.float32)[
        :, :, None, None, None
    ]
    third_total = jnp.sum(frame_counts).astype(jnp.float32) * grid_rows * grid_rows
    first_pre = jnp.dot(clip_input, third_down, preferred_element_type=jnp.float32)
    first_gelu, slope_first = gelu_pair(first_pre)
    first_act = (first_gelu * frame_mask).astype(jnp.bfloat16)
    first_pad = spread_rows(extended(first_act, (("space", 1),), 1))
    mid_pre = depthwise(first_pad, third_depth)
    mid_gelu, slope_mid = gelu_pair(mid_pre)
    mid_act = mid_gelu.astype(jnp.bfloat16)
    third_sum = jnp.dot(mid_act, third_up, preferred_element_type=jnp.float32)
    moments = (
        jnp.sum(third_sum * frame_mask, axis=(0, 1, 2, 3)),
        jnp.sum(third_sum * third_sum * frame_mask, axis=(0, 1, 2, 3)),
    )
    moment_one, moment_two = group_total(jnp.stack(moments))
    third_center = moment_one / third_total
    third_scale = lax.rsqrt(moment_two / third_total - third_center * third_center + eps)
    third_hat = (third_sum - third_center) * third_scale
    even_hat = third_hat[:, 0:1, ::2, ::2, :]
    third_even = (
        clip_input[:, 0:1, ::2, ::2, :].astype(jnp.float32) + even_hat * third_gain + third_shift
    )
    late_entry = third_even.astype(jnp.bfloat16)
    late_mask = (2 * slab_index < frame_counts).astype(jnp.float32)[:, None, None, None, None]
    late_first = jnp.dot(late_entry, fourth_down, preferred_element_type=jnp.float32)
    late_gelu, slope_late = gelu_pair(late_first)
    late_act = (late_gelu * late_mask).astype(jnp.bfloat16)
    late_pad = spread_rows(extended(late_act, (("space", 1),), 1))
    late_mid = depthwise(late_pad, fourth_depth)
    late_mid_gelu, slope_late_mid = gelu_pair(late_mid)
    late_mid_act = late_mid_gelu.astype(jnp.bfloat16)
    late_sum = jnp.dot(late_mid_act, fourth_up, preferred_element_type=jnp.float32).astype(
        jnp.bfloat16
    )
    skipped = jnp.dot(late_entry, fourth_skip, preferred_element_type=jnp.float32).astype(
        jnp.bfloat16
    )
    late_counts = (frame_counts + 1) // 2
    pool_count = late_counts.astype(jnp.float32) * half_rows * half_rows
    late_total = jnp.sum(late_counts).astype(jnp.float32) * half_rows * half_rows
    pool_scale = pool_count[:, None, None, None, None]
    sum_values = late_sum.astype(jnp.float32)
    late_moments = group_total(
        jnp.stack(
            (
                jnp.sum(sum_values * late_mask, axis=(0, 1, 2, 3)),
                jnp.sum(sum_values * sum_values * late_mask, axis=(0, 1, 2, 3)),
            )
        )
    )
    late_center = late_moments[0] / late_total
    late_scale = lax.rsqrt(late_moments[1] / late_total - late_center * late_center + eps)
    late_hat = (sum_values - late_center) * late_scale
    late_post, slope_post = gelu_pair(
        late_hat * fourth_gain + fourth_shift + skipped.astype(jnp.float32)
    )
    pooled_term = jnp.sum(late_post * late_mask, axis=(1, 2, 3)) / pool_count[:, None]
    own_start = lax.axis_index("clip") * clip_count
    grad_rows = lax.dynamic_slice_in_dim(logit_grad, own_start, clip_count, 0)
    bias_grad = jnp.sum(logit_grad, axis=0)
    pooled_grad = lax.dot_general(
        grad_rows,
        classifier.astype(jnp.float32),
        (((1,), (1,)), ((), ())),
        precision=lax.Precision.HIGHEST,
    ).astype(jnp.bfloat16)
    pre_grad = (
        pooled_grad.astype(jnp.float32)[:, None, None, None, :] * late_mask / pool_scale * slope_post
    )
    back_one = jnp.sum(pre_grad, axis=(0, 1, 2, 3))
    back_two = jnp.sum(pre_grad * late_hat, axis=(0, 1, 2, 3))
    late_back = group_total(jnp.concatenate((jnp.stack((back_one, back_two)), pooled_term)))
    late_sum_grad = (
        fourth_gain
        * late_scale
        * (pre_grad - late_mask * (late_back[0] + late_hat * late_back[1]) / late_total)
    ).astype(jnp.bfloat16)
    late_skip_grad = pre_grad.astype(jnp.bfloat16)
    pooled = late_back[2:].astype(jnp.bfloat16)
    logits = jnp.dot(pooled, classifier, preferred_element_type=jnp.float32) + class_bias
    all_pooled = lax.all_gather(pooled, "clip", axis=0, tiled=True)
    own_width = late_width // (lax.axis_size("clip") * lax.axis_size("space"))
    own_first = (lax.axis_index("clip") * lax.axis_size("space") + slab_index) * own_width
    classifier_grad = lax.dot_general(
        lax.dynamic_slice_in_dim(all_pooled, own_first, own_width, 1).astype(jnp.float32),
        logit_grad,
        (((0,), (0,)), ((), ())),
        precision=lax.Precision.HIGHEST,
    )
    fourth_up_term = contract_rows(late_mid_act, late_sum_grad)
    late_mid_grad = (back_project(late_sum_grad, fourth_up) * slope_late_mid).astype(jnp.bfloat16)
    late_grad_pad = spread_rows(extended(late_mid_grad, (("space", 1),), 1))
    late_act_grad = depthwise_back(late_grad_pad, fourth_depth)
    fourth_depth_term = kernel_grad(late_pad, late_mid_grad, fourth_depth)
    late_first_grad = (late_act_grad * late_mask * slope_late).astype(jnp.bfloat16)
    fourth_down_term = contract_rows(late_entry, late_first_grad)
    fourth_skip_term = contract_rows(late_entry, late_skip_grad)
    entry_grad = back_project(late_first_grad, fourth_down) + back_project(
        late_skip_grad, fourth_skip
    )
    local_one = jnp.sum(entry_grad * frame_mask[:, 0:1], axis=(0, 1, 2, 3))
    local_two = jnp.sum(entry_grad * even_hat * frame_mask[:, 0:1], axis=(0, 1, 2, 3))
    total_one, total_two = group_total(jnp.stack((local_one, local_two)))
    out_grad = place_even(entry_grad, local_frames)
    third_sum_grad = (
        third_gain
        * third_scale
        * (out_grad - frame_mask * (total_one + third_hat * total_two) / third_total)
    ).astype(jnp.bfloat16)
    third_up_term = contract_rows(mid_act, third_sum_grad)
    mid_grad = (back_project(third_sum_grad, third_up) * slope_mid).astype(jnp.bfloat16)
    mid_grad_pad = spread_rows(extended(mid_grad, (("space", 1),), 1))
    first_act_grad = depthwise_back(mid_grad_pad, third_depth)
    third_depth_term = kernel_grad(first_pad, mid_grad, third_depth)
    first_grad = (first_act_grad * frame_mask * slope_first).astype(jnp.bfloat16)
    third_down_term = contract_rows(clip_input, first_grad)
    clip_grad = (out_grad + back_project(first_grad, third_down)).astype(jnp.bfloat16)
    small = jnp.concatenate((local_two, local_one, back_two, back_one))
    small = lax.psum(small, ("clip", "space"))
    device = lax.axis_index("clip") * lax.axis_size("space") + slab_index
    wide = third_gain.shape[0]
    vectors = []
    for first, size in ((0, wide), (wide, wide), (2 * wide, late_width), (2 * wide + late_width, late_width)):
        piece = size // (late_width // own_width)
        vectors.append(lax.dynamic_slice_in_dim(small, first + device * piece, piece, 0))
    return (
        logits,
        clip_grad,
        reduce_rows(third_down_term),
        reduce_rows(third_depth_term),
        reduce_rows(third_up_term),
        vectors[0],
        vectors[1],
        reduce_rows(fourth_down_term),
        reduce_rows(fourth_skip_term),
        reduce_rows(fourth_depth_term),
        reduce_rows(fourth_up_term),
        vectors[2],
        vectors[3],
        classifier_grad,
        bias_grad,
    )


def solution(mesh):
    return jax.shard_map(
        per_device,
        mesh=mesh,
        in_specs=(
            P("clip", "space", None, None, None),
            P("clip"),
            P(),
            P(),
            P(),
            P(),
            P(),
            P(),
            P(),
            P(),
            P(),
            P(),
            P(),
            P(),
            P(),
            P(),
        ),
        out_specs=(
            P("clip", None),
            P("clip", "space", None, None, None),
            P(("clip", "space"), None),
            P(("clip", "space"), None),
            P(("clip", "space"), None),
            P(("clip", "space")),
            P(("clip", "space")),
            P(("clip", "space"), None),
            P(("clip", "space"), None),
            P(("clip", "space"), None),
            P(("clip", "space"), None),
            P(("clip", "space")),
            P(("clip", "space")),
            P(("clip", "space"), None),
            P(),
        ),
        check_vma=False,
    )
```

```python
import jax
import jax.numpy as jnp
from jax import lax
from jax.sharding import PartitionSpec as P

eps = 1e-05


def extended(array, sides, width):
    for axis, dim in sides:
        size, length = (lax.axis_size(axis), array.shape[dim])
        up = [(i, (i + 1) % size) for i in range(size - 1)]
        down = [(j, i) for i, j in up]
        last = lax.slice_in_dim(array, length - width, length, axis=dim)
        first = lax.slice_in_dim(array, 0, width, axis=dim)
        before = lax.ppermute(last, axis, up)
        after = lax.ppermute(first, axis, down)
        array = jnp.concatenate([before, array, after], axis=dim)
    return array


def gelu_pair(values):
    result, pullback = jax.vjp(jax.nn.gelu, values)
    return (result, pullback(jnp.ones_like(values))[0])


def spread_rows(source):
    return jnp.pad(source, ((0, 0), (0, 0), (1, 1), (1, 1), (0, 0)))


def depth_conv(padded, kernel):
    channels = kernel.shape[0]
    filters = jnp.transpose(kernel).reshape(3, 3, 3, 1, channels)
    return lax.conv_general_dilated(
        padded,
        filters,
        (1, 1, 1),
        "VALID",
        dimension_numbers=("NDHWC", "DHWIO", "NDHWC"),
        feature_group_count=channels,
        precision=lax.Precision.HIGHEST,
    )


def depthwise(padded, kernel):
    return depth_conv(padded.astype(jnp.float32), kernel)


def depthwise_back(padded, kernel):
    return depth_conv(padded.astype(jnp.float32), kernel[:, ::-1])


def kernel_grad(padded, gradient, kernel):
    padded_wide = padded.astype(jnp.float32)
    _, pullback = jax.vjp(lambda weights: depth_conv(padded_wide, weights), kernel)
    return pullback(gradient.astype(jnp.float32))[0]


def contract_rows(left, right):
    return lax.dot_general(
        left, right, (((0, 1, 2, 3), (0, 1, 2, 3)), ((), ())), preferred_element_type=jnp.float32
    )


def back_project(gradient, weight):
    return lax.dot_general(
        gradient, weight, (((4,), (1,)), ((), ())), preferred_element_type=jnp.float32
    )


def place_even(sparse, frames):
    clip_count, _, half_rows, _, channels = sparse.shape
    even_grid = sparse.reshape(clip_count, 1, half_rows, 1, half_rows, 1, channels)
    even_grid = jnp.pad(even_grid, ((0, 0), (0, 0), (0, 0), (0, 1), (0, 0), (0, 1), (0, 0)))
    even_grid = even_grid.reshape(clip_count, 1, 2 * half_rows, 2 * half_rows, channels)
    return jnp.pad(even_grid, ((0, 0), (0, frames - 1), (0, 0), (0, 0), (0, 0)))


def group_total(values):
    size = lax.axis_size("space")
    copies = jnp.broadcast_to(values[None], (size,) + values.shape)
    received = lax.all_to_all(copies, "space", split_axis=0, concat_axis=0, tiled=True)
    return jnp.sum(received, axis=0)


def reduce_rows(term, axes=("clip", "space")):
    parts = 1
    for axis in axes:
        parts *= lax.axis_size(axis)
    pieces = term.astype(jnp.bfloat16).reshape((parts, term.shape[0] // parts) + term.shape[1:])
    received = lax.all_to_all(pieces, axes, split_axis=0, concat_axis=0, tiled=True)
    return jnp.sum(received.astype(jnp.float32), axis=0)


def per_device(
    clip_input,
    frame_counts,
    third_down,
    third_depth,
    third_up,
    third_gain,
    third_shift,
    fourth_down,
    fourth_skip,
    fourth_depth,
    fourth_up,
    fourth_gain,
    fourth_shift,
    classifier,
    class_bias,
    logit_grad,
):
    clip_count, local_frames, grid_rows = (
        clip_input.shape[0],
        clip_input.shape[1],
        clip_input.shape[2],
    )
    half_rows = grid_rows // 2
    slab_index = lax.axis_index("space")
    late_width = fourth_up.shape[1]
    frame_ids = 2 * slab_index + jnp.arange(local_frames, dtype=jnp.int32)
    frame_mask = (frame_ids[None, :] < frame_counts[:, None]).astype(jnp.float32)[
        :, :, None, None, None
    ]
    third_total = jnp.sum(frame_counts).astype(jnp.float32) * grid_rows * grid_rows
    first_pre = jnp.dot(clip_input, third_down, preferred_element_type=jnp.float32)
    first_gelu, slope_first = gelu_pair(first_pre)
    first_act = (first_gelu * frame_mask).astype(jnp.bfloat16)
    first_pad = spread_rows(extended(first_act, (("space", 1),), 1))
    mid_pre = depthwise(first_pad, third_depth)
    mid_gelu, slope_mid = gelu_pair(mid_pre)
    mid_act = mid_gelu.astype(jnp.bfloat16)
    third_sum = jnp.dot(mid_act, third_up, preferred_element_type=jnp.float32)
    moments = (
        jnp.sum(third_sum * frame_mask, axis=(0, 1, 2, 3)),
        jnp.sum(third_sum * third_sum * frame_mask, axis=(0, 1, 2, 3)),
    )
    moment_one, moment_two = group_total(jnp.stack(moments))
    third_center = moment_one / third_total
    third_scale = lax.rsqrt(moment_two / third_total - third_center * third_center + eps)
    third_hat = (third_sum - third_center) * third_scale
    even_hat = third_hat[:, 0:1, ::2, ::2, :]
    third_even = (
        clip_input[:, 0:1, ::2, ::2, :].astype(jnp.float32) + even_hat * third_gain + third_shift
    )
    late_entry = third_even.astype(jnp.bfloat16)
    late_mask = (2 * slab_index < frame_counts).astype(jnp.float32)[:, None, None, None, None]
    late_first = jnp.dot(late_entry, fourth_down, preferred_element_type=jnp.float32)
    late_gelu, slope_late = gelu_pair(late_first)
    late_act = (late_gelu * late_mask).astype(jnp.bfloat16)
    late_pad = spread_rows(extended(late_act, (("space", 1),), 1))
    late_mid = depthwise(late_pad, fourth_depth)
    late_mid_gelu, slope_late_mid = gelu_pair(late_mid)
    late_mid_act = late_mid_gelu.astype(jnp.bfloat16)
    late_sum = jnp.dot(late_mid_act, fourth_up, preferred_element_type=jnp.float32).astype(
        jnp.bfloat16
    )
    skipped = jnp.dot(late_entry, fourth_skip, preferred_element_type=jnp.float32).astype(
        jnp.bfloat16
    )
    late_counts = (frame_counts + 1) // 2
    pool_count = late_counts.astype(jnp.float32) * half_rows * half_rows
    late_total = jnp.sum(late_counts).astype(jnp.float32) * half_rows * half_rows
    pool_scale = pool_count[:, None, None, None, None]
    sum_values = late_sum.astype(jnp.float32)
    late_moments = group_total(
        jnp.stack(
            (
                jnp.sum(sum_values * late_mask, axis=(0, 1, 2, 3)),
                jnp.sum(sum_values * sum_values * late_mask, axis=(0, 1, 2, 3)),
            )
        )
    )
    late_center = late_moments[0] / late_total
    late_scale = lax.rsqrt(late_moments[1] / late_total - late_center * late_center + eps)
    late_hat = (sum_values - late_center) * late_scale
    late_post, slope_post = gelu_pair(
        late_hat * fourth_gain + fourth_shift + skipped.astype(jnp.float32)
    )
    pooled_term = jnp.sum(late_post * late_mask, axis=(1, 2, 3)) / pool_count[:, None]
    own_start = lax.axis_index("clip") * clip_count
    grad_rows = lax.dynamic_slice_in_dim(logit_grad, own_start, clip_count, 0)
    bias_grad = jnp.sum(logit_grad, axis=0)
    pooled_grad = lax.dot_general(
        grad_rows,
        classifier.astype(jnp.float32),
        (((1,), (1,)), ((), ())),
        precision=lax.Precision.HIGHEST,
    ).astype(jnp.bfloat16)
    pre_grad = (
        pooled_grad.astype(jnp.float32)[:, None, None, None, :] * late_mask / pool_scale * slope_post
    )
    back_one = jnp.sum(pre_grad, axis=(0, 1, 2, 3))
    back_two = jnp.sum(pre_grad * late_hat, axis=(0, 1, 2, 3))
    late_back = group_total(jnp.concatenate((jnp.stack((back_one, back_two)), pooled_term)))
    late_sum_grad = (
        fourth_gain
        * late_scale
        * (pre_grad - late_mask * (late_back[0] + late_hat * late_back[1]) / late_total)
    ).astype(jnp.bfloat16)
    late_skip_grad = pre_grad.astype(jnp.bfloat16)
    pooled = late_back[2:].astype(jnp.bfloat16)
    logits = jnp.dot(pooled, classifier, preferred_element_type=jnp.float32) + class_bias
    fourth_up_term = contract_rows(late_mid_act, late_sum_grad)
    late_mid_grad = (back_project(late_sum_grad, fourth_up) * slope_late_mid).astype(jnp.bfloat16)
    late_grad_pad = spread_rows(extended(late_mid_grad, (("space", 1),), 1))
    late_act_grad = depthwise_back(late_grad_pad, fourth_depth)
    fourth_depth_term = kernel_grad(late_pad, late_mid_grad, fourth_depth)
    late_first_grad = (late_act_grad * late_mask * slope_late).astype(jnp.bfloat16)
    fourth_down_term = contract_rows(late_entry, late_first_grad)
    fourth_skip_term = contract_rows(late_entry, late_skip_grad)
    entry_grad = back_project(late_first_grad, fourth_down) + back_project(
        late_skip_grad, fourth_skip
    )
    local_one = jnp.sum(entry_grad * frame_mask[:, 0:1], axis=(0, 1, 2, 3))
    local_two = jnp.sum(entry_grad * even_hat * frame_mask[:, 0:1], axis=(0, 1, 2, 3))
    total_one, total_two = group_total(jnp.stack((local_one, local_two)))
    out_grad = place_even(entry_grad, local_frames)
    third_sum_grad = (
        third_gain
        * third_scale
        * (out_grad - frame_mask * (total_one + third_hat * total_two) / third_total)
    ).astype(jnp.bfloat16)
    third_up_term = contract_rows(mid_act, third_sum_grad)
    mid_grad = (back_project(third_sum_grad, third_up) * slope_mid).astype(jnp.bfloat16)
    mid_grad_pad = spread_rows(extended(mid_grad, (("space", 1),), 1))
    first_act_grad = depthwise_back(mid_grad_pad, third_depth)
    third_depth_term = kernel_grad(first_pad, mid_grad, third_depth)
    first_grad = (first_act_grad * frame_mask * slope_first).astype(jnp.bfloat16)
    third_down_term = contract_rows(clip_input, first_grad)
    clip_grad = (out_grad + back_project(first_grad, third_down)).astype(jnp.bfloat16)
    parts = lax.axis_size("clip") * lax.axis_size("space")
    small_terms = [
        term.reshape(parts, -1)
        for term in (local_two, local_one, back_two, back_one, third_depth_term, fourth_depth_term)
    ]
    widths = [term.shape[1] for term in small_terms]
    pooled_pieces = jnp.moveaxis(pooled.astype(jnp.float32).reshape(clip_count, parts, -1), 1, 0)
    own_width = pooled_pieces.shape[2]
    packed = jnp.concatenate(small_terms + [pooled_pieces.reshape(parts, -1)], axis=1)
    length = packed.shape[1]
    packed = jnp.pad(packed, ((0, 0), (0, -length % 1024))).reshape(parts, -1, 128)
    received = lax.all_to_all(packed, ("clip", "space"), split_axis=0, concat_axis=0, tiled=True)
    received = received.reshape(parts, -1)
    totals = jnp.sum(received[:, : sum(widths)], axis=0)
    ends = [sum(widths[: i + 1]) for i in range(len(widths))]
    pieces = [totals[end - width : end] for width, end in zip(widths, ends)]
    gathered = received[:, sum(widths) : length].reshape(
        lax.axis_size("clip"), lax.axis_size("space"), clip_count, own_width
    )[:, 0]
    classifier_grad = lax.dot_general(
        gathered.reshape(-1, own_width),
        logit_grad,
        (((0,), (0,)), ((), ())),
        precision=lax.Precision.HIGHEST,
    )
    return (
        logits,
        clip_grad,
        reduce_rows(third_down_term),
        pieces[4].reshape(-1, third_depth.shape[1]),
        reduce_rows(third_up_term),
        pieces[0],
        pieces[1],
        reduce_rows(fourth_down_term),
        reduce_rows(fourth_skip_term),
        pieces[5].reshape(-1, fourth_depth.shape[1]),
        reduce_rows(fourth_up_term),
        pieces[2],
        pieces[3],
        classifier_grad,
        bias_grad,
    )


def solution(mesh):
    return jax.shard_map(
        per_device,
        mesh=mesh,
        in_specs=(
            P("clip", "space", None, None, None),
            P("clip"),
            P(),
            P(),
            P(),
            P(),
            P(),
            P(),
            P(),
            P(),
            P(),
            P(),
            P(),
            P(),
            P(),
            P(),
        ),
        out_specs=(
            P("clip", None),
            P("clip", "space", None, None, None),
            P(("clip", "space"), None),
            P(("clip", "space"), None),
            P(("clip", "space"), None),
            P(("clip", "space")),
            P(("clip", "space")),
            P(("clip", "space"), None),
            P(("clip", "space"), None),
            P(("clip", "space"), None),
            P(("clip", "space"), None),
            P(("clip", "space")),
            P(("clip", "space")),
            P(("clip", "space"), None),
            P(),
        ),
        check_vma=False,
    )
```

```python
import functools
import math

import jax
import jax.numpy as jnp
from jax import lax
from jax.experimental import pallas as pl
from jax.experimental.pallas import tpu as pltpu
from jax.sharding import PartitionSpec as P

eps = 1e-05
f32 = jnp.float32
bf16 = jnp.bfloat16
mib = 1 << 20


def gelu_terms(x):
    c = math.sqrt(2.0 / math.pi)
    x2 = x * x
    t = jnp.tanh(x * (c + (c * 0.044715) * x2))
    return x2, t


def gelu(x):
    _, t = gelu_terms(x)
    return x * (0.5 + 0.5 * t)


def gelu_slope(x):
    c = math.sqrt(2.0 / math.pi)
    x2, t = gelu_terms(x)
    return 0.5 + 0.5 * t + (0.5 * x) * ((1.0 - t * t) * (c + (3.0 * c * 0.044715) * x2))


def gelu_both(x):
    c = math.sqrt(2.0 / math.pi)
    x2, t = gelu_terms(x)
    cdf = 0.5 + 0.5 * t
    return x * cdf, cdf + (0.5 * x) * ((1.0 - t * t) * (c + (3.0 * c * 0.044715) * x2))


def valid_rows(shape, group, used):
    return lax.broadcasted_iota(jnp.int32, shape, 0) % group < used


def row_sums(values):
    rows, width = values.shape
    return jnp.sum(values.reshape(rows // 8, 8, width), axis=0)


def dot(left, right):
    return jnp.dot(left, right, preferred_element_type=f32)


def dot_t(left, right):
    return lax.dot_general(left, right, (((1,), (1,)), ((), ())), preferred_element_type=f32)


def t_dot(left, right):
    return lax.dot_general(left, right, (((0,), (0,)), ((), ())), preferred_element_type=f32)


def put_lanes(ref, start, values):
    rows, channels = values.shape
    for j in range(channels // 128):
        ref[j, pl.ds(start, rows), :] = values[:, 128 * j : 128 * (j + 1)]


def get_lanes(ref, start, rows):
    return jnp.concatenate([ref[j, pl.ds(start, rows), :] for j in range(ref.shape[0])], axis=1)


def get_even(ref, start, count):
    return jnp.concatenate(
        [ref[j, pl.ds(start, count, stride=2), :] for j in range(ref.shape[0])], axis=1
    )


def put_even(ref, start, values):
    rows, channels = values.shape
    for j in range(channels // 128):
        ref[j, pl.ds(start, rows, stride=2), :] = values[:, 128 * j : 128 * (j + 1)]


def conv_rows(taps, load, rows):
    sums = [None, None, None]
    for a in range(3):
        for b in range(3):
            block = load(a, b)
            for e in range(3):
                i = 9 * a + 3 * b + e
                term = block * taps(i)
                sums[e] = term if sums[e] is None else sums[e] + term
    return pltpu.roll(sums[0], 1, 0) + sums[1] + pltpu.roll(sums[2], rows - 1, 0)


def first_kernel(par_ref, scal_ref, x_ref, w_ref, first_ref, actz_ref, actc_ref, even_ref, xpad, xe):
    k = pl.program_id(0)
    _, _, height, width, _ = x_ref.shape
    pitch = xe.shape[1]

    @pl.when(k == 0)
    def _():
        xpad[...] = jnp.zeros_like(xpad)
        xe[...] = jnp.zeros_like(xe)

    for slot, act_ref in ((0, actz_ref), (1, actc_ref)):
        frame = par_ref[0] if slot == 0 else 1 - par_ref[0]
        for h in range(height):
            xpad[pl.ds(h * pitch, width), :] = x_ref[0, frame, h]
        first = dot(xpad[...], w_ref[...])
        first_ref[0, slot] = first
        act_ref[0] = (gelu(first) * scal_ref[slot, k]).astype(bf16)
    for h in range(0, height, 2):
        put_lanes(xe, 0, x_ref[0, 0, h].astype(f32))
        even_ref[0, pl.ds(h // 2 * (pitch // 2), pitch // 2), :] = get_even(xe, 0, pitch // 2)


def fill_frames(frames, sources, pad, rows):
    for s, source in enumerate(sources):
        frames[s, pl.ds(pad, rows), :] = source[0].astype(f32)


def clear_edges(frames, pad, rows):
    edge = jnp.zeros((pad, frames.shape[-1]), f32)
    for s in range(frames.shape[0]):
        frames[s, pl.ds(0, pad), :] = edge
        frames[s, pl.ds(pad + rows, pad), :] = edge


def mid_kernel(
    width, par_ref, scal_ref, rz_ref, oz_ref, oc_ref, rc_ref, taps_ref, up_ref,
    mid_ref, act_ref, even_ref, moment_ref, frames, sums, total,
):
    k = pl.program_id(0)
    rows = oz_ref.shape[1]
    pitch = 16
    chunk = 2 * pitch

    @pl.when(k == 0)
    def _():
        clear_edges(frames, pitch, rows)
        total[...] = jnp.zeros_like(total)

    fill_frames(frames, (rz_ref, oz_ref, oc_ref, rc_ref), pitch, rows)

    for slot in range(2):
        def step(c, _):
            start = pl.multiple_of(c * chunk, chunk)
            mid = conv_rows(
                lambda i: taps_ref[pl.ds(i, 1), :],
                lambda a, b: frames[slot + a, pl.ds(pl.multiple_of(start + pitch * b, pitch), chunk), :],
                chunk,
            )
            mid_ref[0, slot, pl.ds(start, chunk), :] = mid
            act = jnp.where(valid_rows(mid.shape, pitch, width), gelu(mid), 0.0)
            act_ref[0, slot, pl.ds(start, chunk), :] = act.astype(bf16)
            return 0

        lax.fori_loop(0, rows // chunk, step, 0)
        third = dot(act_ref[0, slot], up_ref[...])
        put_lanes(sums, slot * rows, third)
        scale = scal_ref[slot, k]
        total[0] += row_sums(third) * scale
        total[1] += row_sums(third * third) * scale
    half = pitch // 2
    for j in range(rows // chunk):
        even_ref[0, pl.ds(half * j, half), :] = get_even(
            sums, par_ref[0] * rows + chunk * j, half
        )

    @pl.when(k == pl.num_programs(0) - 1)
    def _():
        moment_ref[...] = jnp.sum(total[...], axis=1)


def norm_stats(received_ref, inverse):
    totals = received_ref[0]
    for i in range(1, received_ref.shape[0]):
        totals = totals + received_ref[i]
    center = totals[0:1] * inverse
    return center, lax.rsqrt(totals[1:2] * inverse - center * center + eps)


def entry_kernel(
    width, scal_ref, moments_ref, even_x_ref, even_ref, gain_ref, shift_ref, down_ref,
    stats_ref, hat_ref, entry_ref, first_ref, act_ref,
):
    center, scale = norm_stats(moments_ref, scal_ref[4, 0])
    stats_ref[0:1] = center
    stats_ref[1:2] = scale
    clips, rows, channels = even_ref.shape
    for k in range(clips):
        hat = (even_ref[k] - center) * scale
        hat_ref[k] = hat
        entry = even_x_ref[k] + hat * gain_ref[...] + shift_ref[...]
        entry = jnp.where(valid_rows(entry.shape, 8, width), entry, 0.0)
        entry_ref[pl.ds(k * rows, rows), :] = entry.astype(bf16)
    late = dot(entry_ref[...], down_ref[...])
    first_ref[...] = late
    for k in range(clips):
        act_ref[k] = (gelu(late[k * rows : (k + 1) * rows]) * scal_ref[2, k]).astype(bf16)


def late_kernel(
    width, scal_ref, rz_ref, own_ref, rc_ref, taps_ref, up_ref,
    mid_ref, act_ref, sum_ref, moment_ref, frames,
):
    clips, rows, channels = own_ref.shape
    pitch = 8
    edge = jnp.zeros((pitch, channels), f32)
    lanes = 128

    def clip_step(k, _):
        for s, source in enumerate((rz_ref, own_ref, rc_ref)):
            frames[s, pl.ds(0, pitch), :] = edge
            frames[s, pl.ds(pitch + rows, pitch), :] = edge
            frames[s, pl.ds(pitch, rows), :] = source[k].astype(f32)
        for l in range(channels // lanes):
            cols = pl.ds(l * lanes, lanes)
            mid = conv_rows(
                lambda i: taps_ref[pl.ds(i, 1), cols],
                lambda a, b: frames[a, pl.ds(pitch * b, rows), cols],
                rows,
            )
            mid_ref[k, :, cols] = mid
            act = jnp.where(valid_rows(mid.shape, pitch, width), gelu(mid), 0.0)
            act_ref[k, :, cols] = act
        return 0

    lax.fori_loop(0, clips, clip_step, 0)


def late_sum_kernel(scal_ref, act_in_ref, up_ref, act_ref, sum_ref, moment_ref):
    clips, rows, channels = act_in_ref.shape
    for k in range(clips):
        act_ref[pl.ds(k * rows, rows), :] = act_in_ref[k].astype(bf16)
    late = dot(act_ref[...], up_ref[...]).astype(bf16)
    sum_ref[...] = late
    wide = late.astype(f32)
    one = two = None
    for k in range(clips):
        block = wide[k * rows : (k + 1) * rows]
        a = row_sums(block) * scal_ref[2, k]
        b = row_sums(block * block) * scal_ref[2, k]
        one, two = (a, b) if one is None else (one + a, two + b)
    moment_ref[0:1] = jnp.sum(one, axis=0, keepdims=True)
    moment_ref[1:2] = jnp.sum(two, axis=0, keepdims=True)


def post_kernel(
    width, scal_ref, moments_ref, sum_ref, skip_ref, gain_ref, shift_ref, pooled_grad_ref,
    stats_ref, back_ref, pooled_ref, pre_ref, skip_grad_ref,
):
    center, scale = norm_stats(moments_ref, scal_ref[4, 1])
    stats_ref[0:1] = center
    stats_ref[1:2] = scale
    clips, rows, channels = sum_ref.shape
    one = two = None
    for k in range(clips):
        hat = (sum_ref[k].astype(f32) - center) * scale
        post, slope = gelu_both(hat * gain_ref[...] + shift_ref[...] + skip_ref[k].astype(f32))
        keep = valid_rows(post.shape, 8, width)
        weight = scal_ref[3, k]
        pooled_ref[pl.ds(k, 1)] = jnp.sum(jnp.where(keep, post, 0.0), axis=0, keepdims=True) * weight
        pre = jnp.where(keep, pooled_grad_ref[pl.ds(k, 1)] * weight * slope, 0.0)
        pre_ref[k] = pre
        skip_grad_ref[k] = pre.astype(bf16)
        a, b = row_sums(pre), row_sums(pre * hat)
        one, two = (a, b) if one is None else (one + a, two + b)
    back_ref[0:1] = jnp.sum(one, axis=0, keepdims=True)
    back_ref[1:2] = jnp.sum(two, axis=0, keepdims=True)


def sum_grad_kernel(
    width, scal_ref, back_ref, stats_ref, sum_ref, pre_ref, gain_ref, up_ref, mid_ref,
    sum_grad_ref, mid_grad_ref,
):
    totals = back_ref[0]
    for i in range(1, back_ref.shape[0]):
        totals = totals + back_ref[i]
    inverse = scal_ref[4, 1]
    center, scale = stats_ref[0:1], stats_ref[1:2]
    lead = gain_ref[...] * scale
    clips, rows, channels = sum_ref.shape
    for k in range(clips):
        hat = (sum_ref[k].astype(f32) - center) * scale
        weight = scal_ref[2, k] * inverse
        grad = lead * (pre_ref[k] - weight * (totals[0:1] + hat * totals[1:2]))
        grad = jnp.where(valid_rows(grad.shape, 8, width), grad, 0.0)
        sum_grad_ref[pl.ds(k * rows, rows), :] = grad.astype(bf16)
    back = dot_t(sum_grad_ref[...], up_ref[...])
    for k in range(clips):
        mid_grad_ref[k] = (back[k * rows : (k + 1) * rows] * gelu_slope(mid_ref[k])).astype(bf16)


def late_back_kernel(
    width, scal_ref, rz_ref, own_ref, rc_ref, taps_ref, first_ref, down_ref, skip_back_ref, hat_ref,
    first_grad_ref, entry_grad_ref, back_ref, frames, grads,
):
    clips, rows, channels = own_ref.shape
    pitch = 8
    edge = jnp.zeros((pitch, channels), f32)
    lanes = 128

    def clip_step(k, _):
        for s, source in enumerate((rz_ref, own_ref, rc_ref)):
            frames[s, pl.ds(0, pitch), :] = edge
            frames[s, pl.ds(pitch + rows, pitch), :] = edge
            frames[s, pl.ds(pitch, rows), :] = source[k].astype(f32)
        for l in range(channels // lanes):
            cols = pl.ds(l * lanes, lanes)
            grad = conv_rows(
                lambda i: taps_ref[pl.ds(26 - i, 1), cols],
                lambda a, b: frames[a, pl.ds(pitch * b, rows), cols],
                rows,
            )
            grad = grad * scal_ref[2, k] * gelu_slope(first_ref[k, :, cols])
            grads[k, :, cols] = jnp.where(valid_rows(grad.shape, pitch, width), grad, 0.0)
        return 0

    lax.fori_loop(0, clips, clip_step, 0)
    for k in range(clips):
        first_grad_ref[pl.ds(k * rows, rows), :] = grads[k].astype(bf16)
    entry = dot_t(first_grad_ref[...], down_ref[...]) + skip_back_ref[...]
    one = two = None
    for k in range(clips):
        block = entry[k * rows : (k + 1) * rows]
        entry_grad_ref[k] = block
        masked = block * scal_ref[2, k]
        a, b = row_sums(masked), row_sums(masked * hat_ref[k])
        one, two = (a, b) if one is None else (one + a, two + b)
    back_ref[0:1] = jnp.sum(one, axis=0, keepdims=True)
    back_ref[1:2] = jnp.sum(two, axis=0, keepdims=True)


def tap_grads(load, grad_of, steps, rows):
    def step(c, totals):
        grad = grad_of(c)
        sides = (pltpu.roll(grad, rows - 1, 0), grad, pltpu.roll(grad, 1, 0))
        new = []
        for a in range(3):
            for b in range(3):
                block = load(c, a, b)
                for e in range(3):
                    new.append(totals[9 * a + 3 * b + e] + row_sums(block * sides[e]))
        return tuple(new)

    return steps, step


def late_taps_kernel(rz_ref, own_ref, rc_ref, grad_ref, out_ref, frames):
    clips, rows, channels = own_ref.shape
    pitch = 8
    edge = jnp.zeros((pitch, channels), f32)
    lanes = 128
    for s, source in enumerate((rz_ref, own_ref, rc_ref)):
        for k in range(clips):
            frames[s, k, pl.ds(0, pitch), :] = edge
            frames[s, k, pl.ds(pitch + rows, pitch), :] = edge
            frames[s, k, pl.ds(pitch, rows), :] = source[k].astype(f32)
    for l in range(channels // lanes):
        cols = pl.ds(l * lanes, lanes)
        steps, step = tap_grads(
            lambda k, a, b: frames[a, k, pl.ds(pitch * b, rows), cols],
            lambda k: grad_ref[k, :, cols].astype(f32),
            clips,
            rows,
        )
        zero = jnp.zeros((8, lanes), f32)
        totals = lax.fori_loop(0, steps, step, (zero,) * 27)
        for i in range(27):
            out_ref[pl.ds(i, 1), cols] = jnp.sum(totals[i], axis=0, keepdims=True)


def third_taps_kernel(rz_ref, oz_ref, oc_ref, rc_ref, gz_ref, gc_ref, out_ref, frames, grads, total):
    k = pl.program_id(0)
    rows, channels = oz_ref.shape[1], oz_ref.shape[2]
    pitch = 16
    chunk = 2 * pitch
    lanes = 128

    @pl.when(k == 0)
    def _():
        clear_edges(frames, pitch, rows)
        total[...] = jnp.zeros_like(total)

    fill_frames(frames, (rz_ref, oz_ref, oc_ref, rc_ref), pitch, rows)
    grads[0] = gz_ref[0].astype(f32)
    grads[1] = gc_ref[0].astype(f32)
    count = rows // chunk
    for l in range(channels // lanes):
        cols = pl.ds(l * lanes, lanes)
        totals = tuple(total[i, :, cols] for i in range(27))
        for slot in range(2):
            steps, step = tap_grads(
                lambda c, a, b: frames[
                    slot + a, pl.ds(pl.multiple_of(c * chunk + pitch * b, pitch), chunk), cols
                ],
                lambda c: grads[slot, pl.ds(pl.multiple_of(c * chunk, chunk), chunk), cols],
                count,
                chunk,
            )
            totals = lax.fori_loop(0, steps, step, totals)
        for i in range(27):
            total[i, :, cols] = totals[i]

    @pl.when(k == pl.num_programs(0) - 1)
    def _():
        out_ref[...] = jnp.sum(total[...], axis=1)


def third_grad_kernel(
    width, par_ref, scal_ref, back_ref, stats_ref, act_ref, mid_ref, entry_grad_ref, gain_ref, up_ref,
    sum_grad_ref, gz_ref, gc_ref, placed,
):
    k = pl.program_id(0)
    totals = back_ref[0]
    for i in range(1, back_ref.shape[0]):
        totals = totals + back_ref[i]
    rows = act_ref.shape[2]
    pitch = 16
    chunk = 2 * pitch
    half = pitch // 2
    center, scale = stats_ref[0:1], stats_ref[1:2]
    lead = gain_ref[...] * scale
    inverse = scal_ref[4, 0]

    @pl.when(k == 0)
    def _():
        placed[...] = jnp.zeros_like(placed)

    for j in range(rows // chunk):
        put_even(
            placed, par_ref[0] * rows + chunk * j, lead * entry_grad_ref[0, pl.ds(half * j, half), :]
        )
    for slot, out in ((0, gz_ref), (1, gc_ref)):
        weight = scal_ref[slot, k] * inverse
        slope_hat = -(lead * scale * totals[1:2]) * weight
        offset = -(lead * (totals[0:1] - center * scale * totals[1:2])) * weight
        third = dot(act_ref[0, slot], up_ref[...])
        grad = get_lanes(placed, slot * rows, rows) + (offset + third * slope_hat)
        sum_grad_ref[0, slot] = grad.astype(bf16)
        back = dot_t(sum_grad_ref[0, slot], up_ref[...]) * gelu_slope(mid_ref[0, slot])
        out[0] = jnp.where(valid_rows(back.shape, pitch, width), back, 0.0).astype(bf16)


def first_grad_kernel(
    width, par_ref, scal_ref, rz_ref, gz_ref, gc_ref, rc_ref, taps_ref, first_ref, x_ref,
    grad_ref, down_grad_ref, frames, xpad,
):
    k = pl.program_id(0)
    rows = gz_ref.shape[1]
    height, width = x_ref.shape[2], x_ref.shape[3]
    pitch = 16
    chunk = 2 * pitch

    @pl.when(k == 0)
    def _():
        clear_edges(frames, pitch, rows)
        xpad[...] = jnp.zeros_like(xpad)
        down_grad_ref[...] = jnp.zeros_like(down_grad_ref)

    fill_frames(frames, (rz_ref, gz_ref, gc_ref, rc_ref), pitch, rows)
    for slot in range(2):
        frame = par_ref[0] if slot == 0 else 1 - par_ref[0]
        for h in range(height):
            xpad[pl.ds(slot * rows + h * pitch, width), :] = x_ref[0, frame, h]
        scale = scal_ref[slot, k]

        def step(c, _):
            start = pl.multiple_of(c * chunk, chunk)
            grad = conv_rows(
                lambda i: taps_ref[pl.ds(26 - i, 1), :],
                lambda a, b: frames[slot + a, pl.ds(pl.multiple_of(start + pitch * b, pitch), chunk), :],
                chunk,
            )
            grad = grad * scale * gelu_slope(first_ref[0, slot, pl.ds(start, chunk), :])
            grad = jnp.where(valid_rows(grad.shape, pitch, width), grad, 0.0)
            grad_ref[0, pl.ds(pl.multiple_of(slot * rows + start, chunk), chunk), :] = grad.astype(bf16)
            return 0

        lax.fori_loop(0, rows // chunk, step, 0)
    down_grad_ref[...] += t_dot(xpad[...], grad_ref[0])


def clip_grad_kernel(par_ref, grad_ref, down_ref, entry_grad_ref, out_ref, wide):
    _, _, height, width, _ = out_ref.shape
    pitch = 16
    half = pitch // 2
    rows = height * pitch
    for slot in range(2):
        frame = par_ref[0] if slot == 0 else 1 - par_ref[0]
        put_lanes(wide, slot * rows, dot_t(grad_ref[0, pl.ds(slot * rows, rows), :], down_ref[...]))
    for j in range(height // 2):
        at = par_ref[0] * rows + 2 * pitch * j
        put_even(wide, at, get_even(wide, at, half) + entry_grad_ref[0, pl.ds(half * j, half), :])
    for slot in range(2):
        frame = par_ref[0] if slot == 0 else 1 - par_ref[0]
        for h in range(height):
            out_ref[0, frame, h] = get_lanes(wide, slot * rows + h * pitch, width).astype(bf16)


smem = pl.BlockSpec(memory_space=pltpu.SMEM)


def whole(shape):
    return pl.BlockSpec(shape, lambda k: (0,) * len(shape))


def by_clip(shape):
    return pl.BlockSpec((1,) + shape[1:], lambda k: (k,) + (0,) * (len(shape) - 1))


def call(kernel, name, inputs, outputs, scratch, clips=None, limit=60, flops=0):
    if clips is None:
        def spec(kind, shape):
            return smem if kind == "s" else pl.BlockSpec(memory_space=pltpu.VMEM)
    else:
        def spec(kind, shape):
            return smem if kind == "s" else whole(shape) if kind == "w" else by_clip(shape)
    size = sum(math.prod(a.shape) * a.dtype.itemsize for a, _ in inputs)
    size += sum(math.prod(s) * jnp.dtype(d).itemsize for s, d, _ in outputs)
    options = {} if clips is None else {"grid": (clips,)}
    return pl.pallas_call(
        kernel,
        name=name,
        out_shape=[jax.ShapeDtypeStruct(s, d) for s, d, _ in outputs],
        in_specs=[spec(kind, a.shape) for a, kind in inputs],
        out_specs=[spec(kind, s) for s, _, kind in outputs],
        scratch_shapes=scratch,
        compiler_params=pltpu.CompilerParams(vmem_limit_bytes=limit * mib),
        cost_estimate=pl.CostEstimate(flops=flops, bytes_accessed=size, transcendentals=0),
        **options,
    )(*[a for a, _ in inputs])


def copies_exchange(values):
    size = lax.axis_size("space")
    copies = jnp.broadcast_to(values[None], (size,) + values.shape)
    return lax.all_to_all(copies, "space", split_axis=0, concat_axis=0, tiled=True)


def swap_neighbours(to_z, to_core):
    size = lax.axis_size("space")
    core = [(i, i ^ 1) for i in range(size)]
    z = [(i, j) for m in range(1, size - 1, 2) for i, j in ((m, m + 1), (m + 1, m))]
    return lax.ppermute(to_z, "space", z), lax.ppermute(to_core, "space", core)


def reduce_rows(term, axes=("clip", "space")):
    parts = 1
    for axis in axes:
        parts *= lax.axis_size(axis)
    pieces = term.astype(bf16).reshape((parts, term.shape[0] // parts) + term.shape[1:])
    received = lax.all_to_all(pieces, axes, split_axis=0, concat_axis=0, tiled=True)
    return jnp.sum(received.astype(f32), axis=0)


def per_device(
    clip_input, frame_counts, third_down, third_depth, third_up, third_gain, third_shift,
    fourth_down, fourth_skip, fourth_depth, fourth_up, fourth_gain, fourth_shift,
    classifier, class_bias, logit_grad,
):
    clips, frames, height, width, channels = clip_input.shape
    inner = third_down.shape[1]
    late_inner = fourth_down.shape[1]
    late_wide = fourth_up.shape[1]
    half_width = width // 2
    rows = height * 16
    late_rows = height // 2 * 8
    late_all = clips * late_rows
    slab = lax.axis_index("space")
    parity = slab & 1
    par = parity.reshape(1)
    flip = (parity == 1)

    frame_ids = 2 * slab + jnp.stack((parity, 1 - parity))
    masks = (frame_ids[:, None] < frame_counts[None, :]).astype(f32)
    late_mask = (2 * slab < frame_counts).astype(f32)
    late_counts = ((frame_counts + 1) // 2).astype(f32)
    cells = (height // 2) * half_width
    third_total = jnp.sum(frame_counts).astype(f32) * (height * width)
    late_total = jnp.sum(late_counts) * cells
    inverses = jnp.stack((1.0 / third_total, 1.0 / late_total))
    scal = jnp.concatenate(
        (
            masks,
            late_mask[None],
            (late_mask / (late_counts * cells))[None],
            jnp.pad(inverses, (0, clips - 2))[None],
        )
    )

    def tap_rows(kernel):
        taps = jnp.transpose(kernel).reshape(3, 9, -1)
        return jnp.where(flip, taps[::-1], taps).reshape(27, -1)

    def tap_columns(rows_out):
        taps = rows_out.reshape(3, 9, -1)
        return jnp.transpose(jnp.where(flip, taps[::-1], taps).reshape(27, -1))

    third_taps = tap_rows(third_depth)
    late_taps = tap_rows(fourth_depth)
    third_gain, third_shift = third_gain[None], third_shift[None]
    fourth_gain, fourth_shift = fourth_gain[None], fourth_shift[None]

    own_start = lax.axis_index("clip") * clips
    grad_rows = lax.dynamic_slice_in_dim(logit_grad, own_start, clips, 0)
    pooled_grad = lax.dot_general(
        grad_rows, classifier.astype(f32), (((1,), (1,)), ((), ())), precision=lax.Precision.HIGHEST
    ).astype(bf16).astype(f32)

    first, act_z, act_c, even_x = call(
        first_kernel, "first",
        [(par, "s"), (scal, "s"), (clip_input, "c"), (third_down, "w")],
        [
            ((clips, 2, rows, inner), f32, "c"),
            ((clips, rows, inner), bf16, "c"),
            ((clips, rows, inner), bf16, "c"),
            ((clips, late_rows, channels), f32, "c"),
        ],
        [pltpu.VMEM((rows, channels), bf16), pltpu.VMEM((channels // 128, 16, 128), f32)],
        clips=clips,
    )
    got_z, got_c = swap_neighbours(act_z, act_c)
    mid, mid_act, even_sum, moments = call(
        functools.partial(mid_kernel, width), "mid",
        [(par, "s"), (scal, "s"), (got_z, "c"), (act_z, "c"), (act_c, "c"), (got_c, "c"),
         (third_taps, "w"), (third_up, "w")],
        [
            ((clips, 2, rows, inner), f32, "c"),
            ((clips, 2, rows, inner), bf16, "c"),
            ((clips, late_rows, channels), f32, "c"),
            ((2, channels), f32, "w"),
        ],
        [
            pltpu.VMEM((4, rows + 32, inner), f32),
            pltpu.VMEM((channels // 128, 2 * rows, 128), f32),
            pltpu.VMEM((2, 8, channels), f32),
        ],
        clips=clips,
    )
    stats, even_hat, entry, late_first, late_act = call(
        functools.partial(entry_kernel, half_width), "entry",
        [(scal, "s"), (copies_exchange(moments), "w"), (even_x, "w"), (even_sum, "w"),
         (third_gain, "w"), (third_shift, "w"), (fourth_down, "w")],
        [
            ((2, channels), f32, "w"),
            ((clips, late_rows, channels), f32, "w"),
            ((late_all, channels), bf16, "w"),
            ((late_all, late_inner), f32, "w"),
            ((clips, late_rows, late_inner), bf16, "w"),
        ],
        [],
    )
    late_first = late_first.reshape(clips, late_rows, late_inner)
    late_z, late_c = swap_neighbours(late_act, late_act)
    skipped = dot(entry, fourth_skip).astype(bf16).reshape(clips, late_rows, late_wide)
    late_mid, late_mid_wide = call(
        lambda scal_ref, z, o, c, t, m, a, fr: late_kernel(
            half_width, scal_ref, z, o, c, t, None, m, a, None, None, fr
        ),
        "late_mid",
        [(scal, "s"), (late_z, "w"), (late_act, "w"), (late_c, "w"), (late_taps, "w")],
        [((clips, late_rows, late_inner), f32, "w"), ((clips, late_rows, late_inner), f32, "w")],
        [pltpu.VMEM((3, late_rows + 16, late_inner), f32)],
    )
    late_mid_act, late_sum, late_moments = call(
        late_sum_kernel, "late_sum",
        [(scal, "s"), (late_mid_wide, "w"), (fourth_up, "w")],
        [
            ((late_all, late_inner), bf16, "w"),
            ((late_all, late_wide), bf16, "w"),
            ((2, late_wide), f32, "w"),
        ],
        [],
    )
    late_sum = late_sum.reshape(clips, late_rows, late_wide)
    late_stats, late_back, pooled_term, pre_grad, skip_grad = call(
        functools.partial(post_kernel, half_width), "post",
        [(scal, "s"), (copies_exchange(late_moments), "w"), (late_sum, "w"), (skipped, "w"),
         (fourth_gain, "w"), (fourth_shift, "w"), (pooled_grad, "w")],
        [
            ((2, late_wide), f32, "w"),
            ((2, late_wide), f32, "w"),
            ((clips, late_wide), f32, "w"),
            ((clips, late_rows, late_wide), f32, "w"),
            ((clips, late_rows, late_wide), bf16, "w"),
        ],
        [],
    )
    received = copies_exchange(jnp.concatenate((late_back, pooled_term)))
    pooled = jnp.sum(received[:, 2:], axis=0).astype(bf16)
    logits = dot(pooled, classifier) + class_bias
    skip_rows = skip_grad.reshape(late_all, late_wide)
    skip_back = dot_t(skip_rows, fourth_skip)
    fourth_skip_term = t_dot(entry, skip_rows)
    late_sum_grad, late_mid_grad = call(
        functools.partial(sum_grad_kernel, half_width), "sum_grad",
        [(scal, "s"), (received, "w"), (late_stats, "w"), (late_sum, "w"), (pre_grad, "w"),
         (fourth_gain, "w"), (fourth_up, "w"), (late_mid, "w")],
        [((late_all, late_wide), bf16, "w"), ((clips, late_rows, late_inner), bf16, "w")],
        [],
    )
    late_gz, late_gc = swap_neighbours(late_mid_grad, late_mid_grad)
    fourth_up_term = t_dot(late_mid_act, late_sum_grad)
    (fourth_depth_term,) = call(
        late_taps_kernel, "late_taps",
        [(late_z, "w"), (late_act, "w"), (late_c, "w"), (late_mid_grad, "w")],
        [((27, late_inner), f32, "w")],
        [pltpu.VMEM((3, clips, late_rows + 16, late_inner), f32)],
    )
    late_first_grad, entry_grad, third_back = call(
        functools.partial(late_back_kernel, half_width), "late_back",
        [(scal, "s"), (late_gz, "w"), (late_mid_grad, "w"), (late_gc, "w"), (late_taps, "w"),
         (late_first, "w"), (fourth_down, "w"), (skip_back, "w"), (even_hat, "w")],
        [
            ((late_all, late_inner), bf16, "w"),
            ((clips, late_rows, channels), f32, "w"),
            ((2, channels), f32, "w"),
        ],
        [
            pltpu.VMEM((3, late_rows + 16, late_inner), f32),
            pltpu.VMEM((clips, late_rows, late_inner), f32),
        ],
    )
    fourth_down_term = t_dot(entry, late_first_grad)
    third_sum_grad, grad_z, grad_c = call(
        functools.partial(third_grad_kernel, width), "third_grad",
        [(par, "s"), (scal, "s"), (copies_exchange(third_back), "w"), (stats, "w"), (mid_act, "c"), (mid, "c"),
         (entry_grad, "c"), (third_gain, "w"), (third_up, "w")],
        [
            ((clips, 2, rows, channels), bf16, "c"),
            ((clips, rows, inner), bf16, "c"),
            ((clips, rows, inner), bf16, "c"),
        ],
        [pltpu.VMEM((channels // 128, 2 * rows, 128), f32)],
        clips=clips,
    )
    third_gz, third_gc = swap_neighbours(grad_z, grad_c)
    third_up_term = t_dot(
        mid_act.reshape(clips * 2 * rows, inner), third_sum_grad.reshape(clips * 2 * rows, channels)
    )
    (third_depth_term,) = call(
        third_taps_kernel, "third_taps",
        [(got_z, "c"), (act_z, "c"), (act_c, "c"), (got_c, "c"), (grad_z, "c"), (grad_c, "c")],
        [((27, inner), f32, "w")],
        [
            pltpu.VMEM((4, rows + 32, inner), f32),
            pltpu.VMEM((2, rows, inner), f32),
            pltpu.VMEM((27, 8, inner), f32),
        ],
        clips=clips,
    )
    first_grad, third_down_term = call(
        functools.partial(first_grad_kernel, width), "first_grad",
        [(par, "s"), (scal, "s"), (third_gz, "c"), (grad_z, "c"), (grad_c, "c"), (third_gc, "c"),
         (third_taps, "w"), (first, "c"), (clip_input, "c")],
        [((clips, 2 * rows, inner), bf16, "c"), ((channels, inner), f32, "w")],
        [pltpu.VMEM((4, rows + 32, inner), f32), pltpu.VMEM((2 * rows, channels), bf16)],
        clips=clips,
    )
    (clip_grad,) = call(
        clip_grad_kernel, "clip_grad",
        [(par, "s"), (first_grad, "c"), (third_down, "w"), (entry_grad, "c")],
        [(clip_input.shape, bf16, "c")],
        [pltpu.VMEM((channels // 128, 2 * rows, 128), f32)],
        clips=clips,
    )

    parts = lax.axis_size("clip") * lax.axis_size("space")
    small_terms = [
        term.reshape(parts, -1)
        for term in (
            third_back[1], third_back[0], late_back[1], late_back[0],
            tap_columns(third_depth_term), tap_columns(fourth_depth_term),
        )
    ]
    widths = [term.shape[1] for term in small_terms]
    pooled_pieces = jnp.moveaxis(pooled.astype(f32).reshape(clips, parts, -1), 1, 0)
    own_width = pooled_pieces.shape[2]
    packed = jnp.concatenate(small_terms + [pooled_pieces.reshape(parts, -1)], axis=1)
    length = packed.shape[1]
    packed = jnp.pad(packed, ((0, 0), (0, -length % 1024))).reshape(parts, -1, 128)
    received = lax.all_to_all(packed, ("clip", "space"), split_axis=0, concat_axis=0, tiled=True)
    received = received.reshape(parts, -1)
    totals = jnp.sum(received[:, : sum(widths)], axis=0)
    ends = [sum(widths[: i + 1]) for i in range(len(widths))]
    pieces = [totals[end - size : end] for size, end in zip(widths, ends)]
    gathered = received[:, sum(widths) : length].reshape(
        lax.axis_size("clip"), lax.axis_size("space"), clips, own_width
    )[:, 0]
    classifier_grad = lax.dot_general(
        gathered.reshape(-1, own_width), logit_grad, (((0,), (0,)), ((), ())),
        precision=lax.Precision.HIGHEST,
    )
    return (
        logits,
        clip_grad,
        reduce_rows(third_down_term),
        pieces[4].reshape(-1, 27),
        reduce_rows(third_up_term),
        pieces[0],
        pieces[1],
        reduce_rows(fourth_down_term),
        reduce_rows(fourth_skip_term),
        pieces[5].reshape(-1, 27),
        reduce_rows(fourth_up_term),
        pieces[2],
        pieces[3],
        classifier_grad,
        jnp.sum(logit_grad, axis=0),
    )


def solution(mesh):
    both = ("clip", "space")
    return jax.shard_map(
        per_device,
        mesh=mesh,
        in_specs=(P("clip", "space", None, None, None), P("clip")) + (P(),) * 14,
        out_specs=(
            P("clip", None),
            P("clip", "space", None, None, None),
            P(both, None),
            P(both, None),
            P(both, None),
            P(both),
            P(both),
            P(both, None),
            P(both, None),
            P(both, None),
            P(both, None),
            P(both),
            P(both),
            P(both, None),
            P(),
        ),
        check_vma=False,
    )
```

```python
import functools
import math

import jax
import jax.numpy as jnp
from jax import lax
from jax.experimental import pallas as pl
from jax.experimental.pallas import tpu as pltpu
from jax.sharding import PartitionSpec as P

eps = 1e-05
f32 = jnp.float32
bf16 = jnp.bfloat16
mib = 1 << 20


def gelu_terms(x):
    c = math.sqrt(2.0 / math.pi)
    x2 = x * x
    t = jnp.tanh(x * (c + (c * 0.044715) * x2))
    return x2, t


def gelu(x):
    _, t = gelu_terms(x)
    return x * (0.5 + 0.5 * t)


def gelu_slope(x):
    c = math.sqrt(2.0 / math.pi)
    x2, t = gelu_terms(x)
    return 0.5 + 0.5 * t + (0.5 * x) * ((1.0 - t * t) * (c + (3.0 * c * 0.044715) * x2))


def gelu_both(x):
    c = math.sqrt(2.0 / math.pi)
    x2, t = gelu_terms(x)
    cdf = 0.5 + 0.5 * t
    return x * cdf, cdf + (0.5 * x) * ((1.0 - t * t) * (c + (3.0 * c * 0.044715) * x2))


def valid_rows(shape, group, used):
    return lax.broadcasted_iota(jnp.int32, shape, 0) % group < used


def row_sums(values):
    rows, width = values.shape
    return jnp.sum(values.reshape(rows // 8, 8, width), axis=0)


def dot(left, right):
    return jnp.dot(left, right, preferred_element_type=f32)


def dot_t(left, right):
    return lax.dot_general(left, right, (((1,), (1,)), ((), ())), preferred_element_type=f32)


def t_dot(left, right):
    return lax.dot_general(left, right, (((0,), (0,)), ((), ())), preferred_element_type=f32)


def put_lanes(ref, start, values):
    rows, channels = values.shape
    for j in range(channels // 128):
        ref[j, pl.ds(start, rows), :] = values[:, 128 * j : 128 * (j + 1)]


def get_lanes(ref, start, rows):
    return jnp.concatenate([ref[j, pl.ds(start, rows), :] for j in range(ref.shape[0])], axis=1)


def get_even(ref, start, count):
    return jnp.concatenate(
        [ref[j, pl.ds(start, count, stride=2), :] for j in range(ref.shape[0])], axis=1
    )


def put_even(ref, start, values):
    rows, channels = values.shape
    for j in range(channels // 128):
        ref[j, pl.ds(start, rows, stride=2), :] = values[:, 128 * j : 128 * (j + 1)]


def conv_rows(taps, load, rows):
    sums = [None, None, None]
    for a in range(3):
        for b in range(3):
            block = load(a, b)
            for e in range(3):
                i = 9 * a + 3 * b + e
                term = block * taps(i)
                sums[e] = term if sums[e] is None else sums[e] + term
    return pltpu.roll(sums[0], 1, 0) + sums[1] + pltpu.roll(sums[2], rows - 1, 0)


def frame_of(slot):
    parity = lax.axis_index("space") & 1
    return parity if slot == 0 else 1 - parity


def frame_mask(counts_ref, k, frame):
    return jnp.where(2 * lax.axis_index("space") + frame < counts_ref[k], 1.0, 0.0).astype(f32)


def cell_total(counts_ref, late, cells):
    total = 0
    for k in range(counts_ref.shape[0]):
        total += (counts_ref[k] + 1) // 2 if late else counts_ref[k]
    return (total * cells).astype(f32)


def received_sum(refs):
    total = None
    for ref in refs:
        for i in range(ref.shape[0]):
            total = ref[i] if total is None else total + ref[i]
    return total


def first_kernel(counts_ref, x_ref, w_ref, first_ref, actz_ref, actc_ref, even_ref, xpad, xe):
    k = pl.program_id(0)
    _, _, height, width, _ = x_ref.shape
    pitch = xe.shape[1]

    @pl.when(k == 0)
    def _():
        xpad[...] = jnp.zeros_like(xpad)
        xe[...] = jnp.zeros_like(xe)

    for slot, act_ref in ((0, actz_ref), (1, actc_ref)):
        frame = frame_of(slot)
        for h in range(height):
            xpad[pl.ds(h * pitch, width), :] = x_ref[0, frame, h]
        first = dot(xpad[...], w_ref[...])
        first_ref[0, slot] = first
        act_ref[0] = (gelu(first) * frame_mask(counts_ref, k, frame)).astype(bf16)
    for h in range(0, height, 2):
        put_lanes(xe, 0, x_ref[0, 0, h].astype(f32))
        even_ref[0, pl.ds(h // 2 * (pitch // 2), pitch // 2), :] = get_even(xe, 0, pitch // 2)


def fill_frames(frames, sources, pad, rows):
    for s, source in enumerate(sources):
        frames[s, pl.ds(pad, rows), :] = source[0].astype(f32)


def clear_edges(frames, pad, rows):
    edge = jnp.zeros((pad, frames.shape[-1]), f32)
    for s in range(frames.shape[0]):
        frames[s, pl.ds(0, pad), :] = edge
        frames[s, pl.ds(pad + rows, pad), :] = edge


def mid_kernel(
    width, counts_ref, rz_ref, oz_ref, oc_ref, rc_ref, taps_ref, up_ref,
    mid_ref, act_ref, even_ref, moment_ref, frames, sums, total,
):
    k = pl.program_id(0)
    rows = oz_ref.shape[1]
    pitch = 16
    chunk = 2 * pitch

    @pl.when(k == 0)
    def _():
        clear_edges(frames, pitch, rows)
        total[...] = jnp.zeros_like(total)

    fill_frames(frames, (rz_ref, oz_ref, oc_ref, rc_ref), pitch, rows)

    for slot in range(2):
        def step(c, _):
            start = pl.multiple_of(c * chunk, chunk)
            mid = conv_rows(
                lambda i: taps_ref[pl.ds(i, 1), :],
                lambda a, b: frames[slot + a, pl.ds(pl.multiple_of(start + pitch * b, pitch), chunk), :],
                chunk,
            )
            mid_ref[0, slot, pl.ds(start, chunk), :] = mid
            act = jnp.where(valid_rows(mid.shape, pitch, width), gelu(mid), 0.0)
            act_ref[0, slot, pl.ds(start, chunk), :] = act.astype(bf16)
            return 0

        lax.fori_loop(0, rows // chunk, step, 0)
        third = dot(act_ref[0, slot], up_ref[...])
        put_lanes(sums, slot * rows, third)
        scale = frame_mask(counts_ref, k, frame_of(slot))
        total[0] += row_sums(third) * scale
        total[1] += row_sums(third * third) * scale
    half = pitch // 2
    for j in range(rows // chunk):
        even_ref[0, pl.ds(half * j, half), :] = get_even(
            sums, frame_of(0) * rows + chunk * j, half
        )

    @pl.when(k == pl.num_programs(0) - 1)
    def _():
        moment_ref[...] = jnp.sum(total[...], axis=1)


def norm_stats(refs, cells):
    totals = received_sum(refs)
    center = totals[0:1] / cells
    return center, lax.rsqrt(totals[1:2] / cells - center * center + eps)


def entry_kernel(
    width, cells, parts, counts_ref, *refs
):
    moments, refs = refs[:parts], refs[parts:]
    (even_x_ref, even_ref, gain_ref, shift_ref, down_ref,
     stats_ref, hat_ref, entry_ref, first_ref, act_ref) = refs
    center, scale = norm_stats(moments, cell_total(counts_ref, False, cells))
    stats_ref[0:1] = center
    stats_ref[1:2] = scale
    clips, rows, channels = even_ref.shape
    for k in range(clips):
        hat = (even_ref[k] - center) * scale
        hat_ref[k] = hat
        entry = even_x_ref[k] + hat * gain_ref[...] + shift_ref[...]
        entry = jnp.where(valid_rows(entry.shape, 8, width), entry, 0.0)
        entry_ref[pl.ds(k * rows, rows), :] = entry.astype(bf16)
    late = dot(entry_ref[...], down_ref[...])
    first_ref[...] = late
    for k in range(clips):
        act_ref[k] = (gelu(late[k * rows : (k + 1) * rows]) * frame_mask(counts_ref, k, 0)).astype(bf16)


def late_kernel(
    width, counts_ref, rz_ref, own_ref, rc_ref, taps_ref, up_ref,
    mid_ref, act_ref, sum_ref, moment_ref, frames, wide,
):
    clips, rows, channels = own_ref.shape
    pitch = 8
    edge = jnp.zeros((pitch, channels), f32)
    lanes = 128

    def clip_step(k, _):
        for s, source in enumerate((rz_ref, own_ref, rc_ref)):
            frames[s, pl.ds(0, pitch), :] = edge
            frames[s, pl.ds(pitch + rows, pitch), :] = edge
            frames[s, pl.ds(pitch, rows), :] = source[k].astype(f32)
        for l in range(channels // lanes):
            cols = pl.ds(l * lanes, lanes)
            mid = conv_rows(
                lambda i: taps_ref[pl.ds(i, 1), cols],
                lambda a, b: frames[a, pl.ds(pitch * b, rows), cols],
                rows,
            )
            mid_ref[k, :, cols] = mid
            wide[k, :, cols] = jnp.where(valid_rows(mid.shape, pitch, width), gelu(mid), 0.0)
        return 0

    lax.fori_loop(0, clips, clip_step, 0)
    for k in range(clips):
        act_ref[pl.ds(k * rows, rows), :] = wide[k].astype(bf16)
    late = dot(act_ref[...], up_ref[...]).astype(bf16)
    sum_ref[...] = late
    late = late.astype(f32)
    one = two = None
    for k in range(clips):
        block = late[k * rows : (k + 1) * rows]
        mask = frame_mask(counts_ref, k, 0)
        a, b = row_sums(block) * mask, row_sums(block * block) * mask
        one, two = (a, b) if one is None else (one + a, two + b)
    moment_ref[0:1] = jnp.sum(one, axis=0, keepdims=True)
    moment_ref[1:2] = jnp.sum(two, axis=0, keepdims=True)


def post_kernel(
    width, cells, parts, counts_ref, *refs
):
    moments, refs = refs[:parts], refs[parts:]
    (sum_ref, skip_ref, gain_ref, shift_ref, pooled_grad_ref,
     stats_ref, back_ref, pooled_ref, pre_ref, skip_grad_ref) = refs
    center, scale = norm_stats(moments, cell_total(counts_ref, True, cells))
    stats_ref[0:1] = center
    stats_ref[1:2] = scale
    clips, rows, channels = sum_ref.shape
    one = two = None
    for k in range(clips):
        hat = (sum_ref[k].astype(f32) - center) * scale
        post, slope = gelu_both(hat * gain_ref[...] + shift_ref[...] + skip_ref[k].astype(f32))
        keep = valid_rows(post.shape, 8, width)
        mask = frame_mask(counts_ref, k, 0)
        pool = ((counts_ref[k] + 1) // 2 * cells).astype(f32)
        pooled_ref[pl.ds(k, 1)] = jnp.sum(jnp.where(keep, post, 0.0), axis=0, keepdims=True) * mask / pool
        pre = jnp.where(keep, pooled_grad_ref[pl.ds(k, 1)] * mask / pool * slope, 0.0)
        pre_ref[k] = pre
        skip_grad_ref[k] = pre.astype(bf16)
        a, b = row_sums(pre), row_sums(pre * hat)
        one, two = (a, b) if one is None else (one + a, two + b)
    back_ref[0:1] = jnp.sum(one, axis=0, keepdims=True)
    back_ref[1:2] = jnp.sum(two, axis=0, keepdims=True)


def sum_grad_kernel(
    width, cells, parts, counts_ref, *refs
):
    received, refs = refs[:parts], refs[parts:]
    (stats_ref, sum_ref, pre_ref, gain_ref, up_ref, mid_ref, sum_grad_ref, mid_grad_ref) = refs
    totals = received_sum(received)[0:2] / cell_total(counts_ref, True, cells)
    center, scale = stats_ref[0:1], stats_ref[1:2]
    lead = gain_ref[...] * scale
    clips, rows, channels = sum_ref.shape
    for k in range(clips):
        hat = (sum_ref[k].astype(f32) - center) * scale
        weight = frame_mask(counts_ref, k, 0)
        grad = lead * (pre_ref[k] - weight * (totals[0:1] + hat * totals[1:2]))
        grad = jnp.where(valid_rows(grad.shape, 8, width), grad, 0.0)
        sum_grad_ref[pl.ds(k * rows, rows), :] = grad.astype(bf16)
    back = dot_t(sum_grad_ref[...], up_ref[...])
    for k in range(clips):
        mid_grad_ref[k] = (back[k * rows : (k + 1) * rows] * gelu_slope(mid_ref[k])).astype(bf16)


def late_back_kernel(
    width, counts_ref, rz_ref, own_ref, rc_ref, taps_ref, first_ref, down_ref, skip_back_ref, hat_ref,
    first_grad_ref, entry_grad_ref, back_ref, frames, grads,
):
    clips, rows, channels = own_ref.shape
    pitch = 8
    edge = jnp.zeros((pitch, channels), f32)
    lanes = 128

    def clip_step(k, _):
        for s, source in enumerate((rz_ref, own_ref, rc_ref)):
            frames[s, pl.ds(0, pitch), :] = edge
            frames[s, pl.ds(pitch + rows, pitch), :] = edge
            frames[s, pl.ds(pitch, rows), :] = source[k].astype(f32)
        for l in range(channels // lanes):
            cols = pl.ds(l * lanes, lanes)
            grad = conv_rows(
                lambda i: taps_ref[pl.ds(26 - i, 1), cols],
                lambda a, b: frames[a, pl.ds(pitch * b, rows), cols],
                rows,
            )
            grad = grad * frame_mask(counts_ref, k, 0) * gelu_slope(first_ref[k, :, cols])
            grads[k, :, cols] = jnp.where(valid_rows(grad.shape, pitch, width), grad, 0.0)
        return 0

    lax.fori_loop(0, clips, clip_step, 0)
    for k in range(clips):
        first_grad_ref[pl.ds(k * rows, rows), :] = grads[k].astype(bf16)
    entry = dot_t(first_grad_ref[...], down_ref[...]) + skip_back_ref[...]
    one = two = None
    for k in range(clips):
        block = entry[k * rows : (k + 1) * rows]
        entry_grad_ref[k] = block
        masked = block * frame_mask(counts_ref, k, 0)
        a, b = row_sums(masked), row_sums(masked * hat_ref[k])
        one, two = (a, b) if one is None else (one + a, two + b)
    back_ref[0:1] = jnp.sum(one, axis=0, keepdims=True)
    back_ref[1:2] = jnp.sum(two, axis=0, keepdims=True)


def tap_grads(load, grad_of, steps, rows):
    def step(c, totals):
        grad = grad_of(c)
        sides = (pltpu.roll(grad, rows - 1, 0), grad, pltpu.roll(grad, 1, 0))
        new = []
        for a in range(3):
            for b in range(3):
                block = load(c, a, b)
                for e in range(3):
                    new.append(totals[9 * a + 3 * b + e] + row_sums(block * sides[e]))
        return tuple(new)

    return steps, step


def tap_table(rows_of_tap):
    swapped = (lax.axis_index("space") & 1) == 1
    rows = [jnp.where(swapped, rows_of_tap[(2 - i // 9) * 9 + i % 9], rows_of_tap[i]) for i in range(27)]
    table = jnp.concatenate(rows + [jnp.zeros_like(rows[0])] * 5, axis=0)
    table = jnp.transpose(table)
    return jnp.concatenate([table, jnp.zeros((table.shape[0], 96), f32)], axis=1)


def late_taps_kernel(rz_ref, own_ref, rc_ref, grad_ref, out_ref, frames):
    clips, rows, channels = own_ref.shape
    pitch = 8
    edge = jnp.zeros((pitch, channels), f32)
    lanes = 128
    for s, source in enumerate((rz_ref, own_ref, rc_ref)):
        for k in range(clips):
            frames[s, k, pl.ds(0, pitch), :] = edge
            frames[s, k, pl.ds(pitch + rows, pitch), :] = edge
            frames[s, k, pl.ds(pitch, rows), :] = source[k].astype(f32)
    for l in range(channels // lanes):
        cols = pl.ds(l * lanes, lanes)
        steps, step = tap_grads(
            lambda k, a, b: frames[a, k, pl.ds(pitch * b, rows), cols],
            lambda k: grad_ref[k, :, cols].astype(f32),
            clips,
            rows,
        )
        zero = jnp.zeros((8, lanes), f32)
        totals = lax.fori_loop(0, steps, step, (zero,) * 27)
        rows_of_tap = [jnp.sum(total, axis=0, keepdims=True) for total in totals]
        out_ref[cols, :] = tap_table(rows_of_tap)


def third_sums_kernel(
    rz_ref, oz_ref, oc_ref, rc_ref, gz_ref, gc_ref, act_ref, sum_grad_ref, out_ref, frames, grads, total, product
):
    k = pl.program_id(0)
    rows, channels = oz_ref.shape[1], oz_ref.shape[2]
    pitch = 16
    chunk = 2 * pitch
    lanes = 128

    @pl.when(k == 0)
    def _():
        clear_edges(frames, pitch, rows)
        total[...] = jnp.zeros_like(total)
        product[...] = jnp.zeros_like(product)

    for slot in range(2):
        product[...] += t_dot(act_ref[0, slot], sum_grad_ref[0, slot])
    fill_frames(frames, (rz_ref, oz_ref, oc_ref, rc_ref), pitch, rows)
    grads[0] = gz_ref[0].astype(f32)
    grads[1] = gc_ref[0].astype(f32)
    count = rows // chunk
    for l in range(channels // lanes):
        cols = pl.ds(l * lanes, lanes)
        totals = tuple(total[i, :, cols] for i in range(27))
        for slot in range(2):
            steps, step = tap_grads(
                lambda c, a, b: frames[
                    slot + a, pl.ds(pl.multiple_of(c * chunk + pitch * b, pitch), chunk), cols
                ],
                lambda c: grads[slot, pl.ds(pl.multiple_of(c * chunk, chunk), chunk), cols],
                count,
                chunk,
            )
            totals = lax.fori_loop(0, steps, step, totals)
        for i in range(27):
            total[i, :, cols] = totals[i]

    @pl.when(k == pl.num_programs(0) - 1)
    def _():
        wide = product.shape[1]
        out_ref[:, pl.ds(0, wide)] = product[...].astype(bf16)
        out_ref[:, pl.ds(wide, lanes)] = tap_table(
            [jnp.sum(total[i], axis=0, keepdims=True) for i in range(27)]
        ).astype(bf16)


def pack_kernel(parts, count, back_ref, third_ref, taps_ref, *refs):
    received, (pooled_ref, out_ref) = refs[:count], refs[count:]
    clips, late_wide = pooled_ref.shape
    pooled_ref[...] = received_sum(received)[2:].astype(bf16)
    pooled = pooled_ref[...].astype(f32)
    wide = third_ref.shape[1]
    own, own_third, own_taps = late_wide // parts, wide // parts, taps_ref.shape[0] // parts
    for d in range(parts):
        at = pl.ds(d * own // 128 * 128, 128)
        third_at = pl.ds(d * own_third // 128 * 128, 128)
        out_ref[d, 0:2] = back_ref[:, at]
        out_ref[d, 2:4] = third_ref[:, third_at]
        out_ref[d, 4 : 4 + clips] = pooled[:, d * own // 128 * 128 : d * own // 128 * 128 + 128]
        out_ref[d, pl.ds(4 + clips, own_taps)] = taps_ref[pl.ds(d * own_taps, own_taps), :]


def third_grad_kernel(
    width, cells, parts, counts_ref, *refs
):
    received, refs = refs[:parts], refs[parts:]
    (stats_ref, act_ref, mid_ref, entry_grad_ref, gain_ref, up_ref,
     sum_grad_ref, gz_ref, gc_ref, placed) = refs
    k = pl.program_id(0)
    totals = received_sum(received) / cell_total(counts_ref, False, cells)
    rows = act_ref.shape[2]
    pitch = 16
    chunk = 2 * pitch
    half = pitch // 2
    center, scale = stats_ref[0:1], stats_ref[1:2]
    lead = gain_ref[...] * scale

    @pl.when(k == 0)
    def _():
        placed[...] = jnp.zeros_like(placed)

    for j in range(rows // chunk):
        put_even(
            placed, frame_of(0) * rows + chunk * j, lead * entry_grad_ref[0, pl.ds(half * j, half), :]
        )
    for slot, out in ((0, gz_ref), (1, gc_ref)):
        weight = frame_mask(counts_ref, k, frame_of(slot))
        slope_hat = -(lead * scale * totals[1:2]) * weight
        offset = -(lead * (totals[0:1] - center * scale * totals[1:2])) * weight
        third = dot(act_ref[0, slot], up_ref[...])
        grad = get_lanes(placed, slot * rows, rows) + (offset + third * slope_hat)
        sum_grad_ref[0, slot] = grad.astype(bf16)
        back = dot_t(sum_grad_ref[0, slot], up_ref[...]) * gelu_slope(mid_ref[0, slot])
        out[0] = jnp.where(valid_rows(back.shape, pitch, width), back, 0.0).astype(bf16)


def first_grad_kernel(
    width, counts_ref, rz_ref, gz_ref, gc_ref, rc_ref, taps_ref, first_ref, x_ref,
    grad_ref, down_grad_ref, frames, xpad, product,
):
    k = pl.program_id(0)
    rows = gz_ref.shape[1]
    height, width = x_ref.shape[2], x_ref.shape[3]
    pitch = 16
    chunk = 2 * pitch

    @pl.when(k == 0)
    def _():
        clear_edges(frames, pitch, rows)
        xpad[...] = jnp.zeros_like(xpad)
        product[...] = jnp.zeros_like(product)

    fill_frames(frames, (rz_ref, gz_ref, gc_ref, rc_ref), pitch, rows)
    for slot in range(2):
        frame = frame_of(slot)
        for h in range(height):
            xpad[pl.ds(slot * rows + h * pitch, width), :] = x_ref[0, frame, h]
        scale = frame_mask(counts_ref, k, frame)

        def step(c, _):
            start = pl.multiple_of(c * chunk, chunk)
            grad = conv_rows(
                lambda i: taps_ref[pl.ds(26 - i, 1), :],
                lambda a, b: frames[slot + a, pl.ds(pl.multiple_of(start + pitch * b, pitch), chunk), :],
                chunk,
            )
            grad = grad * scale * gelu_slope(first_ref[0, slot, pl.ds(start, chunk), :])
            grad = jnp.where(valid_rows(grad.shape, pitch, width), grad, 0.0)
            grad_ref[0, pl.ds(pl.multiple_of(slot * rows + start, chunk), chunk), :] = grad.astype(bf16)
            return 0

        lax.fori_loop(0, rows // chunk, step, 0)
    product[...] += t_dot(xpad[...], grad_ref[0])

    @pl.when(k == pl.num_programs(0) - 1)
    def _():
        down_grad_ref[...] = product[...].astype(bf16)


def clip_grad_kernel(grad_ref, down_ref, entry_grad_ref, out_ref, wide):
    _, _, height, width, _ = out_ref.shape
    pitch = 16
    half = pitch // 2
    rows = height * pitch
    for slot in range(2):
        put_lanes(wide, slot * rows, dot_t(grad_ref[0, pl.ds(slot * rows, rows), :], down_ref[...]))
    for j in range(height // 2):
        at = frame_of(0) * rows + 2 * pitch * j
        put_even(wide, at, get_even(wide, at, half) + entry_grad_ref[0, pl.ds(half * j, half), :])
    for slot in range(2):
        frame = frame_of(slot)
        for h in range(height):
            out_ref[0, frame, h] = get_lanes(wide, slot * rows + h * pitch, width).astype(bf16)


smem = pl.BlockSpec(memory_space=pltpu.SMEM)


def whole(shape):
    return pl.BlockSpec(shape, lambda k: (0,) * len(shape))


def by_clip(shape):
    return pl.BlockSpec((1,) + shape[1:], lambda k: (k,) + (0,) * (len(shape) - 1))


def call(kernel, name, inputs, outputs, scratch, clips=None, limit=60, flops=0):
    if clips is None:
        def spec(kind, shape):
            return smem if kind == "s" else pl.BlockSpec(memory_space=pltpu.VMEM)
    else:
        def spec(kind, shape):
            return smem if kind == "s" else whole(shape) if kind == "w" else by_clip(shape)
    size = sum(math.prod(a.shape) * a.dtype.itemsize for a, _ in inputs)
    size += sum(math.prod(s) * jnp.dtype(d).itemsize for s, d, _ in outputs)
    options = {} if clips is None else {"grid": (clips,)}
    return pl.pallas_call(
        kernel,
        name=name,
        out_shape=[jax.ShapeDtypeStruct(s, d) for s, d, _ in outputs],
        in_specs=[spec(kind, a.shape) for a, kind in inputs],
        out_specs=[spec(kind, s) for s, _, kind in outputs],
        scratch_shapes=scratch,
        compiler_params=pltpu.CompilerParams(vmem_limit_bytes=limit * mib),
        cost_estimate=pl.CostEstimate(flops=flops, bytes_accessed=size, transcendentals=0),
        **options,
    )(*[a for a, _ in inputs])


def group_parts(values):
    size = lax.axis_size("space")
    if size > 8:
        copies = jnp.broadcast_to(values[None], (size,) + values.shape)
        return [lax.all_to_all(copies, "space", split_axis=0, concat_axis=0, tiled=True)]
    pair = values + lax.ppermute(values, "space", [(i, i ^ 1) for i in range(size)])
    others = [lax.ppermute(pair, "space", [(i, i ^ b) for i in range(size)]) for b in range(2, size, 2)]
    return [part[None] for part in [pair] + others]


def swap_neighbours(to_z, to_core):
    size = lax.axis_size("space")
    core = [(i, i ^ 1) for i in range(size)]
    z = [(i, j) for m in range(1, size - 1, 2) for i, j in ((m, m + 1), (m + 1, m))]
    return lax.ppermute(to_z, "space", z), lax.ppermute(to_core, "space", core)


def reduce_rows(term):
    return add_rows(send_rows(term))


def add_rows(received):
    return jnp.sum(received.astype(f32), axis=0)


def send_rows(term):
    parts = lax.axis_size("clip") * lax.axis_size("space")
    pieces = term.astype(bf16).reshape((parts, term.shape[0] // parts) + term.shape[1:])
    return lax.all_to_all(pieces, ("clip", "space"), split_axis=0, concat_axis=0, tiled=True)


def core_swap(values):
    return lax.ppermute(values, "space", [(i, i ^ 1) for i in range(lax.axis_size("space"))])


def own_rows(left_ref, block, out):
    core = lax.axis_index("space") & 1
    out[0] = jnp.transpose(left_ref[...])
    for j in range(out.shape[1] // block // 2):
        start = pl.multiple_of((2 * j + core) * block, block)
        out[1, pl.ds(j * block, block), :] = out[0, pl.ds(start, block), :]


def skip_product_kernel(block, left_ref, left_other_ref, right_ref, right_other_ref, out_ref, left, left_other):
    half = left.shape[1] // 2

    @pl.when(pl.program_id(0) == 0)
    def _():
        own_rows(left_ref, block, left)
        own_rows(left_other_ref, block, left_other)

    total = dot(left[1, pl.ds(0, half)], right_ref[...]) + dot(left_other[1, pl.ds(0, half)], right_other_ref[...])
    for j in range(out_ref.shape[0]):
        out_ref[j] = total[j * block : (j + 1) * block].astype(bf16)


def skip_product(left, left_other, right, right_other, parts):
    block = left.shape[1] // parts
    wide = right.shape[1]
    lanes = min(wide, 512)
    rows, deep = left.shape
    return pl.pallas_call(
        functools.partial(skip_product_kernel, block),
        name="skip_product",
        grid=(wide // lanes,),
        out_shape=jax.ShapeDtypeStruct((parts // 2, block, wide), bf16),
        in_specs=[pl.BlockSpec((rows, deep), lambda n: (0, 0))] * 2
        + [pl.BlockSpec((rows, lanes), lambda n: (0, n))] * 2,
        out_specs=pl.BlockSpec((parts // 2, block, lanes), lambda n: (0, 0, n)),
        scratch_shapes=[pltpu.VMEM((2, deep, rows), bf16)] * 2,
        compiler_params=pltpu.CompilerParams(vmem_limit_bytes=60 * mib),
        cost_estimate=pl.CostEstimate(
            flops=2 * rows * deep * wide, bytes_accessed=deep * wide + 4 * rows * (deep + wide), transcendentals=0
        ),
    )(left, left_other, right, right_other)


def two_products_kernel(
    up_block, down_block, act_ref, act_other_ref, sum_ref, sum_other_ref,
    entry_ref, entry_other_ref, first_ref, first_other_ref, out_ref, act, act_other, entry, entry_other,
):
    own_rows(act_ref, up_block, act)
    own_rows(act_other_ref, up_block, act_other)
    own_rows(entry_ref, down_block, entry)
    own_rows(entry_other_ref, down_block, entry_other)
    half = act.shape[1] // 2
    up = dot(act[1, pl.ds(0, half)], sum_ref[...]) + dot(act_other[1, pl.ds(0, half)], sum_other_ref[...])
    half = entry.shape[1] // 2
    down = dot(entry[1, pl.ds(0, half)], first_ref[...]) + dot(entry_other[1, pl.ds(0, half)], first_other_ref[...])
    fold = up.shape[1] // down.shape[1]
    part = down_block // fold
    for j in range(out_ref.shape[0]):
        block = down[j * down_block : (j + 1) * down_block]
        block = jnp.concatenate([block[i * part : (i + 1) * part] for i in range(fold)], axis=1)
        out_ref[j] = jnp.concatenate([up[j * up_block : (j + 1) * up_block], block], axis=0).astype(bf16)


def after(values, token):
    return lax.optimization_barrier((values, token))[0]


def sum_over_clip(pieces):
    return lax.psum_scatter(pieces, "clip", scatter_dimension=0, tiled=True)


def sum_over_chips(pieces):
    size = lax.axis_size("space")
    groups = [[2 * z + c for z in range(size // 2)] for c in range(2)]
    return lax.psum_scatter(pieces, "space", scatter_dimension=0, tiled=True, axis_index_groups=groups)


def per_device(
    clip_input, frame_counts, third_down, third_depth, third_up, third_gain, third_shift,
    fourth_down, fourth_skip, fourth_depth, fourth_up, fourth_gain, fourth_shift,
    classifier, class_bias, logit_grad,
):
    clips, frames, height, width, channels = clip_input.shape
    inner = third_down.shape[1]
    late_inner = fourth_down.shape[1]
    late_wide = fourth_up.shape[1]
    half_width = width // 2
    rows = height * 16
    late_rows = height // 2 * 8
    late_all = clips * late_rows
    flip = (lax.axis_index("space") & 1) == 1
    cells = height * width
    late_cells = (height // 2) * half_width

    def tap_rows(kernel):
        taps = jnp.transpose(kernel).reshape(3, 9, -1)
        return jnp.where(flip, taps[::-1], taps).reshape(27, -1)

    third_taps = tap_rows(third_depth)
    late_taps = tap_rows(fourth_depth)
    third_gain, third_shift = third_gain[None], third_shift[None]
    fourth_gain, fourth_shift = fourth_gain[None], fourth_shift[None]

    own_start = lax.axis_index("clip") * clips
    grad_rows = lax.dynamic_slice_in_dim(logit_grad, own_start, clips, 0)
    pooled_grad = lax.dot_general(
        grad_rows, classifier.astype(f32), (((1,), (1,)), ((), ())), precision=lax.Precision.HIGHEST
    ).astype(bf16).astype(f32)

    first, act_z, act_c, even_x = call(
        first_kernel, "first",
        [(frame_counts, "s"), (clip_input, "c"), (third_down, "w")],
        [
            ((clips, 2, rows, inner), f32, "c"),
            ((clips, rows, inner), bf16, "c"),
            ((clips, rows, inner), bf16, "c"),
            ((clips, late_rows, channels), f32, "c"),
        ],
        [pltpu.VMEM((rows, channels), bf16), pltpu.VMEM((channels // 128, 16, 128), f32)],
        clips=clips,
    )
    got_z, got_c = swap_neighbours(act_z, act_c)
    mid, mid_act, even_sum, moments = call(
        functools.partial(mid_kernel, width), "mid",
        [(frame_counts, "s"), (got_z, "c"), (act_z, "c"), (act_c, "c"), (got_c, "c"),
         (third_taps, "w"), (third_up, "w")],
        [
            ((clips, 2, rows, inner), f32, "c"),
            ((clips, 2, rows, inner), bf16, "c"),
            ((clips, late_rows, channels), f32, "c"),
            ((2, channels), f32, "w"),
        ],
        [
            pltpu.VMEM((4, rows + 32, inner), f32),
            pltpu.VMEM((channels // 128, 2 * rows, 128), f32),
            pltpu.VMEM((2, 8, channels), f32),
        ],
        clips=clips,
    )
    moments = [(part, "w") for part in group_parts(moments)]
    stats, even_hat, entry, late_first, late_act = call(
        functools.partial(entry_kernel, half_width, cells, len(moments)), "entry",
        [(frame_counts, "s"), *moments, (even_x, "w"), (even_sum, "w"),
         (third_gain, "w"), (third_shift, "w"), (fourth_down, "w")],
        [
            ((2, channels), f32, "w"),
            ((clips, late_rows, channels), f32, "w"),
            ((late_all, channels), bf16, "w"),
            ((late_all, late_inner), f32, "w"),
            ((clips, late_rows, late_inner), bf16, "w"),
        ],
        [],
    )
    late_first = late_first.reshape(clips, late_rows, late_inner)
    late_z, late_c = swap_neighbours(late_act, late_act)
    skipped = dot(entry, fourth_skip).astype(bf16).reshape(clips, late_rows, late_wide)
    late_mid, late_mid_act, late_sum, late_moments = call(
        functools.partial(late_kernel, half_width), "late_mid",
        [(frame_counts, "s"), (late_z, "w"), (late_act, "w"), (late_c, "w"), (late_taps, "w"), (fourth_up, "w")],
        [
            ((clips, late_rows, late_inner), f32, "w"),
            ((late_all, late_inner), bf16, "w"),
            ((late_all, late_wide), bf16, "w"),
            ((2, late_wide), f32, "w"),
        ],
        [
            pltpu.VMEM((3, late_rows + 16, late_inner), f32),
            pltpu.VMEM((clips, late_rows, late_inner), f32),
        ],
    )
    late_sum = late_sum.reshape(clips, late_rows, late_wide)
    late_moments = [(part, "w") for part in group_parts(late_moments)]
    late_stats, late_back, pooled_term, pre_grad, skip_grad = call(
        functools.partial(post_kernel, half_width, late_cells, len(late_moments)), "post",
        [(frame_counts, "s"), *late_moments, (late_sum, "w"), (skipped, "w"),
         (fourth_gain, "w"), (fourth_shift, "w"), (pooled_grad, "w")],
        [
            ((2, late_wide), f32, "w"),
            ((2, late_wide), f32, "w"),
            ((clips, late_wide), f32, "w"),
            ((clips, late_rows, late_wide), f32, "w"),
            ((clips, late_rows, late_wide), bf16, "w"),
        ],
        [],
    )
    received = group_parts(jnp.concatenate((late_back, pooled_term)))
    skip_rows = skip_grad.reshape(late_all, late_wide)
    skip_back = dot_t(skip_rows, fourth_skip)
    parts = lax.axis_size("clip") * lax.axis_size("space")
    by_pairs = channels // parts % 32 == 0 and late_inner // parts % 16 == 0
    if by_pairs:
        entry_other = core_swap(entry)
        skip_pieces = skip_product(entry, entry_other, after(skip_rows, received[0]), core_swap(skip_rows), parts)
        late_stats = after(late_stats, skip_pieces)
        skip_pieces = sum_over_clip(skip_pieces)
    else:
        fourth_skip_grad = reduce_rows(t_dot(entry, skip_rows))
    late_sum_grad, late_mid_grad = call(
        functools.partial(sum_grad_kernel, half_width, late_cells, len(received)), "sum_grad",
        [(frame_counts, "s"), *[(part, "w") for part in received], (late_stats, "w"), (late_sum, "w"), (pre_grad, "w"),
         (fourth_gain, "w"), (fourth_up, "w"), (late_mid, "w")],
        [((late_all, late_wide), bf16, "w"), ((clips, late_rows, late_inner), bf16, "w")],
        [],
    )
    late_gz, late_gc = swap_neighbours(late_mid_grad, late_mid_grad)
    late_first_grad, entry_grad, third_back = call(
        functools.partial(late_back_kernel, half_width), "late_back",
        [(frame_counts, "s"), (late_gz, "w"), (late_mid_grad, "w"), (late_gc, "w"), (late_taps, "w"),
         (late_first, "w"), (fourth_down, "w"), (skip_back, "w"), (even_hat, "w")],
        [
            ((late_all, late_inner), bf16, "w"),
            ((clips, late_rows, channels), f32, "w"),
            ((2, channels), f32, "w"),
        ],
        [
            pltpu.VMEM((3, late_rows + 16, late_inner), f32),
            pltpu.VMEM((clips, late_rows, late_inner), f32),
        ],
    )
    back_parts = group_parts(third_back)
    (late_taps_table,) = call(
        late_taps_kernel, "late_taps",
        [(late_z, "w"), (late_act, "w"), (late_c, "w"), (after(late_mid_grad, back_parts[0]), "w")],
        [((late_inner, 128), f32, "w")],
        [pltpu.VMEM((3, clips, late_rows + 16, late_inner), f32)],
    )
    if by_pairs:
        up_block, down_block = late_inner // parts, channels // parts
        (pieces,) = call(
            functools.partial(two_products_kernel, up_block, down_block), "two_products",
            [(late_mid_act, "w"), (core_swap(late_mid_act), "w"), (after(late_sum_grad, back_parts[0]), "w"), (core_swap(late_sum_grad), "w"),
             (entry, "w"), (entry_other, "w"), (late_first_grad, "w"), (core_swap(late_first_grad), "w")],
            [((parts // 2, up_block + down_block * late_inner // late_wide, late_wide), bf16, "w")],
            [pltpu.VMEM((2, late_inner, late_all), bf16)] * 2 + [pltpu.VMEM((2, channels, late_all), bf16)] * 2,
        )
        stats = after(stats, pieces)
        pieces = sum_over_clip(pieces)
    else:
        fourth_up_grad = reduce_rows(t_dot(late_mid_act, late_sum_grad))
        fourth_down_grad = reduce_rows(t_dot(entry, late_first_grad))
    back_parts = [(part, "w") for part in back_parts]
    third_sum_grad, grad_z, grad_c = call(
        functools.partial(third_grad_kernel, width, cells, len(back_parts)), "third_grad",
        [(frame_counts, "s"), *back_parts, (stats, "w"), (mid_act, "c"), (mid, "c"),
         (entry_grad, "c"), (third_gain, "w"), (third_up, "w")],
        [
            ((clips, 2, rows, channels), bf16, "c"),
            ((clips, rows, inner), bf16, "c"),
            ((clips, rows, inner), bf16, "c"),
        ],
        [pltpu.VMEM((channels // 128, 2 * rows, 128), f32)],
        clips=clips,
    )
    third_gz, third_gc = swap_neighbours(grad_z, grad_c)
    (third_terms,) = call(
        third_sums_kernel, "third_sums",
        [(got_z, "c"), (act_z, "c"), (act_c, "c"), (got_c, "c"), (grad_z, "c"), (grad_c, "c"),
         (mid_act, "c"), (third_sum_grad, "c")],
        [((inner, channels + 128), bf16, "w")],
        [
            pltpu.VMEM((4, rows + 32, inner), f32),
            pltpu.VMEM((2, rows, inner), f32),
            pltpu.VMEM((27, 8, inner), f32),
            pltpu.VMEM((inner, channels), f32),
        ],
        clips=clips,
    )
    first = after(first, third_terms)
    third_terms = send_rows(third_terms)
    first_grad, third_down_term = call(
        functools.partial(first_grad_kernel, width), "first_grad",
        [(frame_counts, "s"), (third_gz, "c"), (grad_z, "c"), (grad_c, "c"), (third_gc, "c"),
         (third_taps, "w"), (first, "c"), (clip_input, "c")],
        [((clips, 2 * rows, inner), bf16, "c"), ((channels, inner), bf16, "w")],
        [
            pltpu.VMEM((4, rows + 32, inner), f32),
            pltpu.VMEM((2 * rows, channels), bf16),
            pltpu.VMEM((channels, inner), f32),
        ],
        clips=clips,
    )
    third_down_rows = send_rows(third_down_term)
    if by_pairs:
        pieces = jnp.concatenate((after(skip_pieces, first_grad), pieces), axis=1)
        pieces = sum_over_chips(pieces)[0].astype(f32)
        fourth_skip_grad = pieces[:down_block]
        fourth_up_grad = pieces[down_block : down_block + up_block]
        fold = late_wide // late_inner
        fourth_down_grad = jnp.moveaxis(
            pieces[down_block + up_block :].reshape(-1, fold, late_inner), 1, 0
        ).reshape(down_block, late_inner)
    third_terms = add_rows(after(third_terms, first_grad))
    (clip_grad,) = call(
        clip_grad_kernel, "clip_grad",
        [(first_grad, "c"), (third_down, "w"), (entry_grad, "c")],
        [(clip_input.shape, bf16, "c")],
        [pltpu.VMEM((channels // 128, 2 * rows, 128), f32)],
        clips=clips,
    )

    own, own_third, own_taps = late_wide // parts, channels // parts, late_inner // parts
    pooled, packed = call(
        functools.partial(pack_kernel, parts, len(received)), "pack",
        [(late_back, "w"), (third_back, "w"), (late_taps_table, "w"), *[(part, "w") for part in received]],
        [((clips, late_wide), bf16, "w"), ((parts, 4 + clips + own_taps, 128), f32, "w")],
        [],
    )
    logits = dot(pooled, classifier) + class_bias
    packed = lax.all_to_all(packed, ("clip", "space"), split_axis=0, concat_axis=0, tiled=True)
    packed = after(packed, first_grad)
    device = lax.axis_index("clip") * lax.axis_size("space") + lax.axis_index("space")
    totals = jnp.sum(packed, axis=0)
    late_sums = lax.dynamic_slice_in_dim(totals[0:2], device * own % 128, own, 1)
    third_sums = lax.dynamic_slice_in_dim(totals[2:4], device * own_third % 128, own_third, 1)
    fourth_depth_grad = totals[4 + clips :, :27]
    gathered = packed.reshape((lax.axis_size("clip"), lax.axis_size("space")) + packed.shape[1:])[:, 0, 4 : 4 + clips]
    gathered = lax.dynamic_slice_in_dim(gathered.reshape(-1, 128), device * own % 128, own, 1)
    classifier_grad = lax.dot_general(
        gathered, logit_grad, (((0,), (0,)), ((), ())), precision=lax.Precision.HIGHEST
    )
    return (
        logits,
        clip_grad,
        add_rows(third_down_rows),
        third_terms[:, channels : channels + 27],
        third_terms[:, :channels],
        third_sums[1],
        third_sums[0],
        fourth_down_grad,
        fourth_skip_grad,
        fourth_depth_grad,
        fourth_up_grad,
        late_sums[1],
        late_sums[0],
        classifier_grad,
        jnp.sum(logit_grad, axis=0),
    )


def solution(mesh):
    both = ("clip", "space")
    return jax.shard_map(
        per_device,
        mesh=mesh,
        in_specs=(P("clip", "space", None, None, None), P("clip")) + (P(),) * 14,
        out_specs=(
            P("clip", None),
            P("clip", "space", None, None, None),
            P(both, None),
            P(both, None),
            P(both, None),
            P(both),
            P(both),
            P(both, None),
            P(both, None),
            P(both, None),
            P(both, None),
            P(both),
            P(both),
            P(both, None),
            P(),
        ),
        check_vma=False,
    )
```

```python
import functools
import math

import jax
import jax.numpy as jnp
from jax import lax
from jax.experimental import pallas as pl
from jax.experimental.pallas import tpu as pltpu
from jax.sharding import PartitionSpec as P

eps = 1e-05
f32 = jnp.float32
bf16 = jnp.bfloat16
mib = 1 << 20
LIMIT = 16


def gelu_terms(x):
    c = math.sqrt(2.0 / math.pi)
    x2 = x * x
    t = jnp.tanh(x * (c + (c * 0.044715) * x2))
    return x2, t


def gelu(x):
    _, t = gelu_terms(x)
    return x * (0.5 + 0.5 * t)


def gelu_slope(x):
    c = math.sqrt(2.0 / math.pi)
    x2, t = gelu_terms(x)
    return 0.5 + 0.5 * t + (0.5 * x) * ((1.0 - t * t) * (c + (3.0 * c * 0.044715) * x2))


def gelu_both(x):
    c = math.sqrt(2.0 / math.pi)
    x2, t = gelu_terms(x)
    cdf = 0.5 + 0.5 * t
    return x * cdf, cdf + (0.5 * x) * ((1.0 - t * t) * (c + (3.0 * c * 0.044715) * x2))


def valid_rows(shape, group, used):
    return lax.broadcasted_iota(jnp.int32, shape, 0) % group < used


def row_sums(values):
    rows, width = values.shape
    return jnp.sum(values.reshape(rows // 8, 8, width), axis=0)


def dot(left, right):
    return jnp.dot(left, right, preferred_element_type=f32)


def dot_t(left, right):
    return lax.dot_general(left, right, (((1,), (1,)), ((), ())), preferred_element_type=f32)


def t_dot(left, right):
    return lax.dot_general(left, right, (((0,), (0,)), ((), ())), preferred_element_type=f32)


def put_lanes(ref, start, values):
    rows, channels = values.shape
    for j in range(channels // 128):
        ref[j, pl.ds(start, rows), :] = values[:, 128 * j : 128 * (j + 1)]


def get_lanes(ref, start, rows):
    return jnp.concatenate([ref[j, pl.ds(start, rows), :] for j in range(ref.shape[0])], axis=1)


def get_even(ref, start, count):
    return jnp.concatenate(
        [ref[j, pl.ds(start, count, stride=2), :] for j in range(ref.shape[0])], axis=1
    )


def put_even(ref, start, values):
    rows, channels = values.shape
    for j in range(channels // 128):
        ref[j, pl.ds(start, rows, stride=2), :] = values[:, 128 * j : 128 * (j + 1)]


def conv_rows(taps, load, rows, times=(0, 1, 2)):
    sums = [None, None, None]
    for a in times:
        for b in range(3):
            block = load(a, b)
            for e in range(3):
                term = block * taps(9 * a + 3 * b + e)
                sums[e] = term if sums[e] is None else sums[e] + term
    return pltpu.roll(sums[0], 1, 0) + sums[1] + pltpu.roll(sums[2], rows - 1, 0)


def split(values, count):
    parts = []
    for _ in range(count):
        parts.append(values.astype(bf16))
        values = values - parts[-1].astype(f32)
    return parts


def frame_of(slot):
    parity = lax.axis_index("space") & 1
    return parity if slot == 0 else 1 - parity


def frame_mask(counts_ref, k, frame):
    return jnp.where(2 * lax.axis_index("space") + frame < counts_ref[k], 1.0, 0.0).astype(f32)


def cell_total(counts_ref, late, cells):
    total = 0
    for k in range(counts_ref.shape[0]):
        total += (counts_ref[k] + 1) // 2 if late else counts_ref[k]
    return (total * cells).astype(f32)


def received_sum(refs):
    total = None
    for ref in refs:
        for i in range(ref.shape[0]):
            total = ref[i] if total is None else total + ref[i]
    return total


def taps_kernel(third_ref, fourth_ref, third_out, fourth_out):
    swapped = (lax.axis_index("space") & 1) == 1
    for source, out in ((third_ref, third_out), (fourth_ref, fourth_out)):
        for a in range(3):
            here, there = source[pl.ds(9 * a, 9), :], source[pl.ds(9 * (2 - a), 9), :]
            out[pl.ds(9 * a, 9), :] = jnp.where(swapped, there, here)


def pooled_grad_kernel(grad_ref, head_ref, out_ref):
    full = sum(dot(part, head_ref[...]) for part in split(grad_ref[...], 3))
    clips = out_ref.shape[0]
    clip = lax.axis_index("clip")
    own = full[:clips]
    for g in range(1, full.shape[0] // clips):
        own = jnp.where(clip == g, full[g * clips : (g + 1) * clips], own)
    out_ref[...] = own.astype(bf16).astype(f32)


def head_kernel(pooled_ref, head_ref, bias_ref, grad_ref, logits_ref, bias_grad_ref):
    logits_ref[...] = dot_t(pooled_ref[...], head_ref[...]) + bias_ref[...]
    bias_grad_ref[...] = jnp.sum(grad_ref[...], axis=0, keepdims=True)


def add_kernel(one_ref, two_ref, out_ref):
    out_ref[...] = one_ref[...] + two_ref[...]


def skipped_kernel(entry_ref, weight_ref, out_ref):
    out_ref[...] = dot(entry_ref[...], weight_ref[...]).astype(bf16)


def first_kernel(counts_ref, x_ref, w_ref, first_ref, actz_ref, actc_ref, even_ref, xpad, xe):
    k = pl.program_id(0)
    _, _, height, width, _ = x_ref.shape
    pitch = xe.shape[1]

    @pl.when(k == 0)
    def _():
        xpad[...] = jnp.zeros_like(xpad)
        xe[...] = jnp.zeros_like(xe)

    for slot, act_ref in ((0, actz_ref), (1, actc_ref)):
        frame = frame_of(slot)
        for h in range(height):
            xpad[pl.ds(h * pitch, width), :] = x_ref[0, frame, h]
        first = dot(xpad[...], w_ref[...])
        first_ref[0, slot] = first
        act_ref[0] = (gelu(first) * frame_mask(counts_ref, k, frame)).astype(bf16)
    for h in range(0, height, 2):
        put_lanes(xe, 0, x_ref[0, 0, h].astype(f32))
        even_ref[0, pl.ds(h // 2 * (pitch // 2), pitch // 2), :] = get_even(xe, 0, pitch // 2)


def fill_frames(frames, sources, pad, rows):
    for s, source in enumerate(sources):
        frames[s, pl.ds(pad, rows), :] = source[0].astype(f32)


def clear_edges(frames, pad, rows):
    edge = jnp.zeros((pad, frames.shape[-1]), f32)
    for s in range(frames.shape[0]):
        frames[s, pl.ds(0, pad), :] = edge
        frames[s, pl.ds(pad + rows, pad), :] = edge


def mid_own_kernel(oz_ref, oc_ref, taps_ref, part_ref, frames):
    rows = oz_ref.shape[1]
    pitch = 16
    chunk = 2 * pitch

    @pl.when(pl.program_id(0) == 0)
    def _():
        clear_edges(frames, pitch, rows)

    fill_frames(frames, (oz_ref, oc_ref), pitch, rows)
    for slot in range(2):
        def step(c, _):
            start = pl.multiple_of(c * chunk, chunk)
            part_ref[0, slot, pl.ds(start, chunk), :] = conv_rows(
                lambda i: taps_ref[pl.ds(i, 1), :],
                lambda a, b: frames[slot + a - 1, pl.ds(pl.multiple_of(start + pitch * b, pitch), chunk), :],
                chunk,
                (1, 2) if slot == 0 else (0, 1),
            )
            return 0

        lax.fori_loop(0, rows // chunk, step, 0)


def mid_kernel(
    width, counts_ref, rz_ref, rc_ref, part_ref, taps_ref, up_ref,
    mid_ref, act_ref, act_even_ref, even_ref, moment_ref, gram_up_ref, act_sum_ref,
    frames, acts, evens, gram, total,
):
    k = pl.program_id(0)
    rows = rz_ref.shape[1]
    pitch = 16
    chunk = 2 * pitch
    half = pitch // 2

    @pl.when(k == 0)
    def _():
        clear_edges(frames, pitch, rows)
        gram[...] = jnp.zeros_like(gram)
        total[...] = jnp.zeros_like(total)

    fill_frames(frames, (rz_ref, rc_ref), pitch, rows)
    for slot in range(2):
        def step(c, _):
            start = pl.multiple_of(c * chunk, chunk)
            mid = part_ref[0, slot, pl.ds(start, chunk), :] + conv_rows(
                lambda i: taps_ref[pl.ds(i, 1), :],
                lambda a, b: frames[slot, pl.ds(pl.multiple_of(start + pitch * b, pitch), chunk), :],
                chunk,
                (0,) if slot == 0 else (2,),
            )
            mid_ref[0, slot, pl.ds(start, chunk), :] = mid
            act = jnp.where(valid_rows(mid.shape, pitch, width), gelu(mid), 0.0)
            act_ref[0, slot, pl.ds(start, chunk), :] = act.astype(bf16)
            put_lanes(acts, slot * rows + start, act)
            return 0

        lax.fori_loop(0, rows // chunk, step, 0)
        act = act_ref[0, slot]
        mask = frame_mask(counts_ref, k, frame_of(slot))
        gram[...] += t_dot(act, act) * mask
        total[...] += row_sums(act.astype(f32)) * mask
    for j in range(rows // chunk):
        at = pl.multiple_of(k * (rows // 4) + half * j, half)
        evens[pl.ds(at, half), :] = get_even(acts, frame_of(0) * rows + chunk * j, half)

    @pl.when(k == pl.num_programs(0) - 1)
    def _():
        act_even_ref[...] = evens[...].astype(bf16)
        even_ref[...] = dot(act_even_ref[...], up_ref[...])
        gram_up = sum(dot(part, up_ref[...]) for part in split(gram[...], 3))
        gram_up_ref[...] = gram_up
        act_sum = jnp.sum(total[...], axis=0, keepdims=True)
        act_sum_ref[...] = act_sum
        rows_of_sum = jnp.concatenate(
            [part.astype(f32) for part in split(act_sum, 3)] + [jnp.zeros((5,) + act_sum.shape[1:], f32)], axis=0
        ).astype(bf16)
        moment_ref[0:1] = jnp.sum(dot(rows_of_sum, up_ref[...]), axis=0, keepdims=True)
        moment_ref[1:2] = jnp.sum(gram_up * up_ref[...].astype(f32), axis=0, keepdims=True)


def norm_stats(refs, cells):
    totals = received_sum(refs)
    center = totals[0:1] / cells
    return center, lax.rsqrt(totals[1:2] / cells - center * center + eps)


def entry_kernel(
    width, cells, count, counts_ref, *refs
):
    moments, refs = refs[:count], refs[count:]
    (even_x_ref, even_ref, gain_ref, shift_ref, down_ref, stats_ref, hat_ref, entry_ref, first_ref, act_ref) = refs
    center, scale = norm_stats(moments, cell_total(counts_ref, False, cells))
    stats_ref[0:1] = center
    stats_ref[1:2] = scale
    clips, rows, channels = even_ref.shape
    for k in range(clips):
        hat = (even_ref[k] - center) * scale
        hat_ref[k] = hat
        entry = even_x_ref[k] + hat * gain_ref[...] + shift_ref[...]
        entry = jnp.where(valid_rows(entry.shape, 8, width), entry, 0.0)
        entry_ref[pl.ds(k * rows, rows), :] = entry.astype(bf16)
    late = dot(entry_ref[...], down_ref[...])
    first_ref[...] = late
    for k in range(clips):
        act_ref[k] = (gelu(late[k * rows : (k + 1) * rows]) * frame_mask(counts_ref, k, 0)).astype(bf16)


def late_kernel(
    width, counts_ref, rz_ref, own_ref, rc_ref, taps_ref, up_ref,
    mid_ref, act_ref, sum_ref, moment_ref, frames, wide,
):
    clips, rows, channels = own_ref.shape
    pitch = 8
    edge = jnp.zeros((pitch, channels), f32)
    lanes = 128

    def clip_step(k, _):
        for s, source in enumerate((rz_ref, own_ref, rc_ref)):
            frames[s, pl.ds(0, pitch), :] = edge
            frames[s, pl.ds(pitch + rows, pitch), :] = edge
            frames[s, pl.ds(pitch, rows), :] = source[k].astype(f32)
        for l in range(channels // lanes):
            cols = pl.ds(l * lanes, lanes)
            mid = conv_rows(
                lambda i: taps_ref[pl.ds(i, 1), cols],
                lambda a, b: frames[a, pl.ds(pitch * b, rows), cols],
                rows,
            )
            mid_ref[k, :, cols] = mid
            wide[k, :, cols] = jnp.where(valid_rows(mid.shape, pitch, width), gelu(mid), 0.0)
        return 0

    lax.fori_loop(0, clips, clip_step, 0)
    for k in range(clips):
        act_ref[pl.ds(k * rows, rows), :] = wide[k].astype(bf16)
    late = dot(act_ref[...], up_ref[...]).astype(bf16)
    sum_ref[...] = late
    late = late.astype(f32)
    one = two = None
    for k in range(clips):
        block = late[k * rows : (k + 1) * rows]
        mask = frame_mask(counts_ref, k, 0)
        a, b = row_sums(block) * mask, row_sums(block * block) * mask
        one, two = (a, b) if one is None else (one + a, two + b)
    moment_ref[0:1] = jnp.sum(one, axis=0, keepdims=True)
    moment_ref[1:2] = jnp.sum(two, axis=0, keepdims=True)


def post_kernel(
    width, cells, count, counts_ref, *refs
):
    moments, refs = refs[:count], refs[count:]
    (sum_ref, skip_ref, gain_ref, shift_ref, pooled_grad_ref, stats_ref, back_ref, pre_ref, skip_grad_ref) = refs
    center, scale = norm_stats(moments, cell_total(counts_ref, True, cells))
    stats_ref[0:1] = center
    stats_ref[1:2] = scale
    clips, rows, channels = sum_ref.shape
    one = two = None
    for k in range(clips):
        hat = (sum_ref[k].astype(f32) - center) * scale
        post, slope = gelu_both(hat * gain_ref[...] + shift_ref[...] + skip_ref[k].astype(f32))
        keep = valid_rows(post.shape, 8, width)
        mask = frame_mask(counts_ref, k, 0)
        pool = ((counts_ref[k] + 1) // 2 * cells).astype(f32)
        pooled = jnp.sum(jnp.where(keep, post, 0.0), axis=0, keepdims=True) * mask / pool
        back_ref[pl.ds(2 + k, 1)] = pooled
        pre = jnp.where(keep, pooled_grad_ref[pl.ds(k, 1)] * mask / pool * slope, 0.0)
        pre_ref[k] = pre
        skip_grad_ref[k] = pre.astype(bf16)
        a, b = row_sums(pre), row_sums(pre * hat)
        one, two = (a, b) if one is None else (one + a, two + b)
    back_ref[0:1] = jnp.sum(one, axis=0, keepdims=True)
    back_ref[1:2] = jnp.sum(two, axis=0, keepdims=True)


def sum_grad_kernel(
    width, cells, count, counts_ref, *refs
):
    received, refs = refs[:count], refs[count:]
    (stats_ref, sum_ref, pre_ref, gain_ref, up_ref, mid_ref, sum_grad_ref, mid_grad_ref, pooled_ref) = refs
    totals = received_sum(received)
    pooled_ref[...] = totals[2:].astype(bf16)
    totals = totals[0:2] / cell_total(counts_ref, True, cells)
    center, scale = stats_ref[0:1], stats_ref[1:2]
    lead = gain_ref[...] * scale
    clips, rows, channels = sum_ref.shape
    for k in range(clips):
        hat = (sum_ref[k].astype(f32) - center) * scale
        weight = frame_mask(counts_ref, k, 0)
        grad = lead * (pre_ref[k] - weight * (totals[0:1] + hat * totals[1:2]))
        grad = jnp.where(valid_rows(grad.shape, 8, width), grad, 0.0)
        sum_grad_ref[pl.ds(k * rows, rows), :] = grad.astype(bf16)
    back = dot_t(sum_grad_ref[...], up_ref[...])
    for k in range(clips):
        mid_grad_ref[k] = (back[k * rows : (k + 1) * rows] * gelu_slope(mid_ref[k])).astype(bf16)


def late_back_kernel(
    width, counts_ref, rz_ref, own_ref, rc_ref, taps_ref, first_ref, down_ref, skip_back_ref, hat_ref,
    first_grad_ref, entry_grad_ref, back_ref, frames, grads,
):
    clips, rows, channels = own_ref.shape
    pitch = 8
    edge = jnp.zeros((pitch, channels), f32)
    lanes = 128

    def clip_step(k, _):
        for s, source in enumerate((rz_ref, own_ref, rc_ref)):
            frames[s, pl.ds(0, pitch), :] = edge
            frames[s, pl.ds(pitch + rows, pitch), :] = edge
            frames[s, pl.ds(pitch, rows), :] = source[k].astype(f32)
        for l in range(channels // lanes):
            cols = pl.ds(l * lanes, lanes)
            grad = conv_rows(
                lambda i: taps_ref[pl.ds(26 - i, 1), cols],
                lambda a, b: frames[a, pl.ds(pitch * b, rows), cols],
                rows,
            )
            grad = grad * frame_mask(counts_ref, k, 0) * gelu_slope(first_ref[k, :, cols])
            grads[k, :, cols] = jnp.where(valid_rows(grad.shape, pitch, width), grad, 0.0)
        return 0

    lax.fori_loop(0, clips, clip_step, 0)
    for k in range(clips):
        first_grad_ref[pl.ds(k * rows, rows), :] = grads[k].astype(bf16)
    entry = dot_t(first_grad_ref[...], down_ref[...]) + skip_back_ref[...]
    one = two = None
    for k in range(clips):
        block = entry[k * rows : (k + 1) * rows]
        entry_grad_ref[k] = block
        masked = block * frame_mask(counts_ref, k, 0)
        a, b = row_sums(masked), row_sums(masked * hat_ref[k])
        one, two = (a, b) if one is None else (one + a, two + b)
    back_ref[0:1] = jnp.sum(one, axis=0, keepdims=True)
    back_ref[1:2] = jnp.sum(two, axis=0, keepdims=True)


def tap_grads(load, grad_of, steps, rows):
    def step(c, totals):
        grad = grad_of(c)
        sides = (pltpu.roll(grad, rows - 1, 0), grad, pltpu.roll(grad, 1, 0))
        new = []
        for a in range(3):
            for b in range(3):
                block = load(c, a, b)
                for e in range(3):
                    new.append(totals[9 * a + 3 * b + e] + row_sums(block * sides[e]))
        return tuple(new)

    return steps, step


def tap_table(rows_of_tap):
    swapped = (lax.axis_index("space") & 1) == 1
    rows = [jnp.where(swapped, rows_of_tap[(2 - i // 9) * 9 + i % 9], rows_of_tap[i]) for i in range(27)]
    table = jnp.concatenate(rows + [jnp.zeros_like(rows[0])] * 5, axis=0)
    table = jnp.transpose(table)
    return jnp.concatenate([table, jnp.zeros((table.shape[0], 96), f32)], axis=1)


def late_taps_kernel(rz_ref, own_ref, rc_ref, grad_ref, out_ref, frames):
    clips, rows, channels = own_ref.shape
    pitch = 8
    edge = jnp.zeros((pitch, channels), f32)
    lanes = 128
    for s, source in enumerate((rz_ref, own_ref, rc_ref)):
        for k in range(clips):
            frames[s, k, pl.ds(0, pitch), :] = edge
            frames[s, k, pl.ds(pitch + rows, pitch), :] = edge
            frames[s, k, pl.ds(pitch, rows), :] = source[k].astype(f32)
    for l in range(channels // lanes):
        cols = pl.ds(l * lanes, lanes)
        steps, step = tap_grads(
            lambda k, a, b: frames[a, k, pl.ds(pitch * b, rows), cols],
            lambda k: grad_ref[k, :, cols].astype(f32),
            clips,
            rows,
        )
        zero = jnp.zeros((8, lanes), f32)
        totals = lax.fori_loop(0, steps, step, (zero,) * 27)
        rows_of_tap = [jnp.sum(total, axis=0, keepdims=True) for total in totals]
        out_ref[cols, :] = tap_table(rows_of_tap)


def third_taps_kernel(
    orders, parts, rz_ref, oz_ref, oc_ref, rc_ref, gz_ref, gc_ref, up_terms_ref, back_ref, third_ref, pooled_ref,
    taps_ref, *refs,
):
    outs, (frames, grads, total, full) = refs[:-4], refs[-4:]
    k = pl.program_id(0)
    rows, channels = oz_ref.shape[1], oz_ref.shape[2]
    pitch = 16
    chunk = 2 * pitch
    lanes = 128

    @pl.when(k == 0)
    def _():
        clear_edges(frames, pitch, rows)
        total[...] = jnp.zeros_like(total)

    fill_frames(frames, (rz_ref, oz_ref, oc_ref, rc_ref), pitch, rows)
    grads[0] = gz_ref[0].astype(f32)
    grads[1] = gc_ref[0].astype(f32)
    count = rows // chunk
    for l in range(channels // lanes):
        cols = pl.ds(l * lanes, lanes)
        totals = tuple(total[i, :, cols] for i in range(27))
        for slot in range(2):
            steps, step = tap_grads(
                lambda c, a, b: frames[
                    slot + a, pl.ds(pl.multiple_of(c * chunk + pitch * b, pitch), chunk), cols
                ],
                lambda c: grads[slot, pl.ds(pl.multiple_of(c * chunk, chunk), chunk), cols],
                count,
                chunk,
            )
            totals = lax.fori_loop(0, steps, step, totals)
        for i in range(27):
            total[i, :, cols] = totals[i]

    @pl.when(k == pl.num_programs(0) - 1)
    def _():
        wide = up_terms_ref.shape[1]
        late_wide = back_ref.shape[1]
        full[:, pl.ds(0, wide)] = up_terms_ref[...].astype(f32)
        full[:, pl.ds(wide, lanes)] = tap_table([jnp.sum(total[i], axis=0, keepdims=True) for i in range(27)])
        own, own_third, own_taps = late_wide // parts, wide // parts, taps_ref.shape[0] // parts
        deep = channels // parts
        clip, space = lax.axis_index("clip"), lax.axis_index("space")
        clips = pooled_ref.shape[0]
        pooled = pooled_ref[...].astype(f32)
        pooled = jnp.concatenate(
            [jnp.where((clip == g) & (space == 0), pooled, 0.0) for g in range(lax.axis_size("clip"))], axis=0
        )
        for d in range(parts):
            at, third_at = d * own // lanes * lanes, d * own_third // lanes * lanes
            block = jnp.concatenate(
                [
                    back_ref[0:2, pl.ds(at, lanes)],
                    third_ref[:, pl.ds(third_at, lanes)],
                    jnp.zeros((4, lanes), f32),
                    pooled[:, at : at + lanes],
                    taps_ref[pl.ds(d * own_taps, own_taps), :],
                ],
                axis=0,
            )
            for i in range(block.shape[0] // deep):
                full[pl.ds(d * deep, deep), pl.ds(wide + (1 + i) * lanes, lanes)] = block[i * deep : (i + 1) * deep]
        if orders is None:
            outs[0][...] = full[...].astype(bf16)
        else:
            clip_count, chips = orders
            keep_ref, send_ref = outs
            for b in range(clip_count):
                for z in range(chips):
                    at = ((clip ^ b) * chips + z) * 2
                    mine = pl.multiple_of((at + (space & 1)) * deep, deep)
                    other = pl.multiple_of((at + 1 - (space & 1)) * deep, deep)
                    keep_ref[b, z] = full[pl.ds(mine, deep), :]
                    send_ref[b, z] = full[pl.ds(other, deep), :].astype(bf16)


def third_grad_kernel(
    width, cells, count, counts_ref, *refs
):
    received, refs = refs[:count], refs[count:]
    (stats_ref, gain_ref, entry_grad_ref, up_ref, act_even_ref, act_sum_ref, gram_up_ref, act_ref, mid_ref,
     gz_ref, gc_ref, terms_ref, back_even, mix, shift, placed) = refs
    k = pl.program_id(0)
    rows = act_ref.shape[2]
    pitch = 16
    chunk = 2 * pitch
    half = pitch // 2

    @pl.when(k == 0)
    def _():
        placed[...] = jnp.zeros_like(placed)
        totals = received_sum(received) / cell_total(counts_ref, False, cells)
        center, scale = stats_ref[0:1], stats_ref[1:2]
        lead = gain_ref[...] * scale
        slope = -(lead * scale * totals[1:2])
        offset = -(lead * (totals[0:1] - center * scale * totals[1:2]))
        grad = (entry_grad_ref[...] * lead).astype(bf16)
        back_even[...] = dot_t(grad, up_ref[...])
        product = sum(dot_t(part, up_ref[...]) for part in split(up_ref[...].astype(f32) * slope, 2))
        mix[0], mix[1] = split(product, 2)
        offsets = [part.astype(f32) for part in split(offset, 2)]
        sums = [part.astype(f32) for part in split(act_sum_ref[...], 2)]
        none = jnp.zeros((4, offset.shape[1]), f32)
        offset_rows = jnp.concatenate(offsets + offsets + [none], axis=0).astype(bf16)
        none = jnp.zeros((4, act_sum_ref.shape[1]), f32)
        sum_rows = jnp.concatenate([sums[0], sums[0], sums[1], sums[1], none], axis=0).astype(bf16)
        shift[...] = jnp.sum(dot_t(offset_rows, up_ref[...])[0:2], axis=0, keepdims=True)
        terms = t_dot(act_even_ref[...], grad) + t_dot(sum_rows, offset_rows) + gram_up_ref[...] * slope
        terms_ref[...] = terms.astype(bf16)

    for j in range(rows // chunk):
        at = pl.multiple_of(k * (rows // 4) + half * j, half)
        put_even(placed, frame_of(0) * rows + chunk * j, back_even[pl.ds(at, half), :])
    for slot, out in ((0, gz_ref), (1, gc_ref)):
        mask = frame_mask(counts_ref, k, frame_of(slot))
        act = act_ref[0, slot]
        back = (dot(act, mix[0]) + dot(act, mix[1]) + shift[...]) * mask + get_lanes(placed, slot * rows, rows)
        back = back * gelu_slope(mid_ref[0, slot])
        out[0] = jnp.where(valid_rows(back.shape, pitch, width), back, 0.0).astype(bf16)


def first_grad_kernel(
    width, orders, counts_ref, rz_ref, gz_ref, gc_ref, rc_ref, taps_ref, first_ref, x_ref,
    grad_ref, *refs
):
    outs, (frames, xpad, product) = refs[:-3], refs[-3:]
    k = pl.program_id(0)
    rows = gz_ref.shape[1]
    height, width = x_ref.shape[2], x_ref.shape[3]
    pitch = 16
    chunk = 2 * pitch

    @pl.when(k == 0)
    def _():
        clear_edges(frames, pitch, rows)
        xpad[...] = jnp.zeros_like(xpad)
        product[...] = jnp.zeros_like(product)

    fill_frames(frames, (rz_ref, gz_ref, gc_ref, rc_ref), pitch, rows)
    for slot in range(2):
        frame = frame_of(slot)
        for h in range(height):
            xpad[pl.ds(slot * rows + h * pitch, width), :] = x_ref[0, frame, h]
        scale = frame_mask(counts_ref, k, frame)

        def step(c, _):
            start = pl.multiple_of(c * chunk, chunk)
            grad = conv_rows(
                lambda i: taps_ref[pl.ds(26 - i, 1), :],
                lambda a, b: frames[slot + a, pl.ds(pl.multiple_of(start + pitch * b, pitch), chunk), :],
                chunk,
            )
            grad = grad * scale * gelu_slope(first_ref[0, slot, pl.ds(start, chunk), :])
            grad = jnp.where(valid_rows(grad.shape, pitch, width), grad, 0.0)
            grad_ref[0, pl.ds(pl.multiple_of(slot * rows + start, chunk), chunk), :] = grad.astype(bf16)
            return 0

        lax.fori_loop(0, rows // chunk, step, 0)
    product[...] += t_dot(grad_ref[0], xpad[...])

    @pl.when(k == pl.num_programs(0) - 1)
    def _():
        terms = jnp.transpose(product[...])
        if orders is None:
            outs[0][...] = terms.astype(bf16)
        else:
            clips, chips, block = orders
            xpad_rows = terms.reshape(clips * chips * 2, block, terms.shape[1])
            space, clip = lax.axis_index("space"), lax.axis_index("clip")
            keep_ref, send_ref, full = outs[0], outs[1], outs[2]
            full[...] = xpad_rows
            for b in range(clips):
                for z in range(chips):
                    at = ((clip ^ b) * chips + z) * 2
                    keep_ref[b, z] = full[at + (space & 1)]
                    send_ref[b, z] = full[at + 1 - (space & 1)].astype(bf16)


def pair_sum_kernel(keep_ref, got_ref, keep_terms_ref, got_terms_ref, *out_refs):
    wide, inner = keep_terms_ref.shape[-1], keep_ref.shape[-1]
    deep = keep_terms_ref.shape[-2]
    for b, out_ref in enumerate(out_refs):
        out_ref[:, :, pl.ds(0, wide)] = (keep_terms_ref[b] + got_terms_ref[b].astype(f32)).astype(bf16)
        total = keep_ref[b] + got_ref[b].astype(f32)
        for i in range(keep_ref.shape[-2] // deep):
            out_ref[:, :, pl.ds(wide + i * inner, inner)] = total[:, i * deep : (i + 1) * deep].astype(bf16)


def chip_totals_kernel(count, *refs):
    terms, outs = refs[:count], refs[count:]
    for z, out_ref in enumerate(outs):
        at = (lax.axis_index("space") // 2) ^ z
        total = terms[0][at].astype(f32)
        for term in terms[1:]:
            total = total + term[at].astype(f32)
        out_ref[...] = total.astype(bf16)


def finish_kernel(count, *refs):
    skip, up = refs[:count], refs[count : 2 * count]
    skip_ref, up_ref, fourth_down_ref = refs[2 * count :]

    def total(terms):
        return sum(term[...].astype(f32) for term in terms)

    skip_ref[...] = total(skip)
    both = total(up)
    block, lanes = up_ref.shape[0], fourth_down_ref.shape[1]
    up_ref[...] = both[:block]
    part = both.shape[0] - block
    for i in range(both.shape[1] // lanes):
        fourth_down_ref[pl.ds(i * part, part), :] = both[block:, i * lanes : (i + 1) * lanes]


def terms_kernel(
    count, clips, wide, small_rows, *refs
):
    received, refs = refs[:count], refs[count:]
    (grad_ref, up_ref, depth_ref, gain_ref, shift_ref, late_gain_ref, late_shift_ref, late_depth_ref, head_ref,
     *down_refs) = refs
    lanes = 128
    total = None
    for ref in received:
        for i in range(ref.shape[0]):
            total = ref[i].astype(f32) if total is None else total + ref[i].astype(f32)
    deep = total.shape[0]
    up_ref[...] = total[:, :wide]
    depth_ref[...] = total[:, wide : wide + 27]
    device = lax.axis_index("clip") * lax.axis_size("space") + lax.axis_index("space")
    end = wide + lanes * (1 + small_rows // deep)
    small = jnp.concatenate([total[:, i : i + lanes] for i in range(wide + lanes, end, lanes)], axis=0)

    def own_lanes(values, width):
        moved = pltpu.roll(values, (lanes - device * width % lanes) % lanes, 1)
        return moved[:, :width]

    late = own_lanes(small, late_gain_ref.shape[1])
    third = own_lanes(small, gain_ref.shape[1])
    late_gain_ref[...] = late[1:2]
    late_shift_ref[...] = late[0:1]
    gain_ref[...] = third[3:4]
    shift_ref[...] = third[2:3]
    everyone = clips * lax.axis_size("clip")
    late_depth_ref[...] = small[8 + everyone :, :27]
    pooled = late[8 : 8 + everyone].astype(bf16)
    head_ref[...] = sum(t_dot(pooled, part) for part in split(grad_ref[...], 3))
    for down_ref in down_refs:
        inner = down_ref.shape[1]
        for i in range(down_ref.shape[0] // deep):
            down_ref[pl.ds(i * deep, deep), :] = total[:, end + i * inner : end + (i + 1) * inner]


def clip_grad_kernel(grad_ref, down_ref, entry_grad_ref, out_ref, wide):
    _, _, height, width, _ = out_ref.shape
    pitch = 16
    half = pitch // 2
    rows = height * pitch
    for slot in range(2):
        put_lanes(wide, slot * rows, dot_t(grad_ref[0, pl.ds(slot * rows, rows), :], down_ref[...]))
    for j in range(height // 2):
        at = frame_of(0) * rows + 2 * pitch * j
        put_even(wide, at, get_even(wide, at, half) + entry_grad_ref[0, pl.ds(half * j, half), :])
    for slot in range(2):
        frame = frame_of(slot)
        for h in range(height):
            out_ref[0, frame, h] = get_lanes(wide, slot * rows + h * pitch, width).astype(bf16)


kernel_micros = {
    "first": 5.3, "mid_own": 5.0, "mid": 8.6, "entry": 3.4, "late_mid": 4.7, "post": 6.0, "skip_sums": 7.0,
    "sum_grad": 4.6, "late_taps": 3.6, "late_back": 5.0, "up_down_sums": 5.5, "third_grad": 6.7, "third_taps": 7.7,
    "up_down_total": 2.3, "skip_total": 3.0, "finish": 2.0, "terms": 1.5, "taps": 0.6, "pooled_grad": 1.5, "head": 1.0, "add": 0.6, "skipped": 2.5, "first_grad": 10.7, "pair_sum": 1.9, "clip_sum": 1.6, "clip_grad": 5.5,
}
smem = pl.BlockSpec(memory_space=pltpu.SMEM)


def whole(shape):
    return pl.BlockSpec(shape, lambda k: (0,) * len(shape))


def by_clip(shape):
    return pl.BlockSpec((1,) + shape[1:], lambda k: (k,) + (0,) * (len(shape) - 1))


def cost(micros):
    return pl.CostEstimate(flops=0, bytes_accessed=int(micros * 3.4e6), transcendentals=0)


def call(kernel, name, inputs, outputs, scratch, clips=None, limit=LIMIT):
    if clips is None:
        def spec(kind, shape):
            return smem if kind == "s" else pl.BlockSpec(memory_space=pltpu.VMEM)
    else:
        def spec(kind, shape):
            return smem if kind == "s" else whole(shape) if kind == "w" else by_clip(shape)
    options = {} if clips is None else {"grid": (clips,)}
    return pl.pallas_call(
        kernel,
        name=name,
        out_shape=[jax.ShapeDtypeStruct(s, d) for s, d, _ in outputs],
        in_specs=[spec(kind, a.shape) for a, kind in inputs],
        out_specs=[spec(kind, s) for s, _, kind in outputs],
        scratch_shapes=scratch,
        compiler_params=pltpu.CompilerParams(vmem_limit_bytes=limit * mib),
        cost_estimate=cost(kernel_micros[name]),
        **options,
    )(*[a for a, _ in inputs])


def group_parts(values):
    size = lax.axis_size("space")
    if size != 8:
        copies = jnp.broadcast_to(values[None], (size,) + values.shape)
        return [lax.all_to_all(copies, "space", split_axis=0, concat_axis=0, tiled=True)]
    (pair,) = call(add_kernel, "add", [(values, "w"), (core_swap(values), "w")], [(values.shape, f32, "w")], [])
    return [part[None] for part in over_chips([pair] * 4)]


def w(arrays):
    return [(array, "w") for array in arrays]


def swap_neighbours(to_z, to_core):
    size = lax.axis_size("space")
    core = [(i, i ^ 1) for i in range(size)]
    z = [(i, j) for m in range(1, size - 1, 2) for i, j in ((m, m + 1), (m + 1, m))]
    return lax.ppermute(to_z, "space", z), lax.ppermute(to_core, "space", core)


def reduce_rows(term):
    return add_rows(send_rows(term))


def add_rows(received):
    return jnp.sum(received.astype(f32), axis=0)


def send_rows(term):
    parts = lax.axis_size("clip") * lax.axis_size("space")
    pieces = term.astype(bf16).reshape((parts, term.shape[0] // parts) + term.shape[1:])
    return lax.all_to_all(pieces, ("clip", "space"), split_axis=0, concat_axis=0, tiled=True)


def core_swap(values):
    return lax.ppermute(values, "space", [(i, i ^ 1) for i in range(lax.axis_size("space"))])


def own_rows(left_ref, out, starts):
    out[0] = jnp.transpose(left_ref[...])
    block = out.shape[1] // 2 // len(starts)
    for j, start in enumerate(starts):
        out[1, pl.ds(j * block, block), :] = out[0, pl.ds(pl.multiple_of(start * block, block), block), :]


def own_blocks(orders):
    space, clip = lax.axis_index("space"), lax.axis_index("clip")
    clips, chips = orders
    return [((clip ^ b) * chips + z) * 2 + (space & 1) for b in range(clips) for z in range(chips)]


def skip_kernel(
    orders, left_ref, left_other_ref, right_ref, right_other_ref, weight_ref, back_ref, *refs
):
    clips, chips = orders
    outs, (left, left_other) = refs[:clips], refs[clips:]

    @pl.when(pl.program_id(0) == 0)
    def _():
        own_rows(left_ref, left, own_blocks(orders))
        own_rows(left_other_ref, left_other, own_blocks(orders))
        back_ref[...] = jnp.zeros_like(back_ref)

    half = left.shape[1] // 2
    total = dot(left[1, pl.ds(0, half)], right_ref[...]) + dot(left_other[1, pl.ds(0, half)], right_other_ref[...])
    block = half // (clips * chips)
    for j in range(clips * chips):
        outs[j // chips][j % chips] = total[j * block : (j + 1) * block].astype(bf16)
    back_ref[...] += dot_t(right_ref[...], weight_ref[...])


def skip_sums(left, left_other, right, right_other, weight, parts, orders):
    block = left.shape[1] // parts
    wide = right.shape[1]
    lanes = 512
    rows, deep = left.shape
    return pl.pallas_call(
        functools.partial(skip_kernel, orders),
        name="skip_sums",
        grid=(wide // lanes,),
        out_shape=[
            jax.ShapeDtypeStruct((rows, deep), f32),
            *[jax.ShapeDtypeStruct((orders[1], block, wide), bf16)] * orders[0],
        ],
        in_specs=[pl.BlockSpec((rows, deep), lambda n: (0, 0))] * 2
        + [pl.BlockSpec((rows, lanes), lambda n: (0, n))] * 2
        + [pl.BlockSpec((deep, lanes), lambda n: (0, n))],
        out_specs=[
            pl.BlockSpec((rows, deep), lambda n: (0, 0)),
            *[pl.BlockSpec((orders[1], block, lanes), lambda n: (0, 0, n))] * orders[0],
        ],
        scratch_shapes=[pltpu.VMEM((2, deep, rows), bf16)] * 2,
        compiler_params=pltpu.CompilerParams(vmem_limit_bytes=LIMIT * mib),
        cost_estimate=cost(kernel_micros["skip_sums"]),
    )(left, left_other, right, right_other, weight)


def products_kernel(
    orders, act_ref, act_other_ref, entry_ref, entry_other_ref, first_ref, first_other_ref, sum_ref, sum_other_ref,
    *refs
):
    clips, chips = orders
    outs, (act, act_other, entry, entry_other, down) = refs[:clips], refs[clips:]
    n = pl.program_id(0)

    @pl.when(n == 0)
    def _():
        blocks = own_blocks(orders)
        own_rows(act_ref, act, blocks)
        own_rows(act_other_ref, act_other, blocks)
        own_rows(entry_ref, entry, blocks)
        own_rows(entry_other_ref, entry_other, blocks)
        half = entry.shape[1] // 2
        down[...] = (
            dot(entry[1, pl.ds(0, half)], first_ref[...]) + dot(entry_other[1, pl.ds(0, half)], first_other_ref[...])
        ).reshape(down.shape)

    half = act.shape[1] // 2
    up = dot(act[1, pl.ds(0, half)], sum_ref[...]) + dot(act_other[1, pl.ds(0, half)], sum_other_ref[...])
    block = half // (clips * chips)
    part = outs[0].shape[1] - block
    for b in range(clips):
        for z in range(chips):
            j = b * chips + z
            under = down[j, pl.ds(pl.multiple_of(n * part, part), part), :]
            outs[b][z] = jnp.concatenate([up[j * block : (j + 1) * block], under], axis=0).astype(bf16)


def up_down_sums(act, act_other, entry, entry_other, first, first_other, sums, sums_other, parts, orders):
    rows, deep = entry.shape
    inner, wide = act.shape[1], sums.shape[1]
    lanes = inner
    clips, chips = orders
    up_block, down_block = inner // parts, deep // parts
    block = up_block + down_block * inner // wide
    same = lambda n: (0, 0)
    return pl.pallas_call(
        functools.partial(products_kernel, orders),
        name="up_down_sums",
        grid=(wide // lanes,),
        out_shape=[jax.ShapeDtypeStruct((chips, block, wide), bf16)] * clips,
        in_specs=[pl.BlockSpec((rows, inner), same)] * 2
        + [pl.BlockSpec((rows, deep), same)] * 2
        + [pl.BlockSpec((rows, inner), same)] * 2
        + [pl.BlockSpec((rows, lanes), lambda n: (0, n))] * 2,
        out_specs=[pl.BlockSpec((chips, block, lanes), lambda n: (0, 0, n))] * clips,
        scratch_shapes=[pltpu.VMEM((2, inner, rows), bf16)] * 2
        + [pltpu.VMEM((2, deep, rows), bf16)] * 2
        + [pltpu.VMEM((clips * chips, down_block, inner), f32)],
        compiler_params=pltpu.CompilerParams(vmem_limit_bytes=LIMIT * mib),
        cost_estimate=cost(kernel_micros["up_down_sums"]),
    )(act, act_other, entry, entry_other, first, first_other, sums, sums_other)


def over_clip(pieces):
    size = len(pieces)
    return [pieces[0]] + [lax.ppermute(pieces[b], "clip", [(i, i ^ b) for i in range(size)]) for b in range(1, size)]


def over_chips(pieces):
    size = len(pieces)
    return [pieces[0]] + [
        lax.ppermute(pieces[z], "space", [(i, i ^ (2 * z)) for i in range(2 * size)]) for z in range(1, size)
    ]


def skipped_sums(entry, weight):
    rows, deep = entry.shape
    wide = weight.shape[1]
    lanes = 512
    return pl.pallas_call(
        skipped_kernel,
        name="skipped",
        grid=(wide // lanes,),
        out_shape=jax.ShapeDtypeStruct((rows, wide), bf16),
        in_specs=[pl.BlockSpec((rows, deep), lambda n: (0, 0)), pl.BlockSpec((deep, lanes), lambda n: (0, n))],
        out_specs=pl.BlockSpec((rows, lanes), lambda n: (0, n)),
        compiler_params=pltpu.CompilerParams(vmem_limit_bytes=LIMIT * mib),
        cost_estimate=cost(kernel_micros["skipped"]),
    )(entry, weight)


def after(values, token):
    return lax.optimization_barrier((values, token))[0]


def per_device(
    clip_input, frame_counts, third_down, third_depth, third_up, third_gain, third_shift,
    fourth_down, fourth_skip, fourth_depth, fourth_up, fourth_gain, fourth_shift,
    classifier, class_bias, logit_grad,
):
    clips, frames, height, width, channels = clip_input.shape
    inner = third_down.shape[1]
    late_inner = fourth_down.shape[1]
    late_wide = fourth_up.shape[1]
    half_width = width // 2
    rows = height * 16
    late_rows = height // 2 * 8
    late_all = clips * late_rows
    cells = height * width
    late_cells = (height // 2) * half_width
    parts = lax.axis_size("clip") * lax.axis_size("space")
    clip_axis, chips = lax.axis_size("clip"), lax.axis_size("space") // 2
    by_pairs = clip_axis == 4 and chips == 4 and channels // parts % 32 == 0 and late_inner // parts % 16 == 0
    orders = (clip_axis, chips) if by_pairs else None
    third_gain, third_shift = third_gain[None], third_shift[None]
    fourth_gain, fourth_shift = fourth_gain[None], fourth_shift[None]
    head = jnp.transpose(classifier)

    first, act_z, act_c, even_x = call(
        first_kernel, "first",
        [(frame_counts, "s"), (clip_input, "c"), (third_down, "w")],
        [
            ((clips, 2, rows, inner), f32, "c"),
            ((clips, rows, inner), bf16, "c"),
            ((clips, rows, inner), bf16, "c"),
            ((clips, late_rows, channels), f32, "c"),
        ],
        [pltpu.VMEM((rows, channels), bf16), pltpu.VMEM((channels // 128, 16, 128), f32)],
        clips=clips,
    )
    got_z, got_c = swap_neighbours(act_z, act_c)
    third_taps, late_taps = call(
        taps_kernel, "taps", w([jnp.transpose(third_depth), jnp.transpose(fourth_depth)]),
        [((27, inner), f32, "w"), ((27, late_inner), f32, "w")], [],
    )
    (mid_part,) = call(
        mid_own_kernel, "mid_own",
        [(act_z, "c"), (act_c, "c"), (third_taps, "w")],
        [((clips, 2, rows, inner), f32, "c")],
        [pltpu.VMEM((2, rows + 32, inner), f32)],
        clips=clips,
    )
    mid, mid_act, act_even, even_sum, moments, gram_up, act_sum = call(
        functools.partial(mid_kernel, width), "mid",
        [(frame_counts, "s"), (got_z, "c"), (got_c, "c"), (mid_part, "c"), (third_taps, "w"), (third_up, "w")],
        [
            ((clips, 2, rows, inner), f32, "c"),
            ((clips, 2, rows, inner), bf16, "c"),
            ((late_all, inner), bf16, "w"),
            ((late_all, channels), f32, "w"),
            ((2, channels), f32, "w"),
            ((inner, channels), f32, "w"),
            ((1, inner), f32, "w"),
        ],
        [
            pltpu.VMEM((2, rows + 32, inner), f32),
            pltpu.VMEM((inner // 128, 2 * rows, 128), f32),
            pltpu.VMEM((late_all, inner), f32),
            pltpu.VMEM((inner, inner), f32),
            pltpu.VMEM((8, inner), f32),
        ],
        clips=clips,
    )
    even_sum = even_sum.reshape(clips, late_rows, channels)
    moments = group_parts(moments)
    stats, even_hat, entry, late_first, late_act = call(
        functools.partial(entry_kernel, half_width, cells, len(moments)), "entry",
        [(frame_counts, "s"), *w(moments), (even_x, "w"), (even_sum, "w"),
         (third_gain, "w"), (third_shift, "w"), (fourth_down, "w")],
        [
            ((2, channels), f32, "w"),
            ((clips, late_rows, channels), f32, "w"),
            ((late_all, channels), bf16, "w"),
            ((late_all, late_inner), f32, "w"),
            ((clips, late_rows, late_inner), bf16, "w"),
        ],
        [],
    )
    late_first = late_first.reshape(clips, late_rows, late_inner)
    late_z, late_c = swap_neighbours(late_act, late_act)
    (pooled_grad,) = call(pooled_grad_kernel, "pooled_grad", w([logit_grad, head]), [((clips, late_wide), f32, "w")], [])
    skipped = skipped_sums(entry, fourth_skip).reshape(clips, late_rows, late_wide)
    late_mid, late_mid_act, late_sum, late_moments = call(
        functools.partial(late_kernel, half_width), "late_mid",
        [(frame_counts, "s"), (late_z, "w"), (late_act, "w"), (late_c, "w"), (late_taps, "w"), (fourth_up, "w")],
        [
            ((clips, late_rows, late_inner), f32, "w"),
            ((late_all, late_inner), bf16, "w"),
            ((late_all, late_wide), bf16, "w"),
            ((2, late_wide), f32, "w"),
        ],
        [
            pltpu.VMEM((3, late_rows + 16, late_inner), f32),
            pltpu.VMEM((clips, late_rows, late_inner), f32),
        ],
    )
    late_sum = late_sum.reshape(clips, late_rows, late_wide)
    late_moments = group_parts(late_moments)
    late_stats, late_back, pre_grad, skip_grad = call(
        functools.partial(post_kernel, half_width, late_cells, len(late_moments)), "post",
        [(frame_counts, "s"), *w(late_moments), (late_sum, "w"), (skipped, "w"),
         (fourth_gain, "w"), (fourth_shift, "w"), (pooled_grad, "w")],
        [
            ((2, late_wide), f32, "w"),
            ((2 + clips, late_wide), f32, "w"),
            ((clips, late_rows, late_wide), f32, "w"),
            ((clips, late_rows, late_wide), bf16, "w"),
        ],
        [],
    )
    received = group_parts(late_back)
    skip_rows = skip_grad.reshape(late_all, late_wide)
    if by_pairs:
        entry_other = core_swap(entry)
        skip_back, *skip_pieces = skip_sums(
            entry, entry_other, skip_rows, core_swap(skip_rows), fourth_skip, parts, (clip_axis, chips)
        )
    else:
        skip_back = dot_t(skip_rows, fourth_skip)
        fourth_skip_grad = reduce_rows(t_dot(entry, skip_rows))
    late_stats = after(late_stats, skip_back)
    late_sum_grad, late_mid_grad, pooled = call(
        functools.partial(sum_grad_kernel, half_width, late_cells, len(received)), "sum_grad",
        [(frame_counts, "s"), *w(received), (late_stats, "w"), (late_sum, "w"), (pre_grad, "w"),
         (fourth_gain, "w"), (fourth_up, "w"), (late_mid, "w")],
        [
            ((late_all, late_wide), bf16, "w"),
            ((clips, late_rows, late_inner), bf16, "w"),
            ((clips, late_wide), bf16, "w"),
        ],
        [],
    )
    late_gz, late_gc = swap_neighbours(late_mid_grad, late_mid_grad)
    if by_pairs:
        skip_pieces = over_clip(after(skip_pieces, late_mid_grad))
    (late_taps_table,) = call(
        late_taps_kernel, "late_taps",
        [(late_z, "w"), (late_act, "w"), (late_c, "w"), (late_mid_grad, "w")],
        [((late_inner, 128), f32, "w")],
        [pltpu.VMEM((3, clips, late_rows + 16, late_inner), f32)],
    )
    late_first = after(late_first, late_taps_table)
    late_first_grad, entry_grad, third_back = call(
        functools.partial(late_back_kernel, half_width), "late_back",
        [(frame_counts, "s"), (late_gz, "w"), (late_mid_grad, "w"), (late_gc, "w"), (late_taps, "w"),
         (late_first, "w"), (fourth_down, "w"), (skip_back, "w"), (even_hat, "w")],
        [
            ((late_all, late_inner), bf16, "w"),
            ((clips, late_rows, channels), f32, "w"),
            ((2, channels), f32, "w"),
        ],
        [
            pltpu.VMEM((3, late_rows + 16, late_inner), f32),
            pltpu.VMEM((clips, late_rows, late_inner), f32),
        ],
    )
    received = group_parts(third_back)
    if by_pairs:
        up_pieces = up_down_sums(
            late_mid_act, core_swap(late_mid_act), entry, entry_other, late_first_grad, core_swap(late_first_grad),
            late_sum_grad, core_swap(late_sum_grad), parts, (clip_axis, chips),
        )
        skip_pieces = call(
            functools.partial(chip_totals_kernel, clip_axis), "skip_total",
            [(part, "w") for part in after(skip_pieces, up_pieces[0])],
            [(skip_pieces[0].shape[1:], bf16, "w")] * chips, [],
        )
        stats = after(stats, skip_pieces[0])
    else:
        fourth_up_grad = reduce_rows(t_dot(late_mid_act, late_sum_grad))
        fourth_down_grad = reduce_rows(t_dot(entry, late_first_grad))
    grad_z, grad_c, up_terms = call(
        functools.partial(third_grad_kernel, width, cells, len(received)), "third_grad",
        [(frame_counts, "s"), *w(received), (stats, "w"), (third_gain, "w"),
         (entry_grad.reshape(late_all, channels), "w"), (third_up, "w"), (act_even, "w"), (act_sum, "w"),
         (gram_up, "w"), (mid_act, "c"), (mid, "c")],
        [
            ((clips, rows, inner), bf16, "c"),
            ((clips, rows, inner), bf16, "c"),
            ((inner, channels), bf16, "w"),
        ],
        [
            pltpu.VMEM((late_all, inner), f32),
            pltpu.VMEM((2, inner, inner), bf16),
            pltpu.VMEM((1, inner), f32),
            pltpu.VMEM((inner // 128, 2 * rows, 128), f32),
        ],
        clips=clips,
    )
    third_gz, third_gc = swap_neighbours(grad_z, grad_c)
    small_rows = 8 + clips * clip_axis + late_inner // parts
    deep = inner // parts
    extra = 128 * (1 + small_rows // deep)
    if by_pairs:
        term_outputs = [
            ((clip_axis, chips, deep, channels + extra), f32, "w"),
            ((clip_axis, chips, deep, channels + extra), bf16, "w"),
        ]
    else:
        term_outputs = [((inner, channels + extra), bf16, "w")]
    third_terms = call(
        functools.partial(third_taps_kernel, orders, parts), "third_taps",
        [(got_z, "c"), (act_z, "c"), (act_c, "c"), (got_c, "c"), (grad_z, "c"), (grad_c, "c"),
         (up_terms, "w"), (late_back, "w"), (third_back, "w"), (pooled, "w"), (late_taps_table, "w")],
        term_outputs,
        [
            pltpu.VMEM((4, rows + 32, inner), f32),
            pltpu.VMEM((2, rows, inner), f32),
            pltpu.VMEM((27, 8, inner), f32),
            pltpu.VMEM((inner, channels + extra), f32),
        ],
        clips=clips,
    )
    first = after(first, third_terms[0])
    if by_pairs:
        up_pieces = over_clip(after(up_pieces, skip_pieces[0]))
        skip_pieces = over_chips(after(skip_pieces, third_terms[0]))
    block = channels // parts
    if by_pairs:
        down_outputs = [
            ((clip_axis, chips, block, inner), f32, "w"),
            ((clip_axis, chips, block, inner), bf16, "w"),
        ]
        down_scratch = [pltpu.VMEM((parts, block, inner), f32)]
    else:
        down_outputs, down_scratch = [((channels, inner), bf16, "w")], []
    first_grad, *down_terms = call(
        functools.partial(first_grad_kernel, width, (clip_axis, chips, block) if by_pairs else None), "first_grad",
        [(frame_counts, "s"), (third_gz, "c"), (grad_z, "c"), (grad_c, "c"), (third_gc, "c"),
         (third_taps, "w"), (first, "c"), (clip_input, "c")],
        [((clips, 2 * rows, inner), bf16, "c"), *down_outputs],
        [
            *down_scratch,
            pltpu.VMEM((4, rows + 32, inner), f32),
            pltpu.VMEM((2 * rows, channels), bf16),
            pltpu.VMEM((inner, channels), f32),
        ],
        clips=clips,
    )
    if by_pairs:
        keep, send = down_terms
        keep_terms, send_terms = third_terms
        clip_parts = call(
            pair_sum_kernel, "pair_sum",
            w([keep, core_swap(send), keep_terms, core_swap(after(send_terms, third_gz))]),
            [((chips, deep, channels + extra + block // deep * inner), bf16, "w")] * clip_axis,
            [],
        )
        up_pieces = call(
            functools.partial(chip_totals_kernel, clip_axis), "up_down_total", w(after(up_pieces, clip_parts[0])),
            [(up_pieces[0].shape[1:], bf16, "w")] * chips, [],
        )
        clip_parts = over_clip(clip_parts)
        up_pieces = over_chips(up_pieces)
        chip_parts = call(
            functools.partial(chip_totals_kernel, clip_axis), "clip_sum", w(after(clip_parts, up_pieces[0])),
            [(clip_parts[0].shape[1:], bf16, "w")] * chips, [],
        )
        third_terms = [part[None] for part in over_chips(chip_parts)]
        up_block = late_inner // parts
        fourth_skip_grad, fourth_up_grad, fourth_down_grad = call(
            functools.partial(finish_kernel, chips), "finish", w(skip_pieces + up_pieces),
            [
                ((block, late_wide), f32, "w"),
                ((up_block, late_wide), f32, "w"),
                ((block, late_inner), f32, "w"),
            ],
            [],
        )
    else:
        third_down_grad = add_rows(send_rows(down_terms[0]))
        third_terms = [send_rows(third_terms[0])]
    (clip_grad,) = call(
        clip_grad_kernel, "clip_grad",
        [(first_grad, "c"), (third_down, "w"), (entry_grad, "c")],
        [(clip_input.shape, bf16, "c")],
        [pltpu.VMEM((channels // 128, 2 * rows, 128), f32)],
        clips=clips,
    )

    logits, bias_grad = call(
        head_kernel, "head", w([after(pooled, first_grad), head, class_bias[None], logit_grad]),
        [((clips, logit_grad.shape[1]), f32, "w"), ((1, logit_grad.shape[1]), f32, "w")], [],
    )
    own, own_third, own_taps = late_wide // parts, channels // parts, late_inner // parts
    third_up_grad, third_depth_grad, gain, shift, late_gain, late_shift, fourth_depth_grad, classifier_grad, *down = call(
        functools.partial(terms_kernel, len(third_terms), clips, channels, small_rows), "terms",
        w(third_terms + [logit_grad]),
        [
            ((deep, channels), f32, "w"),
            ((deep, 27), f32, "w"),
            ((1, own_third), f32, "w"),
            ((1, own_third), f32, "w"),
            ((1, own), f32, "w"),
            ((1, own), f32, "w"),
            ((own_taps, 27), f32, "w"),
            ((own, logit_grad.shape[1]), f32, "w"),
            *([((block, inner), f32, "w")] if by_pairs else []),
        ],
        [],
    )
    if by_pairs:
        (third_down_grad,) = down
    return (
        logits,
        clip_grad,
        third_down_grad,
        third_depth_grad,
        third_up_grad,
        gain.reshape(-1),
        shift.reshape(-1),
        fourth_down_grad,
        fourth_skip_grad,
        fourth_depth_grad,
        fourth_up_grad,
        late_gain.reshape(-1),
        late_shift.reshape(-1),
        classifier_grad,
        bias_grad.reshape(-1),
    )


def solution(mesh):
    both = ("clip", "space")
    return jax.shard_map(
        per_device,
        mesh=mesh,
        in_specs=(P("clip", "space", None, None, None), P("clip")) + (P(),) * 14,
        out_specs=(
            P("clip", None),
            P("clip", "space", None, None, None),
            P(both, None),
            P(both, None),
            P(both, None),
            P(both),
            P(both),
            P(both, None),
            P(both, None),
            P(both, None),
            P(both, None),
            P(both),
            P(both),
            P(both, None),
            P(),
        ),
        check_vma=False,
    )
```

```python
import functools
import math

import jax
import jax.numpy as jnp
from jax import lax
from jax.experimental import pallas as pl
from jax.experimental.pallas import tpu as pltpu
from jax.sharding import PartitionSpec as P

eps = 1e-05
f32 = jnp.float32
bf16 = jnp.bfloat16
mib = 1 << 20
LIMIT = 16


def gelu_terms(x):
    c = math.sqrt(2.0 / math.pi)
    x2 = x * x
    t = jnp.tanh(x * (c + (c * 0.044715) * x2))
    return x2, t


def gelu(x):
    _, t = gelu_terms(x)
    return x * (0.5 + 0.5 * t)


def gelu_slope(x):
    c = math.sqrt(2.0 / math.pi)
    x2, t = gelu_terms(x)
    return 0.5 + 0.5 * t + (0.5 * x) * ((1.0 - t * t) * (c + (3.0 * c * 0.044715) * x2))


def gelu_both(x):
    c = math.sqrt(2.0 / math.pi)
    x2, t = gelu_terms(x)
    cdf = 0.5 + 0.5 * t
    return x * cdf, cdf + (0.5 * x) * ((1.0 - t * t) * (c + (3.0 * c * 0.044715) * x2))


def valid_rows(shape, group, used):
    return lax.broadcasted_iota(jnp.int32, shape, 0) % group < used


def row_sums(values):
    rows, width = values.shape
    return jnp.sum(values.reshape(rows // 8, 8, width), axis=0)


def dot(left, right):
    return jnp.dot(left, right, preferred_element_type=f32)


def dot_t(left, right):
    return lax.dot_general(left, right, (((1,), (1,)), ((), ())), preferred_element_type=f32)


def t_dot(left, right):
    return lax.dot_general(left, right, (((0,), (0,)), ((), ())), preferred_element_type=f32)


def put_lanes(ref, start, values):
    rows, channels = values.shape
    for j in range(channels // 128):
        ref[j, pl.ds(start, rows), :] = values[:, 128 * j : 128 * (j + 1)]


def get_lanes(ref, start, rows):
    return jnp.concatenate([ref[j, pl.ds(start, rows), :] for j in range(ref.shape[0])], axis=1)


def get_even(ref, start, count):
    return jnp.concatenate(
        [ref[j, pl.ds(start, count, stride=2), :] for j in range(ref.shape[0])], axis=1
    )


def put_even(ref, start, values):
    rows, channels = values.shape
    for j in range(channels // 128):
        ref[j, pl.ds(start, rows, stride=2), :] = values[:, 128 * j : 128 * (j + 1)]


def conv_rows(taps, load, rows, times=(0, 1, 2)):
    sums = [None, None, None]
    for a in times:
        for b in range(3):
            block = load(a, b)
            for e in range(3):
                term = block * taps(9 * a + 3 * b + e)
                sums[e] = term if sums[e] is None else sums[e] + term
    return pltpu.roll(sums[0], 1, 0) + sums[1] + pltpu.roll(sums[2], rows - 1, 0)


def split(values, count):
    parts = []
    for _ in range(count):
        parts.append(values.astype(bf16))
        values = values - parts[-1].astype(f32)
    return parts


def frame_of(slot):
    parity = lax.axis_index("space") & 1
    return parity if slot == 0 else 1 - parity


def frame_mask(counts_ref, k, frame):
    return jnp.where(2 * lax.axis_index("space") + frame < counts_ref[k], 1.0, 0.0).astype(f32)


def cell_total(counts_ref, late, cells):
    total = 0
    for k in range(counts_ref.shape[0]):
        total += (counts_ref[k] + 1) // 2 if late else counts_ref[k]
    return (total * cells).astype(f32)


def received_sum(refs):
    total = None
    for ref in refs:
        for i in range(ref.shape[0]):
            total = ref[i] if total is None else total + ref[i]
    return total


def taps_kernel(third_ref, fourth_ref, third_out, fourth_out):
    swapped = (lax.axis_index("space") & 1) == 1
    for source, out in ((third_ref, third_out), (fourth_ref, fourth_out)):
        for a in range(3):
            here, there = source[pl.ds(9 * a, 9), :], source[pl.ds(9 * (2 - a), 9), :]
            out[pl.ds(9 * a, 9), :] = jnp.where(swapped, there, here)


def pooled_grad_kernel(grad_ref, head_ref, out_ref):
    full = sum(dot(part, head_ref[...]) for part in split(grad_ref[...], 3))
    clips = out_ref.shape[0]
    clip = lax.axis_index("clip")
    own = full[:clips]
    for g in range(1, full.shape[0] // clips):
        own = jnp.where(clip == g, full[g * clips : (g + 1) * clips], own)
    out_ref[...] = own.astype(bf16).astype(f32)


def head_kernel(pooled_ref, head_ref, grad_ref, logits_ref, bias_grad_ref):
    terms = sum(dot_t(part, head_ref[...]) for part in split(pooled_ref[...], 3))
    clips, classes = terms.shape
    wide = logits_ref.shape[1] // 2
    logits_ref[...] = jnp.zeros_like(logits_ref)
    for k in range(clips):
        logits_ref[pl.ds(k // 2, 1), pl.ds(k % 2 * wide, classes)] = terms[k : k + 1]
    bias_grad_ref[...] = jnp.sum(grad_ref[...], axis=0, keepdims=True)


def add_kernel(one_ref, two_ref, out_ref):
    out_ref[...] = one_ref[...] + two_ref[...]


def skipped_kernel(entry_ref, weight_ref, out_ref):
    out_ref[...] = dot(entry_ref[...], weight_ref[...]).astype(bf16)


def first_kernel(counts_ref, x_ref, w_ref, first_ref, actz_ref, actc_ref, even_ref, xpad, xe):
    k = pl.program_id(0)
    _, _, height, width, _ = x_ref.shape
    pitch = xe.shape[1]

    @pl.when(k == 0)
    def _():
        xpad[...] = jnp.zeros_like(xpad)
        xe[...] = jnp.zeros_like(xe)

    for slot, act_ref in ((0, actz_ref), (1, actc_ref)):
        frame = frame_of(slot)
        for h in range(height):
            xpad[pl.ds(h * pitch, width), :] = x_ref[0, frame, h]
        first = dot(xpad[...], w_ref[...])
        first_ref[0, slot] = first
        act_ref[0] = (gelu(first) * frame_mask(counts_ref, k, frame)).astype(bf16)
    for h in range(0, height, 2):
        put_lanes(xe, 0, x_ref[0, 0, h].astype(f32))
        even_ref[0, pl.ds(h // 2 * (pitch // 2), pitch // 2), :] = get_even(xe, 0, pitch // 2)


def fill_frames(frames, sources, pad, rows):
    for s, source in enumerate(sources):
        frames[s, pl.ds(pad, rows), :] = source[0].astype(f32)


def clear_edges(frames, pad, rows):
    edge = jnp.zeros((pad, frames.shape[-1]), f32)
    for s in range(frames.shape[0]):
        frames[s, pl.ds(0, pad), :] = edge
        frames[s, pl.ds(pad + rows, pad), :] = edge


def mid_own_kernel(oz_ref, oc_ref, taps_ref, part_ref, frames):
    rows = oz_ref.shape[1]
    pitch = 16
    chunk = 2 * pitch

    @pl.when(pl.program_id(0) == 0)
    def _():
        clear_edges(frames, pitch, rows)

    fill_frames(frames, (oz_ref, oc_ref), pitch, rows)
    for slot in range(2):
        def step(c, _):
            start = pl.multiple_of(c * chunk, chunk)
            part_ref[0, slot, pl.ds(start, chunk), :] = conv_rows(
                lambda i: taps_ref[pl.ds(i, 1), :],
                lambda a, b: frames[slot + a - 1, pl.ds(pl.multiple_of(start + pitch * b, pitch), chunk), :],
                chunk,
                (1, 2) if slot == 0 else (0, 1),
            )
            return 0

        lax.fori_loop(0, rows // chunk, step, 0)


def mid_kernel(
    width, counts_ref, rz_ref, rc_ref, part_ref, taps_ref, up_ref,
    mid_ref, act_ref, act_even_ref, even_ref, moment_ref, gram_up_ref, act_sum_ref,
    frames, acts, evens, gram, total,
):
    k = pl.program_id(0)
    rows = rz_ref.shape[1]
    pitch = 16
    chunk = 2 * pitch
    half = pitch // 2

    @pl.when(k == 0)
    def _():
        clear_edges(frames, pitch, rows)
        gram[...] = jnp.zeros_like(gram)
        total[...] = jnp.zeros_like(total)

    fill_frames(frames, (rz_ref, rc_ref), pitch, rows)
    for slot in range(2):
        def step(c, _):
            start = pl.multiple_of(c * chunk, chunk)
            mid = part_ref[0, slot, pl.ds(start, chunk), :] + conv_rows(
                lambda i: taps_ref[pl.ds(i, 1), :],
                lambda a, b: frames[slot, pl.ds(pl.multiple_of(start + pitch * b, pitch), chunk), :],
                chunk,
                (0,) if slot == 0 else (2,),
            )
            mid_ref[0, slot, pl.ds(start, chunk), :] = mid
            act = jnp.where(valid_rows(mid.shape, pitch, width), gelu(mid), 0.0)
            act_ref[0, slot, pl.ds(start, chunk), :] = act.astype(bf16)
            put_lanes(acts, slot * rows + start, act)
            return 0

        lax.fori_loop(0, rows // chunk, step, 0)
        act = act_ref[0, slot]
        mask = frame_mask(counts_ref, k, frame_of(slot))
        gram[...] += t_dot(act, act) * mask
        total[...] += row_sums(act.astype(f32)) * mask
    for j in range(rows // chunk):
        at = pl.multiple_of(k * (rows // 4) + half * j, half)
        evens[pl.ds(at, half), :] = get_even(acts, frame_of(0) * rows + chunk * j, half)

    @pl.when(k == pl.num_programs(0) - 1)
    def _():
        act_even_ref[...] = evens[...].astype(bf16)
        even_ref[...] = dot(act_even_ref[...], up_ref[...])
        gram_up = sum(dot(part, up_ref[...]) for part in split(gram[...], 3))
        gram_up_ref[...] = gram_up
        act_sum = jnp.sum(total[...], axis=0, keepdims=True)
        act_sum_ref[...] = act_sum
        rows_of_sum = jnp.concatenate(
            [part.astype(f32) for part in split(act_sum, 3)] + [jnp.zeros((5,) + act_sum.shape[1:], f32)], axis=0
        ).astype(bf16)
        moment_ref[0:1] = jnp.sum(dot(rows_of_sum, up_ref[...]), axis=0, keepdims=True)
        moment_ref[1:2] = jnp.sum(gram_up * up_ref[...].astype(f32), axis=0, keepdims=True)


def norm_stats(refs, cells):
    totals = received_sum(refs)
    center = totals[0:1] / cells
    return center, lax.rsqrt(totals[1:2] / cells - center * center + eps)


def entry_kernel(
    width, cells, count, counts_ref, *refs
):
    moments, refs = refs[:count], refs[count:]
    (even_x_ref, even_ref, gain_ref, shift_ref, down_ref, stats_ref, hat_ref, entry_ref, first_ref, act_ref) = refs
    center, scale = norm_stats(moments, cell_total(counts_ref, False, cells))
    stats_ref[0:1] = center
    stats_ref[1:2] = scale
    clips, rows, channels = even_ref.shape
    for k in range(clips):
        hat = (even_ref[k] - center) * scale
        hat_ref[k] = hat
        entry = even_x_ref[k] + hat * gain_ref[...] + shift_ref[...]
        entry = jnp.where(valid_rows(entry.shape, 8, width), entry, 0.0)
        entry_ref[pl.ds(k * rows, rows), :] = entry.astype(bf16)
    late = dot(entry_ref[...], down_ref[...])
    first_ref[...] = late
    for k in range(clips):
        act_ref[k] = (gelu(late[k * rows : (k + 1) * rows]) * frame_mask(counts_ref, k, 0)).astype(bf16)


def late_kernel(
    width, counts_ref, rz_ref, own_ref, rc_ref, taps_ref, up_ref,
    mid_ref, act_ref, sum_ref, moment_ref, frames, wide,
):
    clips, rows, channels = own_ref.shape
    pitch = 8
    edge = jnp.zeros((pitch, channels), f32)
    lanes = 128

    def clip_step(k, _):
        for s, source in enumerate((rz_ref, own_ref, rc_ref)):
            frames[s, pl.ds(0, pitch), :] = edge
            frames[s, pl.ds(pitch + rows, pitch), :] = edge
            frames[s, pl.ds(pitch, rows), :] = source[k].astype(f32)
        for l in range(channels // lanes):
            cols = pl.ds(l * lanes, lanes)
            mid = conv_rows(
                lambda i: taps_ref[pl.ds(i, 1), cols],
                lambda a, b: frames[a, pl.ds(pitch * b, rows), cols],
                rows,
            )
            mid_ref[k, :, cols] = mid
            wide[k, :, cols] = jnp.where(valid_rows(mid.shape, pitch, width), gelu(mid), 0.0)
        return 0

    lax.fori_loop(0, clips, clip_step, 0)
    for k in range(clips):
        act_ref[pl.ds(k * rows, rows), :] = wide[k].astype(bf16)
    late = dot(act_ref[...], up_ref[...]).astype(bf16)
    sum_ref[...] = late
    late = late.astype(f32)
    one = two = None
    for k in range(clips):
        block = late[k * rows : (k + 1) * rows]
        mask = frame_mask(counts_ref, k, 0)
        a, b = row_sums(block) * mask, row_sums(block * block) * mask
        one, two = (a, b) if one is None else (one + a, two + b)
    moment_ref[0:1] = jnp.sum(one, axis=0, keepdims=True)
    moment_ref[1:2] = jnp.sum(two, axis=0, keepdims=True)


def post_kernel(
    width, cells, count, counts_ref, *refs
):
    moments, refs = refs[:count], refs[count:]
    (sum_ref, skip_ref, gain_ref, shift_ref, pooled_grad_ref, stats_ref, back_ref, pooled_ref, pre_ref,
     skip_grad_ref) = refs
    center, scale = norm_stats(moments, cell_total(counts_ref, True, cells))
    stats_ref[0:1] = center
    stats_ref[1:2] = scale
    clips, rows, channels = sum_ref.shape
    one = two = None
    for k in range(clips):
        hat = (sum_ref[k].astype(f32) - center) * scale
        post, slope = gelu_both(hat * gain_ref[...] + shift_ref[...] + skip_ref[k].astype(f32))
        keep = valid_rows(post.shape, 8, width)
        mask = frame_mask(counts_ref, k, 0)
        pool = ((counts_ref[k] + 1) // 2 * cells).astype(f32)
        pooled = jnp.sum(jnp.where(keep, post, 0.0), axis=0, keepdims=True) * mask / pool
        pooled_ref[pl.ds(k, 1)] = pooled
        pre = jnp.where(keep, pooled_grad_ref[pl.ds(k, 1)] * mask / pool * slope, 0.0)
        pre_ref[k] = pre
        skip_grad_ref[k] = pre.astype(bf16)
        a, b = row_sums(pre), row_sums(pre * hat)
        one, two = (a, b) if one is None else (one + a, two + b)
    back_ref[0:1] = jnp.sum(one, axis=0, keepdims=True)
    back_ref[1:2] = jnp.sum(two, axis=0, keepdims=True)


def sum_grad_kernel(
    width, cells, count, counts_ref, *refs
):
    received, refs = refs[:count], refs[count:]
    (stats_ref, sum_ref, pre_ref, gain_ref, up_ref, mid_ref, sum_grad_ref, mid_grad_ref) = refs
    totals = received_sum(received) / cell_total(counts_ref, True, cells)
    center, scale = stats_ref[0:1], stats_ref[1:2]
    lead = gain_ref[...] * scale
    clips, rows, channels = sum_ref.shape
    for k in range(clips):
        hat = (sum_ref[k].astype(f32) - center) * scale
        weight = frame_mask(counts_ref, k, 0)
        grad = lead * (pre_ref[k] - weight * (totals[0:1] + hat * totals[1:2]))
        grad = jnp.where(valid_rows(grad.shape, 8, width), grad, 0.0)
        sum_grad_ref[pl.ds(k * rows, rows), :] = grad.astype(bf16)
    back = dot_t(sum_grad_ref[...], up_ref[...])
    for k in range(clips):
        mid_grad_ref[k] = (back[k * rows : (k + 1) * rows] * gelu_slope(mid_ref[k])).astype(bf16)


def late_back_kernel(
    width, counts_ref, rz_ref, own_ref, rc_ref, taps_ref, first_ref, down_ref, skip_back_ref, hat_ref, logits_ref,
    first_grad_ref, entry_grad_ref, back_ref, frames, grads,
):
    clips, rows, channels = own_ref.shape
    pitch = 8
    edge = jnp.zeros((pitch, channels), f32)
    lanes = 128

    def clip_step(k, _):
        for s, source in enumerate((rz_ref, own_ref, rc_ref)):
            frames[s, pl.ds(0, pitch), :] = edge
            frames[s, pl.ds(pitch + rows, pitch), :] = edge
            frames[s, pl.ds(pitch, rows), :] = source[k].astype(f32)
        for l in range(channels // lanes):
            cols = pl.ds(l * lanes, lanes)
            grad = conv_rows(
                lambda i: taps_ref[pl.ds(26 - i, 1), cols],
                lambda a, b: frames[a, pl.ds(pitch * b, rows), cols],
                rows,
            )
            grad = grad * frame_mask(counts_ref, k, 0) * gelu_slope(first_ref[k, :, cols])
            grads[k, :, cols] = jnp.where(valid_rows(grad.shape, pitch, width), grad, 0.0)
        return 0

    lax.fori_loop(0, clips, clip_step, 0)
    for k in range(clips):
        first_grad_ref[pl.ds(k * rows, rows), :] = grads[k].astype(bf16)
    entry = dot_t(first_grad_ref[...], down_ref[...]) + skip_back_ref[...]
    one = two = None
    for k in range(clips):
        block = entry[k * rows : (k + 1) * rows]
        entry_grad_ref[k] = block
        masked = block * frame_mask(counts_ref, k, 0)
        a, b = row_sums(masked), row_sums(masked * hat_ref[k])
        one, two = (a, b) if one is None else (one + a, two + b)
    back_ref[0:1] = jnp.sum(one, axis=0, keepdims=True)
    back_ref[1:2] = jnp.sum(two, axis=0, keepdims=True)
    back_ref[2:] = logits_ref[...]


def tap_grads(load, grad_of, steps, rows):
    def step(c, totals):
        grad = grad_of(c)
        sides = (pltpu.roll(grad, rows - 1, 0), grad, pltpu.roll(grad, 1, 0))
        new = []
        for a in range(3):
            for b in range(3):
                block = load(c, a, b)
                for e in range(3):
                    new.append(totals[9 * a + 3 * b + e] + row_sums(block * sides[e]))
        return tuple(new)

    return steps, step


def tap_table(rows_of_tap):
    swapped = (lax.axis_index("space") & 1) == 1
    rows = [jnp.where(swapped, rows_of_tap[(2 - i // 9) * 9 + i % 9], rows_of_tap[i]) for i in range(27)]
    table = jnp.concatenate(rows + [jnp.zeros_like(rows[0])] * 5, axis=0)
    table = jnp.transpose(table)
    return jnp.concatenate([table, jnp.zeros((table.shape[0], 96), f32)], axis=1)


def late_taps_kernel(rz_ref, own_ref, rc_ref, grad_ref, out_ref, frames):
    clips, rows, channels = own_ref.shape
    pitch = 8
    edge = jnp.zeros((pitch, channels), f32)
    lanes = 128
    for s, source in enumerate((rz_ref, own_ref, rc_ref)):
        for k in range(clips):
            frames[s, k, pl.ds(0, pitch), :] = edge
            frames[s, k, pl.ds(pitch + rows, pitch), :] = edge
            frames[s, k, pl.ds(pitch, rows), :] = source[k].astype(f32)
    for l in range(channels // lanes):
        cols = pl.ds(l * lanes, lanes)
        steps, step = tap_grads(
            lambda k, a, b: frames[a, k, pl.ds(pitch * b, rows), cols],
            lambda k: grad_ref[k, :, cols].astype(f32),
            clips,
            rows,
        )
        zero = jnp.zeros((8, lanes), f32)
        totals = lax.fori_loop(0, steps, step, (zero,) * 27)
        rows_of_tap = [jnp.sum(total, axis=0, keepdims=True) for total in totals]
        out_ref[cols, :] = tap_table(rows_of_tap)


def third_taps_kernel(
    orders, parts, rz_ref, oz_ref, oc_ref, rc_ref, gz_ref, gc_ref, up_terms_ref, back_ref, third_ref, pooled_ref,
    taps_ref, *refs,
):
    outs, (frames, grads, total, full) = refs[:-4], refs[-4:]
    k = pl.program_id(0)
    rows, channels = oz_ref.shape[1], oz_ref.shape[2]
    pitch = 16
    chunk = 2 * pitch
    lanes = 128

    @pl.when(k == 0)
    def _():
        clear_edges(frames, pitch, rows)
        total[...] = jnp.zeros_like(total)

    fill_frames(frames, (rz_ref, oz_ref, oc_ref, rc_ref), pitch, rows)
    grads[0] = gz_ref[0].astype(f32)
    grads[1] = gc_ref[0].astype(f32)
    count = rows // chunk
    for l in range(channels // lanes):
        cols = pl.ds(l * lanes, lanes)
        totals = tuple(total[i, :, cols] for i in range(27))
        for slot in range(2):
            steps, step = tap_grads(
                lambda c, a, b: frames[
                    slot + a, pl.ds(pl.multiple_of(c * chunk + pitch * b, pitch), chunk), cols
                ],
                lambda c: grads[slot, pl.ds(pl.multiple_of(c * chunk, chunk), chunk), cols],
                count,
                chunk,
            )
            totals = lax.fori_loop(0, steps, step, totals)
        for i in range(27):
            total[i, :, cols] = totals[i]

    @pl.when(k == pl.num_programs(0) - 1)
    def _():
        wide = up_terms_ref.shape[1]
        late_wide = back_ref.shape[1]
        full[:, pl.ds(0, wide)] = up_terms_ref[...].astype(f32)
        full[:, pl.ds(wide, lanes)] = tap_table([jnp.sum(total[i], axis=0, keepdims=True) for i in range(27)])
        own, own_third, own_taps = late_wide // parts, wide // parts, taps_ref.shape[0] // parts
        deep = channels // parts
        clip, space = lax.axis_index("clip"), lax.axis_index("space")
        pooled = pooled_ref[...]
        pooled = jnp.concatenate(
            [jnp.where(clip == g, pooled, 0.0) for g in range(lax.axis_size("clip"))], axis=0
        )
        for d in range(parts):
            at, third_at = d * own // lanes * lanes, d * own_third // lanes * lanes
            block = jnp.concatenate(
                [
                    back_ref[0:2, pl.ds(at, lanes)],
                    third_ref[0:2, pl.ds(third_at, lanes)],
                    jnp.zeros((4, lanes), f32),
                    pooled[:, at : at + lanes],
                    taps_ref[pl.ds(d * own_taps, own_taps), :],
                ],
                axis=0,
            )
            for i in range(block.shape[0] // deep):
                full[pl.ds(d * deep, deep), pl.ds(wide + (1 + i) * lanes, lanes)] = block[i * deep : (i + 1) * deep]
        if orders is None:
            outs[0][...] = full[...].astype(bf16)
        else:
            clip_count, chips = orders
            keep_ref, send_ref = outs
            for b in range(clip_count):
                for z in range(chips):
                    at = ((clip ^ b) * chips + z) * 2
                    mine = pl.multiple_of((at + (space & 1)) * deep, deep)
                    other = pl.multiple_of((at + 1 - (space & 1)) * deep, deep)
                    keep_ref[b, z] = full[pl.ds(mine, deep), :]
                    send_ref[b, z] = full[pl.ds(other, deep), :].astype(bf16)


def third_grad_kernel(
    width, cells, count, counts_ref, *refs
):
    received, refs = refs[:count], refs[count:]
    (stats_ref, gain_ref, entry_grad_ref, up_ref, act_even_ref, act_sum_ref, gram_up_ref, bias_ref, act_ref, mid_ref,
     gz_ref, gc_ref, terms_ref, logits_ref, back_even, mix, shift, placed) = refs
    k = pl.program_id(0)
    rows = act_ref.shape[2]
    pitch = 16
    chunk = 2 * pitch
    half = pitch // 2

    @pl.when(k == 0)
    def _():
        placed[...] = jnp.zeros_like(placed)
        totals = received_sum(received)
        clips, classes = logits_ref.shape
        wide = totals.shape[1] // 2
        for i in range(clips):
            row = totals[2 + i // 2 : 3 + i // 2, i % 2 * wide : i % 2 * wide + classes]
            logits_ref[pl.ds(i, 1)] = row + bias_ref[...]
        totals = totals[0:2] / cell_total(counts_ref, False, cells)
        center, scale = stats_ref[0:1], stats_ref[1:2]
        lead = gain_ref[...] * scale
        slope = -(lead * scale * totals[1:2])
        offset = -(lead * (totals[0:1] - center * scale * totals[1:2]))
        grad = (entry_grad_ref[...] * lead).astype(bf16)
        back_even[...] = dot_t(grad, up_ref[...])
        product = sum(dot_t(part, up_ref[...]) for part in split(up_ref[...].astype(f32) * slope, 2))
        mix[0], mix[1] = split(product, 2)
        offsets = [part.astype(f32) for part in split(offset, 2)]
        sums = [part.astype(f32) for part in split(act_sum_ref[...], 2)]
        none = jnp.zeros((4, offset.shape[1]), f32)
        offset_rows = jnp.concatenate(offsets + offsets + [none], axis=0).astype(bf16)
        none = jnp.zeros((4, act_sum_ref.shape[1]), f32)
        sum_rows = jnp.concatenate([sums[0], sums[0], sums[1], sums[1], none], axis=0).astype(bf16)
        shift[...] = jnp.sum(dot_t(offset_rows, up_ref[...])[0:2], axis=0, keepdims=True)
        terms = t_dot(act_even_ref[...], grad) + t_dot(sum_rows, offset_rows) + gram_up_ref[...] * slope
        terms_ref[...] = terms.astype(bf16)

    for j in range(rows // chunk):
        at = pl.multiple_of(k * (rows // 4) + half * j, half)
        put_even(placed, frame_of(0) * rows + chunk * j, back_even[pl.ds(at, half), :])
    for slot, out in ((0, gz_ref), (1, gc_ref)):
        mask = frame_mask(counts_ref, k, frame_of(slot))
        act = act_ref[0, slot]
        back = (dot(act, mix[0]) + dot(act, mix[1]) + shift[...]) * mask + get_lanes(placed, slot * rows, rows)
        back = back * gelu_slope(mid_ref[0, slot])
        out[0] = jnp.where(valid_rows(back.shape, pitch, width), back, 0.0).astype(bf16)


def first_grad_kernel(
    width, orders, counts_ref, rz_ref, gz_ref, gc_ref, rc_ref, taps_ref, first_ref, x_ref,
    grad_ref, *refs
):
    outs, (frames, xpad, product) = refs[:-3], refs[-3:]
    k = pl.program_id(0)
    rows = gz_ref.shape[1]
    height, width = x_ref.shape[2], x_ref.shape[3]
    pitch = 16
    chunk = 2 * pitch

    @pl.when(k == 0)
    def _():
        clear_edges(frames, pitch, rows)
        xpad[...] = jnp.zeros_like(xpad)
        product[...] = jnp.zeros_like(product)

    fill_frames(frames, (rz_ref, gz_ref, gc_ref, rc_ref), pitch, rows)
    for slot in range(2):
        frame = frame_of(slot)
        for h in range(height):
            xpad[pl.ds(slot * rows + h * pitch, width), :] = x_ref[0, frame, h]
        scale = frame_mask(counts_ref, k, frame)

        def step(c, _):
            start = pl.multiple_of(c * chunk, chunk)
            grad = conv_rows(
                lambda i: taps_ref[pl.ds(26 - i, 1), :],
                lambda a, b: frames[slot + a, pl.ds(pl.multiple_of(start + pitch * b, pitch), chunk), :],
                chunk,
            )
            grad = grad * scale * gelu_slope(first_ref[0, slot, pl.ds(start, chunk), :])
            grad = jnp.where(valid_rows(grad.shape, pitch, width), grad, 0.0)
            grad_ref[0, pl.ds(pl.multiple_of(slot * rows + start, chunk), chunk), :] = grad.astype(bf16)
            return 0

        lax.fori_loop(0, rows // chunk, step, 0)
    product[...] += t_dot(grad_ref[0], xpad[...])

    @pl.when(k == pl.num_programs(0) - 1)
    def _():
        terms = jnp.transpose(product[...])
        if orders is None:
            outs[0][...] = terms.astype(bf16)
        else:
            clips, chips, block = orders
            xpad_rows = terms.reshape(clips * chips * 2, block, terms.shape[1])
            space, clip = lax.axis_index("space"), lax.axis_index("clip")
            keep_ref, send_ref, full = outs[0], outs[1], outs[2]
            full[...] = xpad_rows
            for b in range(clips):
                for z in range(chips):
                    at = ((clip ^ b) * chips + z) * 2
                    keep_ref[b, z] = full[at + (space & 1)]
                    send_ref[b, z] = full[at + 1 - (space & 1)].astype(bf16)


def pair_sum_kernel(keep_ref, got_ref, keep_terms_ref, got_terms_ref, *out_refs):
    wide, inner = keep_terms_ref.shape[-1], keep_ref.shape[-1]
    deep = keep_terms_ref.shape[-2]
    for b, out_ref in enumerate(out_refs):
        out_ref[:, :, pl.ds(0, wide)] = (keep_terms_ref[b] + got_terms_ref[b].astype(f32)).astype(bf16)
        total = keep_ref[b] + got_ref[b].astype(f32)
        for i in range(keep_ref.shape[-2] // deep):
            out_ref[:, :, pl.ds(wide + i * inner, inner)] = total[:, i * deep : (i + 1) * deep].astype(bf16)


def chip_totals_kernel(count, *refs):
    terms, outs = refs[:count], refs[count:]
    for z, out_ref in enumerate(outs):
        at = (lax.axis_index("space") // 2) ^ z
        total = terms[0][at].astype(f32)
        for term in terms[1:]:
            total = total + term[at].astype(f32)
        out_ref[...] = total.astype(bf16)


def finish_kernel(count, *refs):
    skip, up = refs[:count], refs[count : 2 * count]
    skip_ref, up_ref, fourth_down_ref = refs[2 * count :]

    def total(terms):
        return sum(term[...].astype(f32) for term in terms)

    skip_ref[...] = total(skip)
    both = total(up)
    block, lanes = up_ref.shape[0], fourth_down_ref.shape[1]
    up_ref[...] = both[:block]
    part = both.shape[0] - block
    for i in range(both.shape[1] // lanes):
        fourth_down_ref[pl.ds(i * part, part), :] = both[block:, i * lanes : (i + 1) * lanes]


def terms_kernel(
    count, clips, wide, small_rows, *refs
):
    received, refs = refs[:count], refs[count:]
    (grad_ref, up_ref, depth_ref, gain_ref, shift_ref, late_gain_ref, late_shift_ref, late_depth_ref, head_ref,
     *down_refs) = refs
    lanes = 128
    total = None
    for ref in received:
        for i in range(ref.shape[0]):
            total = ref[i].astype(f32) if total is None else total + ref[i].astype(f32)
    deep = total.shape[0]
    up_ref[...] = total[:, :wide]
    depth_ref[...] = total[:, wide : wide + 27]
    device = lax.axis_index("clip") * lax.axis_size("space") + lax.axis_index("space")
    end = wide + lanes * (1 + small_rows // deep)
    small = jnp.concatenate([total[:, i : i + lanes] for i in range(wide + lanes, end, lanes)], axis=0)

    def own_lanes(values, width):
        moved = pltpu.roll(values, (lanes - device * width % lanes) % lanes, 1)
        return moved[:, :width]

    late = own_lanes(small, late_gain_ref.shape[1])
    third = own_lanes(small, gain_ref.shape[1])
    late_gain_ref[...] = late[1:2]
    late_shift_ref[...] = late[0:1]
    gain_ref[...] = third[3:4]
    shift_ref[...] = third[2:3]
    everyone = clips * lax.axis_size("clip")
    late_depth_ref[...] = small[8 + everyone :, :27]
    pooled = late[8 : 8 + everyone].astype(bf16)
    head_ref[...] = sum(t_dot(pooled, part) for part in split(grad_ref[...], 3))
    for down_ref in down_refs:
        inner = down_ref.shape[1]
        for i in range(down_ref.shape[0] // deep):
            down_ref[pl.ds(i * deep, deep), :] = total[:, end + i * inner : end + (i + 1) * inner]


def clip_grad_kernel(grad_ref, down_ref, entry_grad_ref, out_ref, wide):
    _, _, height, width, _ = out_ref.shape
    pitch = 16
    half = pitch // 2
    rows = height * pitch
    for slot in range(2):
        put_lanes(wide, slot * rows, dot_t(grad_ref[0, pl.ds(slot * rows, rows), :], down_ref[...]))
    for j in range(height // 2):
        at = frame_of(0) * rows + 2 * pitch * j
        put_even(wide, at, get_even(wide, at, half) + entry_grad_ref[0, pl.ds(half * j, half), :])
    for slot in range(2):
        frame = frame_of(slot)
        for h in range(height):
            out_ref[0, frame, h] = get_lanes(wide, slot * rows + h * pitch, width).astype(bf16)


kernel_micros = {
    "first": 5.3, "mid_own": 5.0, "mid": 8.6, "entry": 3.4, "late_mid": 4.7, "post": 6.0, "skip_sums": 7.0,
    "sum_grad": 4.6, "late_taps": 3.6, "late_back": 5.0, "up_down_sums": 5.5, "third_grad": 6.7, "third_taps": 7.7,
    "up_down_total": 2.3, "skip_total": 3.0, "skip_phase": 1.0, "up_down_phase": 1.0, "finish": 2.0, "terms": 1.5, "taps": 0.6, "pooled_grad": 1.5, "head": 1.0, "add": 0.6, "skipped": 2.5, "first_grad": 10.7, "pair_sum": 1.9, "clip_sum": 1.6, "clip_grad": 5.5,
}
smem = pl.BlockSpec(memory_space=pltpu.SMEM)


def whole(shape):
    return pl.BlockSpec(shape, lambda k: (0,) * len(shape))


def by_clip(shape):
    return pl.BlockSpec((1,) + shape[1:], lambda k: (k,) + (0,) * (len(shape) - 1))


def cost(micros):
    return pl.CostEstimate(flops=0, bytes_accessed=int(micros * 3.4e6), transcendentals=0)


def call(kernel, name, inputs, outputs, scratch, clips=None, limit=LIMIT):
    if clips is None:
        def spec(kind, shape):
            return smem if kind == "s" else pl.BlockSpec(memory_space=pltpu.VMEM)
    else:
        def spec(kind, shape):
            return smem if kind == "s" else whole(shape) if kind == "w" else by_clip(shape)
    options = {} if clips is None else {"grid": (clips,)}
    return pl.pallas_call(
        kernel,
        name=name,
        out_shape=[jax.ShapeDtypeStruct(s, d) for s, d, _ in outputs],
        in_specs=[spec(kind, a.shape) for a, kind in inputs],
        out_specs=[spec(kind, s) for s, _, kind in outputs],
        scratch_shapes=scratch,
        compiler_params=pltpu.CompilerParams(vmem_limit_bytes=limit * mib),
        cost_estimate=cost(kernel_micros[name]),
        **options,
    )(*[a for a, _ in inputs])


def group_parts(values):
    size = lax.axis_size("space")
    if size != 8:
        copies = jnp.broadcast_to(values[None], (size,) + values.shape)
        return [lax.all_to_all(copies, "space", split_axis=0, concat_axis=0, tiled=True)]
    (pair,) = call(add_kernel, "add", [(values, "w"), (core_swap(values), "w")], [(values.shape, f32, "w")], [])
    return [part[None] for part in over_chips([pair] * 4)]


def w(arrays):
    return [(array, "w") for array in arrays]


def swap_neighbours(to_z, to_core):
    size = lax.axis_size("space")
    core = [(i, i ^ 1) for i in range(size)]
    z = [(i, j) for m in range(1, size - 1, 2) for i, j in ((m, m + 1), (m + 1, m))]
    return lax.ppermute(to_z, "space", z), lax.ppermute(to_core, "space", core)


def reduce_rows(term):
    return add_rows(send_rows(term))


def add_rows(received):
    return jnp.sum(received.astype(f32), axis=0)


def send_rows(term):
    parts = lax.axis_size("clip") * lax.axis_size("space")
    pieces = term.astype(bf16).reshape((parts, term.shape[0] // parts) + term.shape[1:])
    return lax.all_to_all(pieces, ("clip", "space"), split_axis=0, concat_axis=0, tiled=True)


def core_swap(values):
    return lax.ppermute(values, "space", [(i, i ^ 1) for i in range(lax.axis_size("space"))])


def own_rows(left_ref, out, starts):
    out[0] = jnp.transpose(left_ref[...])
    block = out.shape[1] // 2 // len(starts)
    for j, start in enumerate(starts):
        out[1, pl.ds(j * block, block), :] = out[0, pl.ds(pl.multiple_of(start * block, block), block), :]


def own_blocks(orders):
    space, clip = lax.axis_index("space"), lax.axis_index("clip")
    clips, chips = orders
    return [((clip ^ b) * chips + z) * 2 + (space & 1) for b in range(clips) for z in range(chips)]


def place(outs, chips, j, values):
    b, z = j // chips, j % chips
    if z < chips // 2:
        outs[b % 2][b // 2, z] = values.astype(bf16)
    else:
        outs[2 + b // 2][b % 2, z - chips // 2] = values.astype(bf16)


def first_phase(pieces):
    keep_low, send_low, keep_high, send_high = pieces
    return [keep_low, clip_swap(send_low, 1), keep_high, clip_swap(send_high, 2)]


def clip_swap(values, bit):
    return lax.ppermute(values, "clip", [(i, i ^ bit) for i in range(lax.axis_size("clip"))])


def phase_kernel(keep_low_ref, got_low_ref, keep_high_ref, got_high_ref, low_ref, low_send_ref, high_ref, high_send_ref):
    for keep, got, out, send in (
        (keep_low_ref, got_low_ref, low_ref, low_send_ref), (keep_high_ref, got_high_ref, high_ref, high_send_ref)
    ):
        out[...] = (keep[0].astype(f32) + got[0].astype(f32)).astype(bf16)
        send[...] = (keep[1].astype(f32) + got[1].astype(f32)).astype(bf16)


def second_phase(name, pieces):
    shape = pieces[0].shape[1:]
    low, low_send, high, high_send = call(phase_kernel, name, w(pieces), [(shape, bf16, "w")] * 4, [])
    return [low, clip_swap(low_send, 2), high, clip_swap(high_send, 1)]


def halves_total_kernel(low_ref, got_low_ref, high_ref, got_high_ref, *outs):
    half = low_ref.shape[0]
    for z, out_ref in enumerate(outs):
        at = (lax.axis_index("space") // 2) ^ z
        low = low_ref[at % half].astype(f32) + got_low_ref[at % half].astype(f32)
        high = high_ref[at % half].astype(f32) + got_high_ref[at % half].astype(f32)
        out_ref[...] = jnp.where(at < half, low, high).astype(bf16)


def skip_kernel(
    orders, left_ref, left_other_ref, right_ref, right_other_ref, weight_ref, back_ref, *refs
):
    clips, chips = orders
    outs, (left, left_other) = refs[:4], refs[4:]

    @pl.when(pl.program_id(0) == 0)
    def _():
        own_rows(left_ref, left, own_blocks(orders))
        own_rows(left_other_ref, left_other, own_blocks(orders))
        back_ref[...] = jnp.zeros_like(back_ref)

    half = left.shape[1] // 2
    total = dot(left[1, pl.ds(0, half)], right_ref[...]) + dot(left_other[1, pl.ds(0, half)], right_other_ref[...])
    block = half // (clips * chips)
    for j in range(clips * chips):
        place(outs, chips, j, total[j * block : (j + 1) * block])
    back_ref[...] += dot_t(right_ref[...], weight_ref[...])


def skip_sums(left, left_other, right, right_other, weight, parts, orders):
    block = left.shape[1] // parts
    wide = right.shape[1]
    lanes = 512
    rows, deep = left.shape
    return pl.pallas_call(
        functools.partial(skip_kernel, orders),
        name="skip_sums",
        grid=(wide // lanes,),
        out_shape=[
            jax.ShapeDtypeStruct((rows, deep), f32),
            *[jax.ShapeDtypeStruct((2, orders[1] // 2, block, wide), bf16)] * 4,
        ],
        in_specs=[pl.BlockSpec((rows, deep), lambda n: (0, 0))] * 2
        + [pl.BlockSpec((rows, lanes), lambda n: (0, n))] * 2
        + [pl.BlockSpec((deep, lanes), lambda n: (0, n))],
        out_specs=[
            pl.BlockSpec((rows, deep), lambda n: (0, 0)),
            *[pl.BlockSpec((2, orders[1] // 2, block, lanes), lambda n: (0, 0, 0, n))] * 4,
        ],
        scratch_shapes=[pltpu.VMEM((2, deep, rows), bf16)] * 2,
        compiler_params=pltpu.CompilerParams(vmem_limit_bytes=LIMIT * mib),
        cost_estimate=cost(kernel_micros["skip_sums"]),
    )(left, left_other, right, right_other, weight)


def products_kernel(
    orders, act_ref, act_other_ref, entry_ref, entry_other_ref, first_ref, first_other_ref, sum_ref, sum_other_ref,
    *refs
):
    clips, chips = orders
    outs, (act, act_other, entry, entry_other, down) = refs[:4], refs[4:]
    n = pl.program_id(0)

    @pl.when(n == 0)
    def _():
        blocks = own_blocks(orders)
        own_rows(act_ref, act, blocks)
        own_rows(act_other_ref, act_other, blocks)
        own_rows(entry_ref, entry, blocks)
        own_rows(entry_other_ref, entry_other, blocks)
        half = entry.shape[1] // 2
        down[...] = (
            dot(entry[1, pl.ds(0, half)], first_ref[...]) + dot(entry_other[1, pl.ds(0, half)], first_other_ref[...])
        ).reshape(down.shape)

    half = act.shape[1] // 2
    up = dot(act[1, pl.ds(0, half)], sum_ref[...]) + dot(act_other[1, pl.ds(0, half)], sum_other_ref[...])
    block = half // (clips * chips)
    part = outs[0].shape[2] - block
    for j in range(clips * chips):
        under = down[j, pl.ds(pl.multiple_of(n * part, part), part), :]
        place(outs, chips, j, jnp.concatenate([up[j * block : (j + 1) * block], under], axis=0))


def up_down_sums(act, act_other, entry, entry_other, first, first_other, sums, sums_other, parts, orders):
    rows, deep = entry.shape
    inner, wide = act.shape[1], sums.shape[1]
    lanes = inner
    clips, chips = orders
    up_block, down_block = inner // parts, deep // parts
    block = up_block + down_block * inner // wide
    same = lambda n: (0, 0)
    return pl.pallas_call(
        functools.partial(products_kernel, orders),
        name="up_down_sums",
        grid=(wide // lanes,),
        out_shape=[jax.ShapeDtypeStruct((2, chips // 2, block, wide), bf16)] * 4,
        in_specs=[pl.BlockSpec((rows, inner), same)] * 2
        + [pl.BlockSpec((rows, deep), same)] * 2
        + [pl.BlockSpec((rows, inner), same)] * 2
        + [pl.BlockSpec((rows, lanes), lambda n: (0, n))] * 2,
        out_specs=[pl.BlockSpec((2, chips // 2, block, lanes), lambda n: (0, 0, 0, n))] * 4,
        scratch_shapes=[pltpu.VMEM((2, inner, rows), bf16)] * 2
        + [pltpu.VMEM((2, deep, rows), bf16)] * 2
        + [pltpu.VMEM((clips * chips, down_block, inner), f32)],
        compiler_params=pltpu.CompilerParams(vmem_limit_bytes=LIMIT * mib),
        cost_estimate=cost(kernel_micros["up_down_sums"]),
    )(act, act_other, entry, entry_other, first, first_other, sums, sums_other)


def over_clip(pieces):
    size = len(pieces)
    return [pieces[0]] + [lax.ppermute(pieces[b], "clip", [(i, i ^ b) for i in range(size)]) for b in range(1, size)]


def over_chips(pieces):
    size = len(pieces)
    return [pieces[0]] + [
        lax.ppermute(pieces[z], "space", [(i, i ^ (2 * z)) for i in range(2 * size)]) for z in range(1, size)
    ]


def skipped_sums(entry, weight):
    rows, deep = entry.shape
    wide = weight.shape[1]
    lanes = 512
    return pl.pallas_call(
        skipped_kernel,
        name="skipped",
        grid=(wide // lanes,),
        out_shape=jax.ShapeDtypeStruct((rows, wide), bf16),
        in_specs=[pl.BlockSpec((rows, deep), lambda n: (0, 0)), pl.BlockSpec((deep, lanes), lambda n: (0, n))],
        out_specs=pl.BlockSpec((rows, lanes), lambda n: (0, n)),
        compiler_params=pltpu.CompilerParams(vmem_limit_bytes=LIMIT * mib),
        cost_estimate=cost(kernel_micros["skipped"]),
    )(entry, weight)


def after(values, token):
    return lax.optimization_barrier((values, token))[0]


def per_device(
    clip_input, frame_counts, third_down, third_depth, third_up, third_gain, third_shift,
    fourth_down, fourth_skip, fourth_depth, fourth_up, fourth_gain, fourth_shift,
    classifier, class_bias, logit_grad,
):
    clips, frames, height, width, channels = clip_input.shape
    inner = third_down.shape[1]
    late_inner = fourth_down.shape[1]
    late_wide = fourth_up.shape[1]
    half_width = width // 2
    rows = height * 16
    late_rows = height // 2 * 8
    late_all = clips * late_rows
    cells = height * width
    late_cells = (height // 2) * half_width
    parts = lax.axis_size("clip") * lax.axis_size("space")
    clip_axis, chips = lax.axis_size("clip"), lax.axis_size("space") // 2
    by_pairs = clip_axis == 4 and chips == 4 and channels // parts % 32 == 0 and late_inner // parts % 16 == 0
    orders = (clip_axis, chips) if by_pairs else None
    third_gain, third_shift = third_gain[None], third_shift[None]
    fourth_gain, fourth_shift = fourth_gain[None], fourth_shift[None]
    head = jnp.transpose(classifier)

    first, act_z, act_c, even_x = call(
        first_kernel, "first",
        [(frame_counts, "s"), (clip_input, "c"), (third_down, "w")],
        [
            ((clips, 2, rows, inner), f32, "c"),
            ((clips, rows, inner), bf16, "c"),
            ((clips, rows, inner), bf16, "c"),
            ((clips, late_rows, channels), f32, "c"),
        ],
        [pltpu.VMEM((rows, channels), bf16), pltpu.VMEM((channels // 128, 16, 128), f32)],
        clips=clips,
    )
    got_z, got_c = swap_neighbours(act_z, act_c)
    third_taps, late_taps = call(
        taps_kernel, "taps", w([jnp.transpose(third_depth), jnp.transpose(fourth_depth)]),
        [((27, inner), f32, "w"), ((27, late_inner), f32, "w")], [],
    )
    (mid_part,) = call(
        mid_own_kernel, "mid_own",
        [(act_z, "c"), (act_c, "c"), (third_taps, "w")],
        [((clips, 2, rows, inner), f32, "c")],
        [pltpu.VMEM((2, rows + 32, inner), f32)],
        clips=clips,
    )
    mid, mid_act, act_even, even_sum, moments, gram_up, act_sum = call(
        functools.partial(mid_kernel, width), "mid",
        [(frame_counts, "s"), (got_z, "c"), (got_c, "c"), (mid_part, "c"), (third_taps, "w"), (third_up, "w")],
        [
            ((clips, 2, rows, inner), f32, "c"),
            ((clips, 2, rows, inner), bf16, "c"),
            ((late_all, inner), bf16, "w"),
            ((late_all, channels), f32, "w"),
            ((2, channels), f32, "w"),
            ((inner, channels), f32, "w"),
            ((1, inner), f32, "w"),
        ],
        [
            pltpu.VMEM((2, rows + 32, inner), f32),
            pltpu.VMEM((inner // 128, 2 * rows, 128), f32),
            pltpu.VMEM((late_all, inner), f32),
            pltpu.VMEM((inner, inner), f32),
            pltpu.VMEM((8, inner), f32),
        ],
        clips=clips,
    )
    even_sum = even_sum.reshape(clips, late_rows, channels)
    moments = group_parts(moments)
    stats, even_hat, entry, late_first, late_act = call(
        functools.partial(entry_kernel, half_width, cells, len(moments)), "entry",
        [(frame_counts, "s"), *w(moments), (even_x, "w"), (even_sum, "w"),
         (third_gain, "w"), (third_shift, "w"), (fourth_down, "w")],
        [
            ((2, channels), f32, "w"),
            ((clips, late_rows, channels), f32, "w"),
            ((late_all, channels), bf16, "w"),
            ((late_all, late_inner), f32, "w"),
            ((clips, late_rows, late_inner), bf16, "w"),
        ],
        [],
    )
    late_first = late_first.reshape(clips, late_rows, late_inner)
    late_z, late_c = swap_neighbours(late_act, late_act)
    (pooled_grad,) = call(pooled_grad_kernel, "pooled_grad", w([logit_grad, head]), [((clips, late_wide), f32, "w")], [])
    skipped = skipped_sums(entry, fourth_skip).reshape(clips, late_rows, late_wide)
    late_mid, late_mid_act, late_sum, late_moments = call(
        functools.partial(late_kernel, half_width), "late_mid",
        [(frame_counts, "s"), (late_z, "w"), (late_act, "w"), (late_c, "w"), (late_taps, "w"), (fourth_up, "w")],
        [
            ((clips, late_rows, late_inner), f32, "w"),
            ((late_all, late_inner), bf16, "w"),
            ((late_all, late_wide), bf16, "w"),
            ((2, late_wide), f32, "w"),
        ],
        [
            pltpu.VMEM((3, late_rows + 16, late_inner), f32),
            pltpu.VMEM((clips, late_rows, late_inner), f32),
        ],
    )
    late_sum = late_sum.reshape(clips, late_rows, late_wide)
    late_moments = group_parts(late_moments)
    late_stats, late_back, pooled, pre_grad, skip_grad = call(
        functools.partial(post_kernel, half_width, late_cells, len(late_moments)), "post",
        [(frame_counts, "s"), *w(late_moments), (late_sum, "w"), (skipped, "w"),
         (fourth_gain, "w"), (fourth_shift, "w"), (pooled_grad, "w")],
        [
            ((2, late_wide), f32, "w"),
            ((2, late_wide), f32, "w"),
            ((clips, late_wide), f32, "w"),
            ((clips, late_rows, late_wide), f32, "w"),
            ((clips, late_rows, late_wide), bf16, "w"),
        ],
        [],
    )
    received = group_parts(late_back)
    logit_terms, bias_grad = call(
        head_kernel, "head", w([after(pooled, received[0]), head, logit_grad]),
        [((clips // 2, channels), f32, "w"), ((1, logit_grad.shape[1]), f32, "w")], [],
    )
    late_stats = after(late_stats, logit_terms)
    skip_rows = skip_grad.reshape(late_all, late_wide)
    if by_pairs:
        entry_other = core_swap(entry)
        skip_back, *skip_pieces = skip_sums(
            entry, entry_other, skip_rows, core_swap(after(skip_rows, received[0])), fourth_skip, parts, (clip_axis, chips)
        )
    else:
        skip_back = dot_t(skip_rows, fourth_skip)
        fourth_skip_grad = reduce_rows(t_dot(entry, skip_rows))
    late_stats = after(late_stats, skip_back)
    late_sum_grad, late_mid_grad = call(
        functools.partial(sum_grad_kernel, half_width, late_cells, len(received)), "sum_grad",
        [(frame_counts, "s"), *w(received), (late_stats, "w"), (late_sum, "w"), (pre_grad, "w"),
         (fourth_gain, "w"), (fourth_up, "w"), (late_mid, "w")],
        [
            ((late_all, late_wide), bf16, "w"),
            ((clips, late_rows, late_inner), bf16, "w"),
        ],
        [],
    )
    late_gz, late_gc = swap_neighbours(late_mid_grad, late_mid_grad)
    if by_pairs:
        skip_pieces = first_phase(after(skip_pieces, late_mid_grad))
    (late_taps_table,) = call(
        late_taps_kernel, "late_taps",
        [(late_z, "w"), (late_act, "w"), (late_c, "w"), (late_mid_grad, "w")],
        [((late_inner, 128), f32, "w")],
        [pltpu.VMEM((3, clips, late_rows + 16, late_inner), f32)],
    )
    late_first = after(late_first, late_taps_table)
    late_first_grad, entry_grad, third_back = call(
        functools.partial(late_back_kernel, half_width), "late_back",
        [(frame_counts, "s"), (late_gz, "w"), (late_mid_grad, "w"), (late_gc, "w"), (late_taps, "w"),
         (late_first, "w"), (fourth_down, "w"), (skip_back, "w"), (even_hat, "w"), (logit_terms, "w")],
        [
            ((late_all, late_inner), bf16, "w"),
            ((clips, late_rows, channels), f32, "w"),
            ((2 + clips // 2, channels), f32, "w"),
        ],
        [
            pltpu.VMEM((3, late_rows + 16, late_inner), f32),
            pltpu.VMEM((clips, late_rows, late_inner), f32),
        ],
    )
    received = group_parts(third_back)
    if by_pairs:
        up_pieces = up_down_sums(
            late_mid_act, core_swap(late_mid_act), entry, entry_other, late_first_grad, core_swap(late_first_grad),
            late_sum_grad, core_swap(late_sum_grad), parts, (clip_axis, chips),
        )
        skip_pieces = second_phase("skip_phase", after(skip_pieces, up_pieces[0]))
        stats = after(stats, skip_pieces[0])
    else:
        fourth_up_grad = reduce_rows(t_dot(late_mid_act, late_sum_grad))
        fourth_down_grad = reduce_rows(t_dot(entry, late_first_grad))
    grad_z, grad_c, up_terms, logits = call(
        functools.partial(third_grad_kernel, width, cells, len(received)), "third_grad",
        [(frame_counts, "s"), *w(received), (stats, "w"), (third_gain, "w"),
         (entry_grad.reshape(late_all, channels), "w"), (third_up, "w"), (act_even, "w"), (act_sum, "w"),
         (gram_up, "w"), (class_bias[None], "w"), (mid_act, "c"), (mid, "c")],
        [
            ((clips, rows, inner), bf16, "c"),
            ((clips, rows, inner), bf16, "c"),
            ((inner, channels), bf16, "w"),
            ((clips, logit_grad.shape[1]), f32, "w"),
        ],
        [
            pltpu.VMEM((late_all, inner), f32),
            pltpu.VMEM((2, inner, inner), bf16),
            pltpu.VMEM((1, inner), f32),
            pltpu.VMEM((inner // 128, 2 * rows, 128), f32),
        ],
        clips=clips,
    )
    third_gz, third_gc = swap_neighbours(grad_z, grad_c)
    small_rows = 8 + clips * clip_axis + late_inner // parts
    deep = inner // parts
    extra = 128 * (1 + small_rows // deep)
    if by_pairs:
        term_outputs = [
            ((clip_axis, chips, deep, channels + extra), f32, "w"),
            ((clip_axis, chips, deep, channels + extra), bf16, "w"),
        ]
    else:
        term_outputs = [((inner, channels + extra), bf16, "w")]
    third_terms = call(
        functools.partial(third_taps_kernel, orders, parts), "third_taps",
        [(got_z, "c"), (act_z, "c"), (act_c, "c"), (got_c, "c"), (grad_z, "c"), (grad_c, "c"),
         (up_terms, "w"), (late_back, "w"), (third_back, "w"), (pooled, "w"), (late_taps_table, "w")],
        term_outputs,
        [
            pltpu.VMEM((4, rows + 32, inner), f32),
            pltpu.VMEM((2, rows, inner), f32),
            pltpu.VMEM((27, 8, inner), f32),
            pltpu.VMEM((inner, channels + extra), f32),
        ],
        clips=clips,
    )
    first = after(first, third_terms[0])
    if by_pairs:
        skip_pieces = call(
            halves_total_kernel, "skip_total", w(after(skip_pieces, third_terms[0])),
            [(skip_pieces[0].shape[1:], bf16, "w")] * chips, [],
        )
        first = after(first, skip_pieces[0])
        up_pieces = first_phase(after(up_pieces, third_terms[0]))
        skip_pieces = over_chips(after(skip_pieces, third_terms[0]))
    block = channels // parts
    if by_pairs:
        down_outputs = [
            ((clip_axis, chips, block, inner), f32, "w"),
            ((clip_axis, chips, block, inner), bf16, "w"),
        ]
        down_scratch = [pltpu.VMEM((parts, block, inner), f32)]
    else:
        down_outputs, down_scratch = [((channels, inner), bf16, "w")], []
    first_grad, *down_terms = call(
        functools.partial(first_grad_kernel, width, (clip_axis, chips, block) if by_pairs else None), "first_grad",
        [(frame_counts, "s"), (third_gz, "c"), (grad_z, "c"), (grad_c, "c"), (third_gc, "c"),
         (third_taps, "w"), (first, "c"), (clip_input, "c")],
        [((clips, 2 * rows, inner), bf16, "c"), *down_outputs],
        [
            *down_scratch,
            pltpu.VMEM((4, rows + 32, inner), f32),
            pltpu.VMEM((2 * rows, channels), bf16),
            pltpu.VMEM((inner, channels), f32),
        ],
        clips=clips,
    )
    (clip_grad,) = call(
        clip_grad_kernel, "clip_grad",
        [(first_grad, "c"), (third_down, "w"), (entry_grad, "c")],
        [(clip_input.shape, bf16, "c")],
        [pltpu.VMEM((channels // 128, 2 * rows, 128), f32)],
        clips=clips,
    )
    if by_pairs:
        keep, send = down_terms
        keep_terms, send_terms = third_terms
        up_pieces = second_phase("up_down_phase", after(up_pieces, first_grad))
        clip_parts = call(
            pair_sum_kernel, "pair_sum",
            w([keep, core_swap(send), keep_terms, core_swap(after(send_terms, third_gz))]),
            [((chips, deep, channels + extra + block // deep * inner), bf16, "w")] * clip_axis,
            [],
        )
        up_pieces = call(
            halves_total_kernel, "up_down_total", w(after(up_pieces, (clip_parts[0], skip_pieces))),
            [(up_pieces[0].shape[1:], bf16, "w")] * chips, [],
        )
        clip_parts = over_clip(clip_parts)
        up_pieces = over_chips(up_pieces)
        chip_parts = call(
            functools.partial(chip_totals_kernel, clip_axis), "clip_sum", w(after(clip_parts, (up_pieces[0], clip_grad))),
            [(clip_parts[0].shape[1:], bf16, "w")] * chips, [],
        )
        third_terms = [part[None] for part in over_chips(chip_parts)]
        up_block = late_inner // parts
        fourth_skip_grad, fourth_up_grad, fourth_down_grad = call(
            functools.partial(finish_kernel, chips), "finish", w(skip_pieces + up_pieces),
            [
                ((block, late_wide), f32, "w"),
                ((up_block, late_wide), f32, "w"),
                ((block, late_inner), f32, "w"),
            ],
            [],
        )
    else:
        third_down_grad = add_rows(send_rows(down_terms[0]))
        third_terms = [send_rows(third_terms[0])]
    own, own_third, own_taps = late_wide // parts, channels // parts, late_inner // parts
    third_up_grad, third_depth_grad, gain, shift, late_gain, late_shift, fourth_depth_grad, classifier_grad, *down = call(
        functools.partial(terms_kernel, len(third_terms), clips, channels, small_rows), "terms",
        w(third_terms + [logit_grad]),
        [
            ((deep, channels), f32, "w"),
            ((deep, 27), f32, "w"),
            ((1, own_third), f32, "w"),
            ((1, own_third), f32, "w"),
            ((1, own), f32, "w"),
            ((1, own), f32, "w"),
            ((own_taps, 27), f32, "w"),
            ((own, logit_grad.shape[1]), f32, "w"),
            *([((block, inner), f32, "w")] if by_pairs else []),
        ],
        [],
    )
    if by_pairs:
        (third_down_grad,) = down
    return (
        logits,
        clip_grad,
        third_down_grad,
        third_depth_grad,
        third_up_grad,
        gain.reshape(-1),
        shift.reshape(-1),
        fourth_down_grad,
        fourth_skip_grad,
        fourth_depth_grad,
        fourth_up_grad,
        late_gain.reshape(-1),
        late_shift.reshape(-1),
        classifier_grad,
        bias_grad.reshape(-1),
    )


def solution(mesh):
    both = ("clip", "space")
    return jax.shard_map(
        per_device,
        mesh=mesh,
        in_specs=(P("clip", "space", None, None, None), P("clip")) + (P(),) * 14,
        out_specs=(
            P("clip", None),
            P("clip", "space", None, None, None),
            P(both, None),
            P(both, None),
            P(both, None),
            P(both),
            P(both),
            P(both, None),
            P(both, None),
            P(both, None),
            P(both, None),
            P(both),
            P(both),
            P(both, None),
            P(),
        ),
        check_vma=False,
    )
```

```python
import functools
import math

import jax
import jax.numpy as jnp
from jax import lax
from jax.experimental import pallas as pl
from jax.experimental.pallas import tpu as pltpu
from jax.sharding import PartitionSpec as P

eps = 1e-05
f32 = jnp.float32
bf16 = jnp.bfloat16
mib = 1 << 20
LIMIT = 16


def gelu_terms(x):
    c = math.sqrt(2.0 / math.pi)
    x2 = x * x
    t = jnp.tanh(x * (c + (c * 0.044715) * x2))
    return x2, t


def gelu(x):
    _, t = gelu_terms(x)
    return x * (0.5 + 0.5 * t)


def gelu_slope(x):
    c = math.sqrt(2.0 / math.pi)
    x2, t = gelu_terms(x)
    return 0.5 + 0.5 * t + (0.5 * x) * ((1.0 - t * t) * (c + (3.0 * c * 0.044715) * x2))


def gelu_both(x):
    c = math.sqrt(2.0 / math.pi)
    x2, t = gelu_terms(x)
    cdf = 0.5 + 0.5 * t
    return x * cdf, cdf + (0.5 * x) * ((1.0 - t * t) * (c + (3.0 * c * 0.044715) * x2))


def valid_rows(shape, group, used):
    return lax.broadcasted_iota(jnp.int32, shape, 0) % group < used


def row_sums(values):
    rows, width = values.shape
    return jnp.sum(values.reshape(rows // 8, 8, width), axis=0)


def dot(left, right):
    return jnp.dot(left, right, preferred_element_type=f32)


def dot_t(left, right):
    return lax.dot_general(left, right, (((1,), (1,)), ((), ())), preferred_element_type=f32)


def t_dot(left, right):
    return lax.dot_general(left, right, (((0,), (0,)), ((), ())), preferred_element_type=f32)


def put_lanes(ref, start, values):
    rows, channels = values.shape
    for j in range(channels // 128):
        ref[j, pl.ds(start, rows), :] = values[:, 128 * j : 128 * (j + 1)]


def get_lanes(ref, start, rows):
    return jnp.concatenate([ref[j, pl.ds(start, rows), :] for j in range(ref.shape[0])], axis=1)


def get_even(ref, start, count):
    return jnp.concatenate(
        [ref[j, pl.ds(start, count, stride=2), :] for j in range(ref.shape[0])], axis=1
    )


def put_even(ref, start, values):
    rows, channels = values.shape
    for j in range(channels // 128):
        ref[j, pl.ds(start, rows, stride=2), :] = values[:, 128 * j : 128 * (j + 1)]


def conv_rows(taps, load, rows, times=(0, 1, 2)):
    sums = [None, None, None]
    for a in times:
        for b in range(3):
            block = load(a, b)
            for e in range(3):
                term = block * taps(9 * a + 3 * b + e)
                sums[e] = term if sums[e] is None else sums[e] + term
    return pltpu.roll(sums[0], 1, 0) + sums[1] + pltpu.roll(sums[2], rows - 1, 0)


def split(values, count):
    parts = []
    for _ in range(count):
        parts.append(values.astype(bf16))
        values = values - parts[-1].astype(f32)
    return parts


def frame_of(slot):
    parity = lax.axis_index("space") & 1
    return parity if slot == 0 else 1 - parity


def frame_mask(counts_ref, k, frame):
    return jnp.where(2 * lax.axis_index("space") + frame < counts_ref[k], 1.0, 0.0).astype(f32)


def cell_total(counts_ref, late, cells):
    total = 0
    for k in range(counts_ref.shape[0]):
        total += (counts_ref[k] + 1) // 2 if late else counts_ref[k]
    return (total * cells).astype(f32)


def received_sum(refs):
    total = None
    for ref in refs:
        for i in range(ref.shape[0]):
            total = ref[i] if total is None else total + ref[i]
    return total


def taps_kernel(third_ref, fourth_ref, third_out, fourth_out):
    swapped = (lax.axis_index("space") & 1) == 1
    for source, out in ((third_ref, third_out), (fourth_ref, fourth_out)):
        for a in range(3):
            here, there = source[pl.ds(9 * a, 9), :], source[pl.ds(9 * (2 - a), 9), :]
            out[pl.ds(9 * a, 9), :] = jnp.where(swapped, there, here)


def pooled_grad_kernel(grad_ref, head_ref, out_ref):
    full = sum(dot(part, head_ref[...]) for part in split(grad_ref[...], 3))
    clips = out_ref.shape[0]
    clip = lax.axis_index("clip")
    own = full[:clips]
    for g in range(1, full.shape[0] // clips):
        own = jnp.where(clip == g, full[g * clips : (g + 1) * clips], own)
    out_ref[...] = own.astype(bf16).astype(f32)


def head_kernel(pooled_ref, head_ref, grad_ref, logits_ref, bias_grad_ref):
    terms = sum(dot_t(part, head_ref[...]) for part in split(pooled_ref[...], 3))
    clips, classes = terms.shape
    wide = logits_ref.shape[1] // 2
    logits_ref[...] = jnp.zeros_like(logits_ref)
    for k in range(clips):
        logits_ref[pl.ds(k // 2, 1), pl.ds(k % 2 * wide, classes)] = terms[k : k + 1]
    bias_grad_ref[...] = jnp.sum(grad_ref[...], axis=0, keepdims=True)


def add_kernel(one_ref, two_ref, out_ref):
    out_ref[...] = one_ref[...] + two_ref[...]


def skipped_kernel(entry_ref, weight_ref, out_ref):
    out_ref[...] = dot(entry_ref[...], weight_ref[...]).astype(bf16)


def first_kernel(counts_ref, x_ref, w_ref, first_ref, actz_ref, actc_ref, even_ref, xpad, xe):
    k = pl.program_id(0)
    _, _, height, width, _ = x_ref.shape
    pitch = xe.shape[1]

    @pl.when(k == 0)
    def _():
        xpad[...] = jnp.zeros_like(xpad)
        xe[...] = jnp.zeros_like(xe)

    for slot, act_ref in ((0, actz_ref), (1, actc_ref)):
        frame = frame_of(slot)
        for h in range(height):
            xpad[pl.ds(h * pitch, width), :] = x_ref[0, frame, h]
        first = dot(xpad[...], w_ref[...])
        first_ref[0, slot] = first
        act_ref[0] = (gelu(first) * frame_mask(counts_ref, k, frame)).astype(bf16)
    for h in range(0, height, 2):
        put_lanes(xe, 0, x_ref[0, 0, h].astype(f32))
        even_ref[0, pl.ds(h // 2 * (pitch // 2), pitch // 2), :] = get_even(xe, 0, pitch // 2)


def fill_frames(frames, sources, pad, rows):
    for s, source in enumerate(sources):
        frames[s, pl.ds(pad, rows), :] = source[0].astype(f32)


def clear_edges(frames, pad, rows):
    edge = jnp.zeros((pad, frames.shape[-1]), f32)
    for s in range(frames.shape[0]):
        frames[s, pl.ds(0, pad), :] = edge
        frames[s, pl.ds(pad + rows, pad), :] = edge


def mid_own_kernel(oz_ref, oc_ref, taps_ref, part_ref, frames):
    rows = oz_ref.shape[1]
    pitch = 16
    chunk = 2 * pitch

    @pl.when(pl.program_id(0) == 0)
    def _():
        clear_edges(frames, pitch, rows)

    fill_frames(frames, (oz_ref, oc_ref), pitch, rows)
    for slot in range(2):
        def step(c, _):
            start = pl.multiple_of(c * chunk, chunk)
            part_ref[0, slot, pl.ds(start, chunk), :] = conv_rows(
                lambda i: taps_ref[pl.ds(i, 1), :],
                lambda a, b: frames[slot + a - 1, pl.ds(pl.multiple_of(start + pitch * b, pitch), chunk), :],
                chunk,
                (1, 2) if slot == 0 else (0, 1),
            )
            return 0

        lax.fori_loop(0, rows // chunk, step, 0)


def mid_kernel(
    width, counts_ref, rz_ref, rc_ref, part_ref, taps_ref, up_ref,
    mid_ref, act_ref, act_even_ref, even_ref, moment_ref, gram_up_ref, act_sum_ref,
    frames, acts, evens, gram, total,
):
    k = pl.program_id(0)
    rows = rz_ref.shape[1]
    pitch = 16
    chunk = 2 * pitch
    half = pitch // 2

    @pl.when(k == 0)
    def _():
        clear_edges(frames, pitch, rows)
        gram[...] = jnp.zeros_like(gram)
        total[...] = jnp.zeros_like(total)

    fill_frames(frames, (rz_ref, rc_ref), pitch, rows)
    for slot in range(2):
        def step(c, _):
            start = pl.multiple_of(c * chunk, chunk)
            mid = part_ref[0, slot, pl.ds(start, chunk), :] + conv_rows(
                lambda i: taps_ref[pl.ds(i, 1), :],
                lambda a, b: frames[slot, pl.ds(pl.multiple_of(start + pitch * b, pitch), chunk), :],
                chunk,
                (0,) if slot == 0 else (2,),
            )
            mid_ref[0, slot, pl.ds(start, chunk), :] = mid
            act = jnp.where(valid_rows(mid.shape, pitch, width), gelu(mid), 0.0)
            act_ref[0, slot, pl.ds(start, chunk), :] = act.astype(bf16)
            put_lanes(acts, slot * rows + start, act)
            return 0

        lax.fori_loop(0, rows // chunk, step, 0)
        act = act_ref[0, slot]
        mask = frame_mask(counts_ref, k, frame_of(slot))
        gram[...] += t_dot(act, act) * mask
        total[...] += row_sums(act.astype(f32)) * mask
    for j in range(rows // chunk):
        at = pl.multiple_of(k * (rows // 4) + half * j, half)
        evens[pl.ds(at, half), :] = get_even(acts, frame_of(0) * rows + chunk * j, half)

    @pl.when(k == pl.num_programs(0) - 1)
    def _():
        act_even_ref[...] = evens[...].astype(bf16)
        even_ref[...] = dot(act_even_ref[...], up_ref[...])
        gram_up = sum(dot(part, up_ref[...]) for part in split(gram[...], 3))
        gram_up_ref[...] = gram_up
        act_sum = jnp.sum(total[...], axis=0, keepdims=True)
        act_sum_ref[...] = act_sum
        rows_of_sum = jnp.concatenate(
            [part.astype(f32) for part in split(act_sum, 3)] + [jnp.zeros((5,) + act_sum.shape[1:], f32)], axis=0
        ).astype(bf16)
        moment_ref[0:1] = jnp.sum(dot(rows_of_sum, up_ref[...]), axis=0, keepdims=True)
        moment_ref[1:2] = jnp.sum(gram_up * up_ref[...].astype(f32), axis=0, keepdims=True)


def norm_stats(refs, cells):
    totals = received_sum(refs)
    center = totals[0:1] / cells
    return center, lax.rsqrt(totals[1:2] / cells - center * center + eps)


def entry_kernel(
    width, cells, count, counts_ref, *refs
):
    moments, refs = refs[:count], refs[count:]
    (even_x_ref, even_ref, gain_ref, shift_ref, down_ref, stats_ref, hat_ref, entry_ref, first_ref, act_ref) = refs
    center, scale = norm_stats(moments, cell_total(counts_ref, False, cells))
    stats_ref[0:1] = center
    stats_ref[1:2] = scale
    clips, rows, channels = even_ref.shape
    for k in range(clips):
        hat = (even_ref[k] - center) * scale
        hat_ref[k] = hat
        entry = even_x_ref[k] + hat * gain_ref[...] + shift_ref[...]
        entry = jnp.where(valid_rows(entry.shape, 8, width), entry, 0.0)
        entry_ref[pl.ds(k * rows, rows), :] = entry.astype(bf16)
    late = dot(entry_ref[...], down_ref[...])
    first_ref[...] = late
    for k in range(clips):
        act_ref[k] = (gelu(late[k * rows : (k + 1) * rows]) * frame_mask(counts_ref, k, 0)).astype(bf16)


def late_kernel(
    width, counts_ref, rz_ref, own_ref, rc_ref, taps_ref, up_ref,
    mid_ref, act_ref, sum_ref, moment_ref, frames, wide,
):
    clips, rows, channels = own_ref.shape
    pitch = 8
    edge = jnp.zeros((pitch, channels), f32)
    lanes = 128

    def clip_step(k, _):
        for s, source in enumerate((rz_ref, own_ref, rc_ref)):
            frames[s, pl.ds(0, pitch), :] = edge
            frames[s, pl.ds(pitch + rows, pitch), :] = edge
            frames[s, pl.ds(pitch, rows), :] = source[k].astype(f32)
        for l in range(channels // lanes):
            cols = pl.ds(l * lanes, lanes)
            mid = conv_rows(
                lambda i: taps_ref[pl.ds(i, 1), cols],
                lambda a, b: frames[a, pl.ds(pitch * b, rows), cols],
                rows,
            )
            mid_ref[k, :, cols] = mid
            wide[k, :, cols] = jnp.where(valid_rows(mid.shape, pitch, width), gelu(mid), 0.0)
        return 0

    lax.fori_loop(0, clips, clip_step, 0)
    for k in range(clips):
        act_ref[pl.ds(k * rows, rows), :] = wide[k].astype(bf16)
    late = dot(act_ref[...], up_ref[...]).astype(bf16)
    sum_ref[...] = late
    late = late.astype(f32)
    one = two = None
    for k in range(clips):
        block = late[k * rows : (k + 1) * rows]
        mask = frame_mask(counts_ref, k, 0)
        a, b = row_sums(block) * mask, row_sums(block * block) * mask
        one, two = (a, b) if one is None else (one + a, two + b)
    moment_ref[0:1] = jnp.sum(one, axis=0, keepdims=True)
    moment_ref[1:2] = jnp.sum(two, axis=0, keepdims=True)


def post_kernel(
    width, cells, count, counts_ref, *refs
):
    moments, refs = refs[:count], refs[count:]
    (sum_ref, skip_ref, gain_ref, shift_ref, pooled_grad_ref, stats_ref, back_ref, pooled_ref, pre_ref,
     skip_grad_ref) = refs
    center, scale = norm_stats(moments, cell_total(counts_ref, True, cells))
    stats_ref[0:1] = center
    stats_ref[1:2] = scale
    clips, rows, channels = sum_ref.shape
    one = two = None
    for k in range(clips):
        hat = (sum_ref[k].astype(f32) - center) * scale
        post, slope = gelu_both(hat * gain_ref[...] + shift_ref[...] + skip_ref[k].astype(f32))
        keep = valid_rows(post.shape, 8, width)
        mask = frame_mask(counts_ref, k, 0)
        pool = ((counts_ref[k] + 1) // 2 * cells).astype(f32)
        pooled = jnp.sum(jnp.where(keep, post, 0.0), axis=0, keepdims=True) * mask / pool
        pooled_ref[pl.ds(k, 1)] = pooled
        pre = jnp.where(keep, pooled_grad_ref[pl.ds(k, 1)] * mask / pool * slope, 0.0)
        pre_ref[k] = pre
        skip_grad_ref[k] = pre.astype(bf16)
        a, b = row_sums(pre), row_sums(pre * hat)
        one, two = (a, b) if one is None else (one + a, two + b)
    back_ref[0:1] = jnp.sum(one, axis=0, keepdims=True)
    back_ref[1:2] = jnp.sum(two, axis=0, keepdims=True)


def sum_grad_kernel(
    width, cells, count, counts_ref, *refs
):
    received, refs = refs[:count], refs[count:]
    (stats_ref, sum_ref, pre_ref, gain_ref, up_ref, mid_ref, sum_grad_ref, mid_grad_ref) = refs
    totals = received_sum(received) / cell_total(counts_ref, True, cells)
    center, scale = stats_ref[0:1], stats_ref[1:2]
    lead = gain_ref[...] * scale
    clips, rows, channels = sum_ref.shape
    for k in range(clips):
        hat = (sum_ref[k].astype(f32) - center) * scale
        weight = frame_mask(counts_ref, k, 0)
        grad = lead * (pre_ref[k] - weight * (totals[0:1] + hat * totals[1:2]))
        grad = jnp.where(valid_rows(grad.shape, 8, width), grad, 0.0)
        sum_grad_ref[pl.ds(k * rows, rows), :] = grad.astype(bf16)
    back = dot_t(sum_grad_ref[...], up_ref[...])
    for k in range(clips):
        mid_grad_ref[k] = (back[k * rows : (k + 1) * rows] * gelu_slope(mid_ref[k])).astype(bf16)


def late_back_kernel(
    width, counts_ref, rz_ref, own_ref, rc_ref, taps_ref, first_ref, down_ref, skip_back_ref, hat_ref, logits_ref,
    first_grad_ref, entry_grad_ref, back_ref, frames, grads,
):
    clips, rows, channels = own_ref.shape
    pitch = 8
    edge = jnp.zeros((pitch, channels), f32)
    lanes = 128

    def clip_step(k, _):
        for s, source in enumerate((rz_ref, own_ref, rc_ref)):
            frames[s, pl.ds(0, pitch), :] = edge
            frames[s, pl.ds(pitch + rows, pitch), :] = edge
            frames[s, pl.ds(pitch, rows), :] = source[k].astype(f32)
        for l in range(channels // lanes):
            cols = pl.ds(l * lanes, lanes)
            grad = conv_rows(
                lambda i: taps_ref[pl.ds(26 - i, 1), cols],
                lambda a, b: frames[a, pl.ds(pitch * b, rows), cols],
                rows,
            )
            grad = grad * frame_mask(counts_ref, k, 0) * gelu_slope(first_ref[k, :, cols])
            grads[k, :, cols] = jnp.where(valid_rows(grad.shape, pitch, width), grad, 0.0)
        return 0

    lax.fori_loop(0, clips, clip_step, 0)
    for k in range(clips):
        first_grad_ref[pl.ds(k * rows, rows), :] = grads[k].astype(bf16)
    entry = dot_t(first_grad_ref[...], down_ref[...]) + skip_back_ref[...]
    one = two = None
    for k in range(clips):
        block = entry[k * rows : (k + 1) * rows]
        entry_grad_ref[k] = block
        masked = block * frame_mask(counts_ref, k, 0)
        a, b = row_sums(masked), row_sums(masked * hat_ref[k])
        one, two = (a, b) if one is None else (one + a, two + b)
    back_ref[0:1] = jnp.sum(one, axis=0, keepdims=True)
    back_ref[1:2] = jnp.sum(two, axis=0, keepdims=True)
    back_ref[2:] = logits_ref[...]


def tap_grads(load, grad_of, steps, rows):
    def step(c, totals):
        grad = grad_of(c)
        sides = (pltpu.roll(grad, rows - 1, 0), grad, pltpu.roll(grad, 1, 0))
        new = []
        for a in range(3):
            for b in range(3):
                block = load(c, a, b)
                for e in range(3):
                    new.append(totals[9 * a + 3 * b + e] + row_sums(block * sides[e]))
        return tuple(new)

    return steps, step


def tap_table(rows_of_tap):
    swapped = (lax.axis_index("space") & 1) == 1
    rows = [jnp.where(swapped, rows_of_tap[(2 - i // 9) * 9 + i % 9], rows_of_tap[i]) for i in range(27)]
    table = jnp.concatenate(rows + [jnp.zeros_like(rows[0])] * 5, axis=0)
    table = jnp.transpose(table)
    return jnp.concatenate([table, jnp.zeros((table.shape[0], 96), f32)], axis=1)


def late_taps_kernel(rz_ref, own_ref, rc_ref, grad_ref, out_ref, frames):
    clips, rows, channels = own_ref.shape
    pitch = 8
    edge = jnp.zeros((pitch, channels), f32)
    lanes = 128
    for s, source in enumerate((rz_ref, own_ref, rc_ref)):
        for k in range(clips):
            frames[s, k, pl.ds(0, pitch), :] = edge
            frames[s, k, pl.ds(pitch + rows, pitch), :] = edge
            frames[s, k, pl.ds(pitch, rows), :] = source[k].astype(f32)
    for l in range(channels // lanes):
        cols = pl.ds(l * lanes, lanes)
        steps, step = tap_grads(
            lambda k, a, b: frames[a, k, pl.ds(pitch * b, rows), cols],
            lambda k: grad_ref[k, :, cols].astype(f32),
            clips,
            rows,
        )
        zero = jnp.zeros((8, lanes), f32)
        totals = lax.fori_loop(0, steps, step, (zero,) * 27)
        rows_of_tap = [jnp.sum(total, axis=0, keepdims=True) for total in totals]
        out_ref[cols, :] = tap_table(rows_of_tap)


def third_taps_kernel(
    orders, parts, rz_ref, oz_ref, oc_ref, rc_ref, gz_ref, gc_ref, up_terms_ref, back_ref, third_ref, pooled_ref,
    taps_ref, *refs,
):
    outs, (frames, grads, total, full) = refs[:-4], refs[-4:]
    k = pl.program_id(0)
    rows, channels = oz_ref.shape[1], oz_ref.shape[2]
    pitch = 16
    chunk = 2 * pitch
    lanes = 128

    @pl.when(k == 0)
    def _():
        clear_edges(frames, pitch, rows)
        total[...] = jnp.zeros_like(total)

    fill_frames(frames, (rz_ref, oz_ref, oc_ref, rc_ref), pitch, rows)
    grads[0] = gz_ref[0].astype(f32)
    grads[1] = gc_ref[0].astype(f32)
    count = rows // chunk
    for l in range(channels // lanes):
        cols = pl.ds(l * lanes, lanes)
        totals = tuple(total[i, :, cols] for i in range(27))
        for slot in range(2):
            steps, step = tap_grads(
                lambda c, a, b: frames[
                    slot + a, pl.ds(pl.multiple_of(c * chunk + pitch * b, pitch), chunk), cols
                ],
                lambda c: grads[slot, pl.ds(pl.multiple_of(c * chunk, chunk), chunk), cols],
                count,
                chunk,
            )
            totals = lax.fori_loop(0, steps, step, totals)
        for i in range(27):
            total[i, :, cols] = totals[i]

    @pl.when(k == pl.num_programs(0) - 1)
    def _():
        wide = up_terms_ref.shape[1]
        late_wide = back_ref.shape[1]
        full[:, pl.ds(0, wide)] = up_terms_ref[...].astype(f32)
        full[:, pl.ds(wide, lanes)] = tap_table([jnp.sum(total[i], axis=0, keepdims=True) for i in range(27)])
        own, own_third, own_taps = late_wide // parts, wide // parts, taps_ref.shape[0] // parts
        deep = channels // parts
        clip, space = lax.axis_index("clip"), lax.axis_index("space")
        pooled = pooled_ref[...]
        pooled = jnp.concatenate(
            [jnp.where(clip == g, pooled, 0.0) for g in range(lax.axis_size("clip"))], axis=0
        )
        for d in range(parts):
            at, third_at = d * own // lanes * lanes, d * own_third // lanes * lanes
            block = jnp.concatenate(
                [
                    back_ref[0:2, pl.ds(at, lanes)],
                    third_ref[0:2, pl.ds(third_at, lanes)],
                    jnp.zeros((4, lanes), f32),
                    pooled[:, at : at + lanes],
                    taps_ref[pl.ds(d * own_taps, own_taps), :],
                ],
                axis=0,
            )
            for i in range(block.shape[0] // deep):
                full[pl.ds(d * deep, deep), pl.ds(wide + (1 + i) * lanes, lanes)] = block[i * deep : (i + 1) * deep]
        if orders is None:
            outs[0][...] = full[...].astype(bf16)
        else:
            clip_count, chips = orders
            keep_ref, send_ref = outs
            for b in range(clip_count):
                for z in range(chips):
                    at = ((clip ^ b) * chips + z) * 2
                    mine = pl.multiple_of((at + (space & 1)) * deep, deep)
                    other = pl.multiple_of((at + 1 - (space & 1)) * deep, deep)
                    keep_ref[b, z] = full[pl.ds(mine, deep), :]
                    send_ref[b, z] = full[pl.ds(other, deep), :].astype(bf16)


def third_grad_kernel(
    width, cells, count, counts_ref, *refs
):
    received, refs = refs[:count], refs[count:]
    (stats_ref, gain_ref, entry_grad_ref, up_ref, act_even_ref, act_sum_ref, gram_up_ref, bias_ref, act_ref, mid_ref,
     gz_ref, gc_ref, terms_ref, logits_ref, back_even, mix, shift, placed) = refs
    k = pl.program_id(0)
    rows = act_ref.shape[2]
    pitch = 16
    chunk = 2 * pitch
    half = pitch // 2

    @pl.when(k == 0)
    def _():
        placed[...] = jnp.zeros_like(placed)
        totals = received_sum(received)
        clips, classes = logits_ref.shape
        wide = totals.shape[1] // 2
        for i in range(clips):
            row = totals[2 + i // 2 : 3 + i // 2, i % 2 * wide : i % 2 * wide + classes]
            logits_ref[pl.ds(i, 1)] = row + bias_ref[...]
        totals = totals[0:2] / cell_total(counts_ref, False, cells)
        center, scale = stats_ref[0:1], stats_ref[1:2]
        lead = gain_ref[...] * scale
        slope = -(lead * scale * totals[1:2])
        offset = -(lead * (totals[0:1] - center * scale * totals[1:2]))
        grad = (entry_grad_ref[...] * lead).astype(bf16)
        back_even[...] = dot_t(grad, up_ref[...])
        product = sum(dot_t(part, up_ref[...]) for part in split(up_ref[...].astype(f32) * slope, 2))
        mix[0], mix[1] = split(product, 2)
        offsets = [part.astype(f32) for part in split(offset, 2)]
        sums = [part.astype(f32) for part in split(act_sum_ref[...], 2)]
        none = jnp.zeros((4, offset.shape[1]), f32)
        offset_rows = jnp.concatenate(offsets + offsets + [none], axis=0).astype(bf16)
        none = jnp.zeros((4, act_sum_ref.shape[1]), f32)
        sum_rows = jnp.concatenate([sums[0], sums[0], sums[1], sums[1], none], axis=0).astype(bf16)
        shift[...] = jnp.sum(dot_t(offset_rows, up_ref[...])[0:2], axis=0, keepdims=True)
        terms = t_dot(act_even_ref[...], grad) + t_dot(sum_rows, offset_rows) + gram_up_ref[...] * slope
        terms_ref[...] = terms.astype(bf16)

    for j in range(rows // chunk):
        at = pl.multiple_of(k * (rows // 4) + half * j, half)
        put_even(placed, frame_of(0) * rows + chunk * j, back_even[pl.ds(at, half), :])
    for slot, out in ((0, gz_ref), (1, gc_ref)):
        mask = frame_mask(counts_ref, k, frame_of(slot))
        act = act_ref[0, slot]
        back = (dot(act, mix[0]) + dot(act, mix[1]) + shift[...]) * mask + get_lanes(placed, slot * rows, rows)
        back = back * gelu_slope(mid_ref[0, slot])
        out[0] = jnp.where(valid_rows(back.shape, pitch, width), back, 0.0).astype(bf16)


def first_grad_kernel(
    width, orders, counts_ref, rz_ref, gz_ref, gc_ref, rc_ref, taps_ref, first_ref, x_ref,
    grad_ref, *refs
):
    outs, (frames, xpad, product) = refs[:-3], refs[-3:]
    k = pl.program_id(0)
    rows = gz_ref.shape[1]
    height, width = x_ref.shape[2], x_ref.shape[3]
    pitch = 16
    chunk = 2 * pitch

    @pl.when(k == 0)
    def _():
        clear_edges(frames, pitch, rows)
        xpad[...] = jnp.zeros_like(xpad)
        product[...] = jnp.zeros_like(product)

    fill_frames(frames, (rz_ref, gz_ref, gc_ref, rc_ref), pitch, rows)
    for slot in range(2):
        frame = frame_of(slot)
        for h in range(height):
            xpad[pl.ds(slot * rows + h * pitch, width), :] = x_ref[0, frame, h]
        scale = frame_mask(counts_ref, k, frame)

        def step(c, _):
            start = pl.multiple_of(c * chunk, chunk)
            grad = conv_rows(
                lambda i: taps_ref[pl.ds(26 - i, 1), :],
                lambda a, b: frames[slot + a, pl.ds(pl.multiple_of(start + pitch * b, pitch), chunk), :],
                chunk,
            )
            grad = grad * scale * gelu_slope(first_ref[0, slot, pl.ds(start, chunk), :])
            grad = jnp.where(valid_rows(grad.shape, pitch, width), grad, 0.0)
            grad_ref[0, pl.ds(pl.multiple_of(slot * rows + start, chunk), chunk), :] = grad.astype(bf16)
            return 0

        lax.fori_loop(0, rows // chunk, step, 0)
    product[...] += t_dot(grad_ref[0], xpad[...])

    @pl.when(k == pl.num_programs(0) - 1)
    def _():
        terms = jnp.transpose(product[...])
        if orders is None:
            outs[0][...] = terms.astype(bf16)
        else:
            clips, chips, block = orders
            xpad_rows = terms.reshape(clips * chips * 2, block, terms.shape[1])
            space, clip = lax.axis_index("space"), lax.axis_index("clip")
            keep_ref, send_ref, full = outs[0], outs[1], outs[2]
            full[...] = xpad_rows
            for b in range(clips):
                for z in range(chips):
                    at = ((clip ^ b) * chips + z) * 2
                    keep_ref[b, z] = full[at + (space & 1)]
                    send_ref[b, z] = full[at + 1 - (space & 1)].astype(bf16)


def pair_sum_kernel(keep_ref, got_ref, keep_terms_ref, got_terms_ref, *out_refs):
    wide, inner = keep_terms_ref.shape[-1], keep_ref.shape[-1]
    deep = keep_terms_ref.shape[-2]
    for b, out_ref in enumerate(out_refs):
        out_ref[:, :, pl.ds(0, wide)] = (keep_terms_ref[b] + got_terms_ref[b].astype(f32)).astype(bf16)
        total = keep_ref[b] + got_ref[b].astype(f32)
        for i in range(keep_ref.shape[-2] // deep):
            out_ref[:, :, pl.ds(wide + i * inner, inner)] = total[:, i * deep : (i + 1) * deep].astype(bf16)


def chip_totals_kernel(count, *refs):
    terms, outs = refs[:count], refs[count:]
    for z, out_ref in enumerate(outs):
        at = (lax.axis_index("space") // 2) ^ z
        total = terms[0][at].astype(f32)
        for term in terms[1:]:
            total = total + term[at].astype(f32)
        out_ref[...] = total.astype(bf16)


def finish_kernel(count, *refs):
    skip, up = refs[:count], refs[count : 2 * count]
    skip_ref, up_ref, fourth_down_ref = refs[2 * count :]

    def total(terms):
        return sum(term[...].astype(f32) for term in terms)

    skip_ref[...] = total(skip)
    both = total(up)
    block, lanes = up_ref.shape[0], fourth_down_ref.shape[1]
    up_ref[...] = both[:block]
    part = both.shape[0] - block
    for i in range(both.shape[1] // lanes):
        fourth_down_ref[pl.ds(i * part, part), :] = both[block:, i * lanes : (i + 1) * lanes]


def terms_kernel(
    count, clips, wide, small_rows, *refs
):
    received, refs = refs[:count], refs[count:]
    (grad_ref, up_ref, depth_ref, gain_ref, shift_ref, late_gain_ref, late_shift_ref, late_depth_ref, head_ref,
     *down_refs) = refs
    lanes = 128
    total = None
    for ref in received:
        for i in range(ref.shape[0]):
            total = ref[i].astype(f32) if total is None else total + ref[i].astype(f32)
    deep = total.shape[0]
    up_ref[...] = total[:, :wide]
    depth_ref[...] = total[:, wide : wide + 27]
    device = lax.axis_index("clip") * lax.axis_size("space") + lax.axis_index("space")
    end = wide + lanes * (1 + small_rows // deep)
    small = jnp.concatenate([total[:, i : i + lanes] for i in range(wide + lanes, end, lanes)], axis=0)

    def own_lanes(values, width):
        moved = pltpu.roll(values, (lanes - device * width % lanes) % lanes, 1)
        return moved[:, :width]

    late = own_lanes(small, late_gain_ref.shape[1])
    third = own_lanes(small, gain_ref.shape[1])
    late_gain_ref[...] = late[1:2]
    late_shift_ref[...] = late[0:1]
    gain_ref[...] = third[3:4]
    shift_ref[...] = third[2:3]
    everyone = clips * lax.axis_size("clip")
    late_depth_ref[...] = small[8 + everyone :, :27]
    pooled = late[8 : 8 + everyone].astype(bf16)
    head_ref[...] = sum(t_dot(pooled, part) for part in split(grad_ref[...], 3))
    for down_ref in down_refs:
        inner = down_ref.shape[1]
        for i in range(down_ref.shape[0] // deep):
            down_ref[pl.ds(i * deep, deep), :] = total[:, end + i * inner : end + (i + 1) * inner]


def clip_grad_kernel(grad_ref, down_ref, entry_grad_ref, out_ref, wide):
    _, _, height, width, _ = out_ref.shape
    pitch = 16
    half = pitch // 2
    rows = height * pitch
    for slot in range(2):
        put_lanes(wide, slot * rows, dot_t(grad_ref[0, pl.ds(slot * rows, rows), :], down_ref[...]))
    for j in range(height // 2):
        at = frame_of(0) * rows + 2 * pitch * j
        put_even(wide, at, get_even(wide, at, half) + entry_grad_ref[0, pl.ds(half * j, half), :])
    for slot in range(2):
        frame = frame_of(slot)
        for h in range(height):
            out_ref[0, frame, h] = get_lanes(wide, slot * rows + h * pitch, width).astype(bf16)


kernel_micros = {
    "first": 5.3, "mid_own": 5.0, "mid": 8.6, "entry": 3.4, "late_mid": 4.7, "post": 6.0, "skip_sums": 7.0,
    "sum_grad": 4.6, "late_taps": 3.6, "late_back": 5.0, "up_down_sums": 5.5, "third_grad": 6.7, "third_taps": 7.7,
    "up_down_total": 2.3, "skip_total": 3.0, "skip_phase": 1.0, "up_down_phase": 1.0, "finish": 2.0, "terms": 1.5, "taps": 0.6, "pooled_grad": 1.5, "head": 1.0, "add": 0.6, "skipped": 2.5, "first_grad": 10.7, "pair_sum": 1.9, "clip_sum": 1.6, "clip_grad": 5.5,
}
smem = pl.BlockSpec(memory_space=pltpu.SMEM)


def whole(shape):
    return pl.BlockSpec(shape, lambda k: (0,) * len(shape))


def by_clip(shape):
    return pl.BlockSpec((1,) + shape[1:], lambda k: (k,) + (0,) * (len(shape) - 1))


def cost(micros):
    return pl.CostEstimate(flops=0, bytes_accessed=int(micros * 3.4e6), transcendentals=0)


def call(kernel, name, inputs, outputs, scratch, clips=None, limit=LIMIT):
    if clips is None:
        def spec(kind, shape):
            return smem if kind == "s" else pl.BlockSpec(memory_space=pltpu.VMEM)
    else:
        def spec(kind, shape):
            return smem if kind == "s" else whole(shape) if kind == "w" else by_clip(shape)
    options = {} if clips is None else {"grid": (clips,)}
    return pl.pallas_call(
        kernel,
        name=name,
        out_shape=[jax.ShapeDtypeStruct(s, d) for s, d, _ in outputs],
        in_specs=[spec(kind, a.shape) for a, kind in inputs],
        out_specs=[spec(kind, s) for s, _, kind in outputs],
        scratch_shapes=scratch,
        compiler_params=pltpu.CompilerParams(vmem_limit_bytes=limit * mib),
        cost_estimate=cost(kernel_micros[name]),
        **options,
    )(*[a for a, _ in inputs])


def group_parts(values):
    size = lax.axis_size("space")
    if size != 8:
        copies = jnp.broadcast_to(values[None], (size,) + values.shape)
        return [lax.all_to_all(copies, "space", split_axis=0, concat_axis=0, tiled=True)]
    (pair,) = call(add_kernel, "add", [(values, "w"), (core_swap(values), "w")], [(values.shape, f32, "w")], [])
    return [part[None] for part in over_chips([pair] * 4)]


def w(arrays):
    return [(array, "w") for array in arrays]


def swap_neighbours(to_z, to_core):
    size = lax.axis_size("space")
    core = [(i, i ^ 1) for i in range(size)]
    z = [(i, j) for m in range(1, size - 1, 2) for i, j in ((m, m + 1), (m + 1, m))]
    return lax.ppermute(to_z, "space", z), lax.ppermute(to_core, "space", core)


def reduce_rows(term):
    return add_rows(send_rows(term))


def add_rows(received):
    return jnp.sum(received.astype(f32), axis=0)


def send_rows(term):
    parts = lax.axis_size("clip") * lax.axis_size("space")
    pieces = term.astype(bf16).reshape((parts, term.shape[0] // parts) + term.shape[1:])
    return lax.all_to_all(pieces, ("clip", "space"), split_axis=0, concat_axis=0, tiled=True)


def core_swap(values):
    return lax.ppermute(values, "space", [(i, i ^ 1) for i in range(lax.axis_size("space"))])


def own_rows(left_ref, out, starts):
    out[0] = jnp.transpose(left_ref[...])
    block = out.shape[1] // 2 // len(starts)
    for j, start in enumerate(starts):
        out[1, pl.ds(j * block, block), :] = out[0, pl.ds(pl.multiple_of(start * block, block), block), :]


def own_blocks(orders):
    space, clip = lax.axis_index("space"), lax.axis_index("clip")
    clips, chips = orders
    return [((clip ^ b) * chips + z) * 2 + (space & 1) for b in range(clips) for z in range(chips)]


def place(outs, chips, j, values):
    b, z = j // chips, j % chips
    if z < chips // 2:
        outs[b % 2][b // 2, z] = values.astype(bf16)
    else:
        outs[2 + b // 2][b % 2, z - chips // 2] = values.astype(bf16)


def first_phase(pieces):
    keep_low, send_low, keep_high, send_high = pieces
    return [keep_low, clip_swap(send_low, 1), keep_high, clip_swap(send_high, 2)]


def clip_swap(values, bit):
    return lax.ppermute(values, "clip", [(i, i ^ bit) for i in range(lax.axis_size("clip"))])


def phase_kernel(keep_low_ref, got_low_ref, keep_high_ref, got_high_ref, low_ref, low_send_ref, high_ref, high_send_ref):
    for keep, got, out, send in (
        (keep_low_ref, got_low_ref, low_ref, low_send_ref), (keep_high_ref, got_high_ref, high_ref, high_send_ref)
    ):
        out[...] = (keep[0].astype(f32) + got[0].astype(f32)).astype(bf16)
        send[...] = (keep[1].astype(f32) + got[1].astype(f32)).astype(bf16)


def second_phase(name, pieces):
    shape = pieces[0].shape[1:]
    low, low_send, high, high_send = call(phase_kernel, name, w(pieces), [(shape, bf16, "w")] * 4, [])
    return [low, clip_swap(low_send, 2), high, clip_swap(high_send, 1)]


def halves_total_kernel(low_ref, got_low_ref, high_ref, got_high_ref, *outs):
    half = low_ref.shape[0]
    for z, out_ref in enumerate(outs):
        at = (lax.axis_index("space") // 2) ^ z
        low = low_ref[at % half].astype(f32) + got_low_ref[at % half].astype(f32)
        high = high_ref[at % half].astype(f32) + got_high_ref[at % half].astype(f32)
        out_ref[...] = jnp.where(at < half, low, high).astype(bf16)


def skip_kernel(
    orders, left_ref, left_other_ref, right_ref, right_other_ref, weight_ref, back_ref, *refs
):
    clips, chips = orders
    outs, (left, left_other) = refs[:4], refs[4:]

    @pl.when(pl.program_id(0) == 0)
    def _():
        own_rows(left_ref, left, own_blocks(orders))
        own_rows(left_other_ref, left_other, own_blocks(orders))
        back_ref[...] = jnp.zeros_like(back_ref)

    half = left.shape[1] // 2
    total = dot(left[1, pl.ds(0, half)], right_ref[...]) + dot(left_other[1, pl.ds(0, half)], right_other_ref[...])
    block = half // (clips * chips)
    for j in range(clips * chips):
        place(outs, chips, j, total[j * block : (j + 1) * block])
    back_ref[...] += dot_t(right_ref[...], weight_ref[...])


def skip_sums(left, left_other, right, right_other, weight, parts, orders):
    block = left.shape[1] // parts
    wide = right.shape[1]
    lanes = 512
    rows, deep = left.shape
    return pl.pallas_call(
        functools.partial(skip_kernel, orders),
        name="skip_sums",
        grid=(wide // lanes,),
        out_shape=[
            jax.ShapeDtypeStruct((rows, deep), f32),
            *[jax.ShapeDtypeStruct((2, orders[1] // 2, block, wide), bf16)] * 4,
        ],
        in_specs=[pl.BlockSpec((rows, deep), lambda n: (0, 0))] * 2
        + [pl.BlockSpec((rows, lanes), lambda n: (0, n))] * 2
        + [pl.BlockSpec((deep, lanes), lambda n: (0, n))],
        out_specs=[
            pl.BlockSpec((rows, deep), lambda n: (0, 0)),
            *[pl.BlockSpec((2, orders[1] // 2, block, lanes), lambda n: (0, 0, 0, n))] * 4,
        ],
        scratch_shapes=[pltpu.VMEM((2, deep, rows), bf16)] * 2,
        compiler_params=pltpu.CompilerParams(vmem_limit_bytes=LIMIT * mib),
        cost_estimate=cost(kernel_micros["skip_sums"]),
    )(left, left_other, right, right_other, weight)


def products_kernel(
    orders, act_ref, act_other_ref, entry_ref, entry_other_ref, first_ref, first_other_ref, sum_ref, sum_other_ref,
    *refs
):
    clips, chips = orders
    outs, (act, act_other, entry, entry_other, down) = refs[:4], refs[4:]
    n = pl.program_id(0)

    @pl.when(n == 0)
    def _():
        blocks = own_blocks(orders)
        own_rows(act_ref, act, blocks)
        own_rows(act_other_ref, act_other, blocks)
        own_rows(entry_ref, entry, blocks)
        own_rows(entry_other_ref, entry_other, blocks)
        half = entry.shape[1] // 2
        down[...] = (
            dot(entry[1, pl.ds(0, half)], first_ref[...]) + dot(entry_other[1, pl.ds(0, half)], first_other_ref[...])
        ).reshape(down.shape)

    half = act.shape[1] // 2
    up = dot(act[1, pl.ds(0, half)], sum_ref[...]) + dot(act_other[1, pl.ds(0, half)], sum_other_ref[...])
    block = half // (clips * chips)
    part = outs[0].shape[2] - block
    for j in range(clips * chips):
        under = down[j, pl.ds(pl.multiple_of(n * part, part), part), :]
        place(outs, chips, j, jnp.concatenate([up[j * block : (j + 1) * block], under], axis=0))


def up_down_sums(act, act_other, entry, entry_other, first, first_other, sums, sums_other, parts, orders):
    rows, deep = entry.shape
    inner, wide = act.shape[1], sums.shape[1]
    lanes = inner
    clips, chips = orders
    up_block, down_block = inner // parts, deep // parts
    block = up_block + down_block * inner // wide
    same = lambda n: (0, 0)
    return pl.pallas_call(
        functools.partial(products_kernel, orders),
        name="up_down_sums",
        grid=(wide // lanes,),
        out_shape=[jax.ShapeDtypeStruct((2, chips // 2, block, wide), bf16)] * 4,
        in_specs=[pl.BlockSpec((rows, inner), same)] * 2
        + [pl.BlockSpec((rows, deep), same)] * 2
        + [pl.BlockSpec((rows, inner), same)] * 2
        + [pl.BlockSpec((rows, lanes), lambda n: (0, n))] * 2,
        out_specs=[pl.BlockSpec((2, chips // 2, block, lanes), lambda n: (0, 0, 0, n))] * 4,
        scratch_shapes=[pltpu.VMEM((2, inner, rows), bf16)] * 2
        + [pltpu.VMEM((2, deep, rows), bf16)] * 2
        + [pltpu.VMEM((clips * chips, down_block, inner), f32)],
        compiler_params=pltpu.CompilerParams(vmem_limit_bytes=LIMIT * mib),
        cost_estimate=cost(kernel_micros["up_down_sums"]),
    )(act, act_other, entry, entry_other, first, first_other, sums, sums_other)


def over_clip(pieces):
    size = len(pieces)
    return [pieces[0]] + [lax.ppermute(pieces[b], "clip", [(i, i ^ b) for i in range(size)]) for b in range(1, size)]


def over_chips(pieces):
    size = len(pieces)
    return [pieces[0]] + [
        lax.ppermute(pieces[z], "space", [(i, i ^ (2 * z)) for i in range(2 * size)]) for z in range(1, size)
    ]


def skipped_sums(entry, weight):
    rows, deep = entry.shape
    wide = weight.shape[1]
    lanes = 512
    return pl.pallas_call(
        skipped_kernel,
        name="skipped",
        grid=(wide // lanes,),
        out_shape=jax.ShapeDtypeStruct((rows, wide), bf16),
        in_specs=[pl.BlockSpec((rows, deep), lambda n: (0, 0)), pl.BlockSpec((deep, lanes), lambda n: (0, n))],
        out_specs=pl.BlockSpec((rows, lanes), lambda n: (0, n)),
        compiler_params=pltpu.CompilerParams(vmem_limit_bytes=LIMIT * mib),
        cost_estimate=cost(kernel_micros["skipped"]),
    )(entry, weight)


def after(values, token):
    return lax.optimization_barrier((values, token))[0]


def per_device(
    clip_input, frame_counts, third_down, third_depth, third_up, third_gain, third_shift,
    fourth_down, fourth_skip, fourth_depth, fourth_up, fourth_gain, fourth_shift,
    classifier, class_bias, logit_grad,
):
    clips, frames, height, width, channels = clip_input.shape
    inner = third_down.shape[1]
    late_inner = fourth_down.shape[1]
    late_wide = fourth_up.shape[1]
    half_width = width // 2
    rows = height * 16
    late_rows = height // 2 * 8
    late_all = clips * late_rows
    cells = height * width
    late_cells = (height // 2) * half_width
    parts = lax.axis_size("clip") * lax.axis_size("space")
    clip_axis, chips = lax.axis_size("clip"), lax.axis_size("space") // 2
    by_pairs = clip_axis == 4 and chips == 4 and channels // parts % 32 == 0 and late_inner // parts % 16 == 0
    orders = (clip_axis, chips) if by_pairs else None
    third_gain, third_shift = third_gain[None], third_shift[None]
    fourth_gain, fourth_shift = fourth_gain[None], fourth_shift[None]
    head = jnp.transpose(classifier)

    first, act_z, act_c, even_x = call(
        first_kernel, "first",
        [(frame_counts, "s"), (clip_input, "c"), (third_down, "w")],
        [
            ((clips, 2, rows, inner), f32, "c"),
            ((clips, rows, inner), bf16, "c"),
            ((clips, rows, inner), bf16, "c"),
            ((clips, late_rows, channels), f32, "c"),
        ],
        [pltpu.VMEM((rows, channels), bf16), pltpu.VMEM((channels // 128, 16, 128), f32)],
        clips=clips,
    )
    got_z, got_c = swap_neighbours(act_z, act_c)
    third_taps, late_taps = call(
        taps_kernel, "taps", w([jnp.transpose(third_depth), jnp.transpose(fourth_depth)]),
        [((27, inner), f32, "w"), ((27, late_inner), f32, "w")], [],
    )
    (mid_part,) = call(
        mid_own_kernel, "mid_own",
        [(act_z, "c"), (act_c, "c"), (third_taps, "w")],
        [((clips, 2, rows, inner), f32, "c")],
        [pltpu.VMEM((2, rows + 32, inner), f32)],
        clips=clips,
    )
    mid, mid_act, act_even, even_sum, moments, gram_up, act_sum = call(
        functools.partial(mid_kernel, width), "mid",
        [(frame_counts, "s"), (got_z, "c"), (got_c, "c"), (mid_part, "c"), (third_taps, "w"), (third_up, "w")],
        [
            ((clips, 2, rows, inner), f32, "c"),
            ((clips, 2, rows, inner), bf16, "c"),
            ((late_all, inner), bf16, "w"),
            ((late_all, channels), f32, "w"),
            ((2, channels), f32, "w"),
            ((inner, channels), f32, "w"),
            ((1, inner), f32, "w"),
        ],
        [
            pltpu.VMEM((2, rows + 32, inner), f32),
            pltpu.VMEM((inner // 128, 2 * rows, 128), f32),
            pltpu.VMEM((late_all, inner), f32),
            pltpu.VMEM((inner, inner), f32),
            pltpu.VMEM((8, inner), f32),
        ],
        clips=clips,
    )
    even_sum = even_sum.reshape(clips, late_rows, channels)
    moments = group_parts(moments)
    stats, even_hat, entry, late_first, late_act = call(
        functools.partial(entry_kernel, half_width, cells, len(moments)), "entry",
        [(frame_counts, "s"), *w(moments), (even_x, "w"), (even_sum, "w"),
         (third_gain, "w"), (third_shift, "w"), (fourth_down, "w")],
        [
            ((2, channels), f32, "w"),
            ((clips, late_rows, channels), f32, "w"),
            ((late_all, channels), bf16, "w"),
            ((late_all, late_inner), f32, "w"),
            ((clips, late_rows, late_inner), bf16, "w"),
        ],
        [],
    )
    late_first = late_first.reshape(clips, late_rows, late_inner)
    late_z, late_c = swap_neighbours(late_act, late_act)
    (pooled_grad,) = call(pooled_grad_kernel, "pooled_grad", w([logit_grad, head]), [((clips, late_wide), f32, "w")], [])
    skipped = skipped_sums(entry, fourth_skip).reshape(clips, late_rows, late_wide)
    late_mid, late_mid_act, late_sum, late_moments = call(
        functools.partial(late_kernel, half_width), "late_mid",
        [(frame_counts, "s"), (late_z, "w"), (late_act, "w"), (late_c, "w"), (late_taps, "w"), (fourth_up, "w")],
        [
            ((clips, late_rows, late_inner), f32, "w"),
            ((late_all, late_inner), bf16, "w"),
            ((late_all, late_wide), bf16, "w"),
            ((2, late_wide), f32, "w"),
        ],
        [
            pltpu.VMEM((3, late_rows + 16, late_inner), f32),
            pltpu.VMEM((clips, late_rows, late_inner), f32),
        ],
    )
    late_sum = late_sum.reshape(clips, late_rows, late_wide)
    late_moments = group_parts(late_moments)
    late_stats, late_back, pooled, pre_grad, skip_grad = call(
        functools.partial(post_kernel, half_width, late_cells, len(late_moments)), "post",
        [(frame_counts, "s"), *w(late_moments), (late_sum, "w"), (skipped, "w"),
         (fourth_gain, "w"), (fourth_shift, "w"), (pooled_grad, "w")],
        [
            ((2, late_wide), f32, "w"),
            ((2, late_wide), f32, "w"),
            ((clips, late_wide), f32, "w"),
            ((clips, late_rows, late_wide), f32, "w"),
            ((clips, late_rows, late_wide), bf16, "w"),
        ],
        [],
    )
    received = group_parts(late_back)
    skip_rows = skip_grad.reshape(late_all, late_wide)
    if by_pairs:
        entry_other = core_swap(entry)
        skip_back, *skip_pieces = skip_sums(
            entry, entry_other, skip_rows, core_swap(after(skip_rows, received[0])), fourth_skip, parts, (clip_axis, chips)
        )
    else:
        skip_back = dot_t(skip_rows, fourth_skip)
        fourth_skip_grad = reduce_rows(t_dot(entry, skip_rows))
    late_stats = after(late_stats, skip_back)
    late_sum_grad, late_mid_grad = call(
        functools.partial(sum_grad_kernel, half_width, late_cells, len(received)), "sum_grad",
        [(frame_counts, "s"), *w(received), (late_stats, "w"), (late_sum, "w"), (pre_grad, "w"),
         (fourth_gain, "w"), (fourth_up, "w"), (late_mid, "w")],
        [
            ((late_all, late_wide), bf16, "w"),
            ((clips, late_rows, late_inner), bf16, "w"),
        ],
        [],
    )
    late_gz, late_gc = swap_neighbours(late_mid_grad, late_mid_grad)
    if by_pairs:
        skip_pieces = first_phase(after(skip_pieces, late_mid_grad))
    logit_terms, bias_grad = call(
        head_kernel, "head", w([after(pooled, late_mid_grad), head, logit_grad]),
        [((clips // 2, channels), f32, "w"), ((1, logit_grad.shape[1]), f32, "w")], [],
    )
    late_first = after(late_first, logit_terms)
    (late_taps_table,) = call(
        late_taps_kernel, "late_taps",
        [(late_z, "w"), (late_act, "w"), (late_c, "w"), (late_mid_grad, "w")],
        [((late_inner, 128), f32, "w")],
        [pltpu.VMEM((3, clips, late_rows + 16, late_inner), f32)],
    )
    late_first = after(late_first, late_taps_table)
    late_first_grad, entry_grad, third_back = call(
        functools.partial(late_back_kernel, half_width), "late_back",
        [(frame_counts, "s"), (late_gz, "w"), (late_mid_grad, "w"), (late_gc, "w"), (late_taps, "w"),
         (late_first, "w"), (fourth_down, "w"), (skip_back, "w"), (even_hat, "w"), (logit_terms, "w")],
        [
            ((late_all, late_inner), bf16, "w"),
            ((clips, late_rows, channels), f32, "w"),
            ((2 + clips // 2, channels), f32, "w"),
        ],
        [
            pltpu.VMEM((3, late_rows + 16, late_inner), f32),
            pltpu.VMEM((clips, late_rows, late_inner), f32),
        ],
    )
    received = group_parts(third_back)
    if by_pairs:
        up_pieces = up_down_sums(
            late_mid_act, core_swap(late_mid_act), entry, entry_other, late_first_grad, core_swap(late_first_grad),
            late_sum_grad, core_swap(late_sum_grad), parts, (clip_axis, chips),
        )
        skip_pieces = second_phase("skip_phase", after(skip_pieces, up_pieces[0]))
        stats = after(stats, skip_pieces[0])
    else:
        fourth_up_grad = reduce_rows(t_dot(late_mid_act, late_sum_grad))
        fourth_down_grad = reduce_rows(t_dot(entry, late_first_grad))
    grad_z, grad_c, up_terms, logits = call(
        functools.partial(third_grad_kernel, width, cells, len(received)), "third_grad",
        [(frame_counts, "s"), *w(received), (stats, "w"), (third_gain, "w"),
         (entry_grad.reshape(late_all, channels), "w"), (third_up, "w"), (act_even, "w"), (act_sum, "w"),
         (gram_up, "w"), (class_bias[None], "w"), (mid_act, "c"), (mid, "c")],
        [
            ((clips, rows, inner), bf16, "c"),
            ((clips, rows, inner), bf16, "c"),
            ((inner, channels), bf16, "w"),
            ((clips, logit_grad.shape[1]), f32, "w"),
        ],
        [
            pltpu.VMEM((late_all, inner), f32),
            pltpu.VMEM((2, inner, inner), bf16),
            pltpu.VMEM((1, inner), f32),
            pltpu.VMEM((inner // 128, 2 * rows, 128), f32),
        ],
        clips=clips,
    )
    third_gz, third_gc = swap_neighbours(grad_z, grad_c)
    small_rows = 8 + clips * clip_axis + late_inner // parts
    deep = inner // parts
    extra = 128 * (1 + small_rows // deep)
    if by_pairs:
        term_outputs = [
            ((clip_axis, chips, deep, channels + extra), f32, "w"),
            ((clip_axis, chips, deep, channels + extra), bf16, "w"),
        ]
    else:
        term_outputs = [((inner, channels + extra), bf16, "w")]
    third_terms = call(
        functools.partial(third_taps_kernel, orders, parts), "third_taps",
        [(got_z, "c"), (act_z, "c"), (act_c, "c"), (got_c, "c"), (grad_z, "c"), (grad_c, "c"),
         (up_terms, "w"), (late_back, "w"), (third_back, "w"), (pooled, "w"), (late_taps_table, "w")],
        term_outputs,
        [
            pltpu.VMEM((4, rows + 32, inner), f32),
            pltpu.VMEM((2, rows, inner), f32),
            pltpu.VMEM((27, 8, inner), f32),
            pltpu.VMEM((inner, channels + extra), f32),
        ],
        clips=clips,
    )
    first = after(first, third_terms[0])
    if by_pairs:
        skip_pieces = call(
            halves_total_kernel, "skip_total", w(after(skip_pieces, third_terms[0])),
            [(skip_pieces[0].shape[1:], bf16, "w")] * chips, [],
        )
        first = after(first, skip_pieces[0])
        up_pieces = first_phase(after(up_pieces, third_terms[0]))
        skip_pieces = over_chips(after(skip_pieces, third_terms[0]))
    block = channels // parts
    if by_pairs:
        down_outputs = [
            ((clip_axis, chips, block, inner), f32, "w"),
            ((clip_axis, chips, block, inner), bf16, "w"),
        ]
        down_scratch = [pltpu.VMEM((parts, block, inner), f32)]
    else:
        down_outputs, down_scratch = [((channels, inner), bf16, "w")], []
    first_grad, *down_terms = call(
        functools.partial(first_grad_kernel, width, (clip_axis, chips, block) if by_pairs else None), "first_grad",
        [(frame_counts, "s"), (third_gz, "c"), (grad_z, "c"), (grad_c, "c"), (third_gc, "c"),
         (third_taps, "w"), (first, "c"), (clip_input, "c")],
        [((clips, 2 * rows, inner), bf16, "c"), *down_outputs],
        [
            *down_scratch,
            pltpu.VMEM((4, rows + 32, inner), f32),
            pltpu.VMEM((2 * rows, channels), bf16),
            pltpu.VMEM((inner, channels), f32),
        ],
        clips=clips,
    )
    (clip_grad,) = call(
        clip_grad_kernel, "clip_grad",
        [(first_grad, "c"), (third_down, "w"), (entry_grad, "c")],
        [(clip_input.shape, bf16, "c")],
        [pltpu.VMEM((channels // 128, 2 * rows, 128), f32)],
        clips=clips,
    )
    if by_pairs:
        keep, send = down_terms
        keep_terms, send_terms = third_terms
        up_pieces = second_phase("up_down_phase", after(up_pieces, first_grad))
        clip_parts = call(
            pair_sum_kernel, "pair_sum",
            w([after(keep, clip_grad), core_swap(send), keep_terms, core_swap(after(send_terms, third_gz))]),
            [((chips, deep, channels + extra + block // deep * inner), bf16, "w")] * clip_axis,
            [],
        )
        up_pieces = call(
            halves_total_kernel, "up_down_total", w(after(up_pieces, (clip_parts[0], skip_pieces))),
            [(up_pieces[0].shape[1:], bf16, "w")] * chips, [],
        )
        clip_parts = over_clip(clip_parts)
        up_pieces = over_chips(up_pieces)
        chip_parts = call(
            functools.partial(chip_totals_kernel, clip_axis), "clip_sum", w(after(clip_parts, up_pieces[0])),
            [(clip_parts[0].shape[1:], bf16, "w")] * chips, [],
        )
        third_terms = [part[None] for part in over_chips(chip_parts)]
        up_block = late_inner // parts
        fourth_skip_grad, fourth_up_grad, fourth_down_grad = call(
            functools.partial(finish_kernel, chips), "finish", w(skip_pieces + up_pieces),
            [
                ((block, late_wide), f32, "w"),
                ((up_block, late_wide), f32, "w"),
                ((block, late_inner), f32, "w"),
            ],
            [],
        )
    else:
        third_down_grad = add_rows(send_rows(down_terms[0]))
        third_terms = [send_rows(third_terms[0])]
    own, own_third, own_taps = late_wide // parts, channels // parts, late_inner // parts
    third_up_grad, third_depth_grad, gain, shift, late_gain, late_shift, fourth_depth_grad, classifier_grad, *down = call(
        functools.partial(terms_kernel, len(third_terms), clips, channels, small_rows), "terms",
        w(third_terms + [logit_grad]),
        [
            ((deep, channels), f32, "w"),
            ((deep, 27), f32, "w"),
            ((1, own_third), f32, "w"),
            ((1, own_third), f32, "w"),
            ((1, own), f32, "w"),
            ((1, own), f32, "w"),
            ((own_taps, 27), f32, "w"),
            ((own, logit_grad.shape[1]), f32, "w"),
            *([((block, inner), f32, "w")] if by_pairs else []),
        ],
        [],
    )
    if by_pairs:
        (third_down_grad,) = down
    return (
        logits,
        clip_grad,
        third_down_grad,
        third_depth_grad,
        third_up_grad,
        gain.reshape(-1),
        shift.reshape(-1),
        fourth_down_grad,
        fourth_skip_grad,
        fourth_depth_grad,
        fourth_up_grad,
        late_gain.reshape(-1),
        late_shift.reshape(-1),
        classifier_grad,
        bias_grad.reshape(-1),
    )


def solution(mesh):
    both = ("clip", "space")
    return jax.shard_map(
        per_device,
        mesh=mesh,
        in_specs=(P("clip", "space", None, None, None), P("clip")) + (P(),) * 14,
        out_specs=(
            P("clip", None),
            P("clip", "space", None, None, None),
            P(both, None),
            P(both, None),
            P(both, None),
            P(both),
            P(both),
            P(both, None),
            P(both, None),
            P(both, None),
            P(both, None),
            P(both),
            P(both),
            P(both, None),
            P(),
        ),
        check_vma=False,
    )
```

```python
import functools
import math

import jax
import jax.numpy as jnp
from jax import lax
from jax.experimental import pallas as pl
from jax.experimental.pallas import tpu as pltpu
from jax.sharding import PartitionSpec as P

eps = 1e-05
f32 = jnp.float32
bf16 = jnp.bfloat16
mib = 1 << 20
LIMIT = 16


def gelu_terms(x):
    c = math.sqrt(2.0 / math.pi)
    x2 = x * x
    t = jnp.tanh(x * (c + (c * 0.044715) * x2))
    return x2, t


def gelu(x):
    _, t = gelu_terms(x)
    return x * (0.5 + 0.5 * t)


def gelu_slope(x):
    c = math.sqrt(2.0 / math.pi)
    x2, t = gelu_terms(x)
    return 0.5 + 0.5 * t + (0.5 * x) * ((1.0 - t * t) * (c + (3.0 * c * 0.044715) * x2))


def gelu_both(x):
    c = math.sqrt(2.0 / math.pi)
    x2, t = gelu_terms(x)
    cdf = 0.5 + 0.5 * t
    return x * cdf, cdf + (0.5 * x) * ((1.0 - t * t) * (c + (3.0 * c * 0.044715) * x2))


def valid_rows(shape, group, used):
    return lax.broadcasted_iota(jnp.int32, shape, 0) % group < used


def row_sums(values):
    rows, width = values.shape
    return jnp.sum(values.reshape(rows // 8, 8, width), axis=0)


def dot(left, right):
    return jnp.dot(left, right, preferred_element_type=f32)


def dot_t(left, right):
    return lax.dot_general(left, right, (((1,), (1,)), ((), ())), preferred_element_type=f32)


def t_dot(left, right):
    return lax.dot_general(left, right, (((0,), (0,)), ((), ())), preferred_element_type=f32)


def put_lanes(ref, start, values):
    rows, channels = values.shape
    for j in range(channels // 128):
        ref[j, pl.ds(start, rows), :] = values[:, 128 * j : 128 * (j + 1)]


def get_lanes(ref, start, rows):
    return jnp.concatenate([ref[j, pl.ds(start, rows), :] for j in range(ref.shape[0])], axis=1)


def get_even(ref, start, count):
    return jnp.concatenate(
        [ref[j, pl.ds(start, count, stride=2), :] for j in range(ref.shape[0])], axis=1
    )


def put_even(ref, start, values):
    rows, channels = values.shape
    for j in range(channels // 128):
        ref[j, pl.ds(start, rows, stride=2), :] = values[:, 128 * j : 128 * (j + 1)]


def conv_rows(taps, load, rows, times=(0, 1, 2)):
    sums = [None, None, None]
    for a in times:
        for b in range(3):
            block = load(a, b)
            for e in range(3):
                term = block * taps(9 * a + 3 * b + e)
                sums[e] = term if sums[e] is None else sums[e] + term
    return pltpu.roll(sums[0], 1, 0) + sums[1] + pltpu.roll(sums[2], rows - 1, 0)


def split(values, count):
    parts = []
    for _ in range(count):
        parts.append(values.astype(bf16))
        values = values - parts[-1].astype(f32)
    return parts


def frame_of(slot):
    parity = lax.axis_index("space") & 1
    return parity if slot == 0 else 1 - parity


def frame_mask(counts_ref, k, frame):
    return jnp.where(2 * lax.axis_index("space") + frame < counts_ref[k], 1.0, 0.0).astype(f32)


def cell_total(counts_ref, late, cells):
    total = 0
    for k in range(counts_ref.shape[0]):
        total += (counts_ref[k] + 1) // 2 if late else counts_ref[k]
    return (total * cells).astype(f32)


def received_sum(refs):
    total = None
    for ref in refs:
        for i in range(ref.shape[0]):
            total = ref[i] if total is None else total + ref[i]
    return total


def taps_kernel(third_ref, fourth_ref, third_out, fourth_out):
    swapped = (lax.axis_index("space") & 1) == 1
    for source, out in ((third_ref, third_out), (fourth_ref, fourth_out)):
        for a in range(3):
            here, there = source[pl.ds(9 * a, 9), :], source[pl.ds(9 * (2 - a), 9), :]
            out[pl.ds(9 * a, 9), :] = jnp.where(swapped, there, here)


def pooled_grad_kernel(grad_ref, head_ref, out_ref):
    full = sum(dot(part, head_ref[...]) for part in split(grad_ref[...], 3))
    clips = out_ref.shape[0]
    clip = lax.axis_index("clip")
    own = full[:clips]
    for g in range(1, full.shape[0] // clips):
        own = jnp.where(clip == g, full[g * clips : (g + 1) * clips], own)
    out_ref[...] = own.astype(bf16).astype(f32)


def head_kernel(pooled_ref, head_ref, grad_ref, logits_ref, bias_grad_ref):
    terms = sum(dot_t(part, head_ref[...]) for part in split(pooled_ref[...], 3))
    clips, classes = terms.shape
    wide = logits_ref.shape[1] // 2
    logits_ref[...] = jnp.zeros_like(logits_ref)
    for k in range(clips):
        logits_ref[pl.ds(k // 2, 1), pl.ds(k % 2 * wide, classes)] = terms[k : k + 1]
    bias_grad_ref[...] = jnp.sum(grad_ref[...], axis=0, keepdims=True)


def add_kernel(one_ref, two_ref, out_ref):
    out_ref[...] = one_ref[...] + two_ref[...]


def skipped_kernel(entry_ref, weight_ref, out_ref):
    out_ref[...] = dot(entry_ref[...], weight_ref[...]).astype(bf16)


def first_kernel(counts_ref, x_ref, w_ref, first_ref, actz_ref, actc_ref, even_ref, xpad, xe):
    k = pl.program_id(0)
    _, _, height, width, _ = x_ref.shape
    pitch = xe.shape[1]

    @pl.when(k == 0)
    def _():
        xpad[...] = jnp.zeros_like(xpad)
        xe[...] = jnp.zeros_like(xe)

    for slot, act_ref in ((0, actz_ref), (1, actc_ref)):
        frame = frame_of(slot)
        for h in range(height):
            xpad[pl.ds(h * pitch, width), :] = x_ref[0, frame, h]
        first = dot(xpad[...], w_ref[...])
        first_ref[0, slot] = first
        act_ref[0] = (gelu(first) * frame_mask(counts_ref, k, frame)).astype(bf16)
    for h in range(0, height, 2):
        put_lanes(xe, 0, x_ref[0, 0, h].astype(f32))
        even_ref[0, pl.ds(h // 2 * (pitch // 2), pitch // 2), :] = get_even(xe, 0, pitch // 2)


def fill_frames(frames, sources, pad, rows):
    for s, source in enumerate(sources):
        frames[s, pl.ds(pad, rows), :] = source[0].astype(f32)


def clear_edges(frames, pad, rows):
    edge = jnp.zeros((pad, frames.shape[-1]), f32)
    for s in range(frames.shape[0]):
        frames[s, pl.ds(0, pad), :] = edge
        frames[s, pl.ds(pad + rows, pad), :] = edge


def mid_own_kernel(oz_ref, oc_ref, taps_ref, part_ref, frames):
    rows = oz_ref.shape[1]
    pitch = 16
    chunk = 2 * pitch

    @pl.when(pl.program_id(0) == 0)
    def _():
        clear_edges(frames, pitch, rows)

    fill_frames(frames, (oz_ref, oc_ref), pitch, rows)
    for slot in range(2):
        def step(c, _):
            start = pl.multiple_of(c * chunk, chunk)
            part_ref[0, slot, pl.ds(start, chunk), :] = conv_rows(
                lambda i: taps_ref[pl.ds(i, 1), :],
                lambda a, b: frames[slot + a - 1, pl.ds(pl.multiple_of(start + pitch * b, pitch), chunk), :],
                chunk,
                (1, 2) if slot == 0 else (0, 1),
            )
            return 0

        lax.fori_loop(0, rows // chunk, step, 0, unroll=True)


def mid_kernel(
    width, counts_ref, rz_ref, rc_ref, part_ref, taps_ref, up_ref,
    mid_ref, act_ref, act_even_ref, even_ref, moment_ref, gram_up_ref, act_sum_ref,
    frames, acts, evens, gram, total,
):
    k = pl.program_id(0)
    rows = rz_ref.shape[1]
    pitch = 16
    chunk = 2 * pitch
    half = pitch // 2

    @pl.when(k == 0)
    def _():
        clear_edges(frames, pitch, rows)
        gram[...] = jnp.zeros_like(gram)
        total[...] = jnp.zeros_like(total)

    fill_frames(frames, (rz_ref, rc_ref), pitch, rows)
    for slot in range(2):
        def step(c, _):
            start = pl.multiple_of(c * chunk, chunk)
            mid = part_ref[0, slot, pl.ds(start, chunk), :] + conv_rows(
                lambda i: taps_ref[pl.ds(i, 1), :],
                lambda a, b: frames[slot, pl.ds(pl.multiple_of(start + pitch * b, pitch), chunk), :],
                chunk,
                (0,) if slot == 0 else (2,),
            )
            mid_ref[0, slot, pl.ds(start, chunk), :] = mid
            act = jnp.where(valid_rows(mid.shape, pitch, width), gelu(mid), 0.0)
            act_ref[0, slot, pl.ds(start, chunk), :] = act.astype(bf16)
            put_lanes(acts, slot * rows + start, act)
            return 0

        lax.fori_loop(0, rows // chunk, step, 0, unroll=True)
        act = act_ref[0, slot]
        mask = frame_mask(counts_ref, k, frame_of(slot))
        gram[...] += t_dot(act, act) * mask
        total[...] += row_sums(act.astype(f32)) * mask
    for j in range(rows // chunk):
        at = pl.multiple_of(k * (rows // 4) + half * j, half)
        evens[pl.ds(at, half), :] = get_even(acts, frame_of(0) * rows + chunk * j, half)

    @pl.when(k == pl.num_programs(0) - 1)
    def _():
        act_even_ref[...] = evens[...].astype(bf16)
        even_ref[...] = dot(act_even_ref[...], up_ref[...])
        gram_up = sum(dot(part, up_ref[...]) for part in split(gram[...], 3))
        gram_up_ref[...] = gram_up
        act_sum = jnp.sum(total[...], axis=0, keepdims=True)
        act_sum_ref[...] = act_sum
        rows_of_sum = jnp.concatenate(
            [part.astype(f32) for part in split(act_sum, 3)] + [jnp.zeros((5,) + act_sum.shape[1:], f32)], axis=0
        ).astype(bf16)
        moment_ref[0:1] = jnp.sum(dot(rows_of_sum, up_ref[...]), axis=0, keepdims=True)
        moment_ref[1:2] = jnp.sum(gram_up * up_ref[...].astype(f32), axis=0, keepdims=True)


def norm_stats(refs, cells):
    totals = received_sum(refs)
    center = totals[0:1] / cells
    return center, lax.rsqrt(totals[1:2] / cells - center * center + eps)


def entry_kernel(
    width, cells, count, counts_ref, *refs
):
    moments, refs = refs[:count], refs[count:]
    (even_x_ref, even_ref, gain_ref, shift_ref, down_ref, stats_ref, hat_ref, entry_ref, first_ref, act_ref) = refs
    center, scale = norm_stats(moments, cell_total(counts_ref, False, cells))
    stats_ref[0:1] = center
    stats_ref[1:2] = scale
    clips, rows, channels = even_ref.shape
    for k in range(clips):
        hat = (even_ref[k] - center) * scale
        hat_ref[k] = hat
        entry = even_x_ref[k] + hat * gain_ref[...] + shift_ref[...]
        entry = jnp.where(valid_rows(entry.shape, 8, width), entry, 0.0)
        entry_ref[pl.ds(k * rows, rows), :] = entry.astype(bf16)
    late = dot(entry_ref[...], down_ref[...])
    first_ref[...] = late
    for k in range(clips):
        act_ref[k] = (gelu(late[k * rows : (k + 1) * rows]) * frame_mask(counts_ref, k, 0)).astype(bf16)


def late_kernel(
    width, counts_ref, rz_ref, own_ref, rc_ref, taps_ref, up_ref,
    mid_ref, act_ref, sum_ref, moment_ref, frames, wide,
):
    clips, rows, channels = own_ref.shape
    pitch = 8
    edge = jnp.zeros((pitch, channels), f32)
    lanes = 128

    def clip_step(k, _):
        for s, source in enumerate((rz_ref, own_ref, rc_ref)):
            frames[s, pl.ds(0, pitch), :] = edge
            frames[s, pl.ds(pitch + rows, pitch), :] = edge
            frames[s, pl.ds(pitch, rows), :] = source[k].astype(f32)
        for l in range(channels // lanes):
            cols = pl.ds(l * lanes, lanes)
            mid = conv_rows(
                lambda i: taps_ref[pl.ds(i, 1), cols],
                lambda a, b: frames[a, pl.ds(pitch * b, rows), cols],
                rows,
            )
            mid_ref[k, :, cols] = mid
            wide[k, :, cols] = jnp.where(valid_rows(mid.shape, pitch, width), gelu(mid), 0.0)
        return 0

    lax.fori_loop(0, clips, clip_step, 0)
    for k in range(clips):
        act_ref[pl.ds(k * rows, rows), :] = wide[k].astype(bf16)
    late = dot(act_ref[...], up_ref[...]).astype(bf16)
    sum_ref[...] = late
    late = late.astype(f32)
    one = two = None
    for k in range(clips):
        block = late[k * rows : (k + 1) * rows]
        mask = frame_mask(counts_ref, k, 0)
        a, b = row_sums(block) * mask, row_sums(block * block) * mask
        one, two = (a, b) if one is None else (one + a, two + b)
    moment_ref[0:1] = jnp.sum(one, axis=0, keepdims=True)
    moment_ref[1:2] = jnp.sum(two, axis=0, keepdims=True)


def post_kernel(
    width, cells, count, counts_ref, *refs
):
    moments, refs = refs[:count], refs[count:]
    (sum_ref, skip_ref, gain_ref, shift_ref, pooled_grad_ref, stats_ref, back_ref, pooled_ref, pre_ref,
     skip_grad_ref) = refs
    center, scale = norm_stats(moments, cell_total(counts_ref, True, cells))
    stats_ref[0:1] = center
    stats_ref[1:2] = scale
    clips, rows, channels = sum_ref.shape
    one = two = None
    for k in range(clips):
        hat = (sum_ref[k].astype(f32) - center) * scale
        post, slope = gelu_both(hat * gain_ref[...] + shift_ref[...] + skip_ref[k].astype(f32))
        keep = valid_rows(post.shape, 8, width)
        mask = frame_mask(counts_ref, k, 0)
        pool = ((counts_ref[k] + 1) // 2 * cells).astype(f32)
        pooled = jnp.sum(jnp.where(keep, post, 0.0), axis=0, keepdims=True) * mask / pool
        pooled_ref[pl.ds(k, 1)] = pooled
        pre = jnp.where(keep, pooled_grad_ref[pl.ds(k, 1)] * mask / pool * slope, 0.0)
        pre_ref[k] = pre
        skip_grad_ref[k] = pre.astype(bf16)
        a, b = row_sums(pre), row_sums(pre * hat)
        one, two = (a, b) if one is None else (one + a, two + b)
    back_ref[0:1] = jnp.sum(one, axis=0, keepdims=True)
    back_ref[1:2] = jnp.sum(two, axis=0, keepdims=True)


def sum_grad_kernel(
    width, cells, count, counts_ref, *refs
):
    received, refs = refs[:count], refs[count:]
    (stats_ref, sum_ref, pre_ref, gain_ref, up_ref, mid_ref, sum_grad_ref, mid_grad_ref) = refs
    totals = received_sum(received) / cell_total(counts_ref, True, cells)
    center, scale = stats_ref[0:1], stats_ref[1:2]
    lead = gain_ref[...] * scale
    clips, rows, channels = sum_ref.shape
    for k in range(clips):
        hat = (sum_ref[k].astype(f32) - center) * scale
        weight = frame_mask(counts_ref, k, 0)
        grad = lead * (pre_ref[k] - weight * (totals[0:1] + hat * totals[1:2]))
        grad = jnp.where(valid_rows(grad.shape, 8, width), grad, 0.0)
        sum_grad_ref[pl.ds(k * rows, rows), :] = grad.astype(bf16)
    back = dot_t(sum_grad_ref[...], up_ref[...])
    for k in range(clips):
        mid_grad_ref[k] = (back[k * rows : (k + 1) * rows] * gelu_slope(mid_ref[k])).astype(bf16)


def late_back_kernel(
    width, counts_ref, rz_ref, own_ref, rc_ref, taps_ref, first_ref, down_ref, skip_back_ref, hat_ref, logits_ref,
    first_grad_ref, entry_grad_ref, back_ref, frames, grads,
):
    clips, rows, channels = own_ref.shape
    pitch = 8
    edge = jnp.zeros((pitch, channels), f32)
    lanes = 128

    def clip_step(k, _):
        for s, source in enumerate((rz_ref, own_ref, rc_ref)):
            frames[s, pl.ds(0, pitch), :] = edge
            frames[s, pl.ds(pitch + rows, pitch), :] = edge
            frames[s, pl.ds(pitch, rows), :] = source[k].astype(f32)
        for l in range(channels // lanes):
            cols = pl.ds(l * lanes, lanes)
            grad = conv_rows(
                lambda i: taps_ref[pl.ds(26 - i, 1), cols],
                lambda a, b: frames[a, pl.ds(pitch * b, rows), cols],
                rows,
            )
            grad = grad * frame_mask(counts_ref, k, 0) * gelu_slope(first_ref[k, :, cols])
            grads[k, :, cols] = jnp.where(valid_rows(grad.shape, pitch, width), grad, 0.0)
        return 0

    lax.fori_loop(0, clips, clip_step, 0)
    for k in range(clips):
        first_grad_ref[pl.ds(k * rows, rows), :] = grads[k].astype(bf16)
    entry = dot_t(first_grad_ref[...], down_ref[...]) + skip_back_ref[...]
    one = two = None
    for k in range(clips):
        block = entry[k * rows : (k + 1) * rows]
        entry_grad_ref[k] = block
        masked = block * frame_mask(counts_ref, k, 0)
        a, b = row_sums(masked), row_sums(masked * hat_ref[k])
        one, two = (a, b) if one is None else (one + a, two + b)
    back_ref[0:1] = jnp.sum(one, axis=0, keepdims=True)
    back_ref[1:2] = jnp.sum(two, axis=0, keepdims=True)
    back_ref[2:] = logits_ref[...]


def tap_grads(load, grad_of, steps, rows):
    def step(c, totals):
        grad = grad_of(c)
        sides = (pltpu.roll(grad, rows - 1, 0), grad, pltpu.roll(grad, 1, 0))
        new = []
        for a in range(3):
            for b in range(3):
                block = load(c, a, b)
                for e in range(3):
                    new.append(totals[9 * a + 3 * b + e] + row_sums(block * sides[e]))
        return tuple(new)

    return steps, step


def tap_table(rows_of_tap):
    swapped = (lax.axis_index("space") & 1) == 1
    rows = [jnp.where(swapped, rows_of_tap[(2 - i // 9) * 9 + i % 9], rows_of_tap[i]) for i in range(27)]
    table = jnp.concatenate(rows + [jnp.zeros_like(rows[0])] * 5, axis=0)
    table = jnp.transpose(table)
    return jnp.concatenate([table, jnp.zeros((table.shape[0], 96), f32)], axis=1)


def late_taps_kernel(rz_ref, own_ref, rc_ref, grad_ref, out_ref, frames):
    clips, rows, channels = own_ref.shape
    pitch = 8
    edge = jnp.zeros((pitch, channels), f32)
    lanes = 128
    for s, source in enumerate((rz_ref, own_ref, rc_ref)):
        for k in range(clips):
            frames[s, k, pl.ds(0, pitch), :] = edge
            frames[s, k, pl.ds(pitch + rows, pitch), :] = edge
            frames[s, k, pl.ds(pitch, rows), :] = source[k].astype(f32)
    for l in range(channels // lanes):
        cols = pl.ds(l * lanes, lanes)
        steps, step = tap_grads(
            lambda k, a, b: frames[a, k, pl.ds(pitch * b, rows), cols],
            lambda k: grad_ref[k, :, cols].astype(f32),
            clips,
            rows,
        )
        zero = jnp.zeros((8, lanes), f32)
        totals = lax.fori_loop(0, steps, step, (zero,) * 27)
        rows_of_tap = [jnp.sum(total, axis=0, keepdims=True) for total in totals]
        out_ref[cols, :] = tap_table(rows_of_tap)


def third_taps_kernel(
    orders, parts, rz_ref, oz_ref, oc_ref, rc_ref, gz_ref, gc_ref, up_terms_ref, back_ref, third_ref, pooled_ref,
    taps_ref, *refs,
):
    outs, (frames, grads, total, full) = refs[:-4], refs[-4:]
    k = pl.program_id(0)
    rows, channels = oz_ref.shape[1], oz_ref.shape[2]
    pitch = 16
    chunk = 2 * pitch
    lanes = 128

    @pl.when(k == 0)
    def _():
        clear_edges(frames, pitch, rows)
        total[...] = jnp.zeros_like(total)

    fill_frames(frames, (rz_ref, oz_ref, oc_ref, rc_ref), pitch, rows)
    grads[0] = gz_ref[0].astype(f32)
    grads[1] = gc_ref[0].astype(f32)
    count = rows // chunk
    for l in range(channels // lanes):
        cols = pl.ds(l * lanes, lanes)
        totals = tuple(total[i, :, cols] for i in range(27))
        for slot in range(2):
            steps, step = tap_grads(
                lambda c, a, b: frames[
                    slot + a, pl.ds(pl.multiple_of(c * chunk + pitch * b, pitch), chunk), cols
                ],
                lambda c: grads[slot, pl.ds(pl.multiple_of(c * chunk, chunk), chunk), cols],
                count,
                chunk,
            )
            totals = lax.fori_loop(0, steps, step, totals, unroll=True)
        for i in range(27):
            total[i, :, cols] = totals[i]

    @pl.when(k == pl.num_programs(0) - 1)
    def _():
        wide = up_terms_ref.shape[1]
        late_wide = back_ref.shape[1]
        full[:, pl.ds(0, wide)] = up_terms_ref[...].astype(f32)
        full[:, pl.ds(wide, lanes)] = tap_table([jnp.sum(total[i], axis=0, keepdims=True) for i in range(27)])
        own, own_third, own_taps = late_wide // parts, wide // parts, taps_ref.shape[0] // parts
        deep = channels // parts
        clip, space = lax.axis_index("clip"), lax.axis_index("space")
        pooled = pooled_ref[...]
        pooled = jnp.concatenate(
            [jnp.where(clip == g, pooled, 0.0) for g in range(lax.axis_size("clip"))], axis=0
        )
        for d in range(parts):
            at, third_at = d * own // lanes * lanes, d * own_third // lanes * lanes
            block = jnp.concatenate(
                [
                    back_ref[0:2, pl.ds(at, lanes)],
                    third_ref[0:2, pl.ds(third_at, lanes)],
                    jnp.zeros((4, lanes), f32),
                    pooled[:, at : at + lanes],
                    taps_ref[pl.ds(d * own_taps, own_taps), :],
                ],
                axis=0,
            )
            for i in range(block.shape[0] // deep):
                full[pl.ds(d * deep, deep), pl.ds(wide + (1 + i) * lanes, lanes)] = block[i * deep : (i + 1) * deep]
        if orders is None:
            outs[0][...] = full[...].astype(bf16)
        else:
            clip_count, chips = orders
            keep_ref, send_ref = outs
            for b in range(clip_count):
                for z in range(chips):
                    at = ((clip ^ b) * chips + z) * 2
                    mine = pl.multiple_of((at + (space & 1)) * deep, deep)
                    other = pl.multiple_of((at + 1 - (space & 1)) * deep, deep)
                    keep_ref[b, z] = full[pl.ds(mine, deep), :]
                    send_ref[b, z] = full[pl.ds(other, deep), :].astype(bf16)


def third_grad_kernel(
    width, cells, count, counts_ref, *refs
):
    received, refs = refs[:count], refs[count:]
    (stats_ref, gain_ref, entry_grad_ref, up_ref, act_even_ref, act_sum_ref, gram_up_ref, bias_ref, act_ref, mid_ref,
     gz_ref, gc_ref, terms_ref, logits_ref, back_even, mix, shift, placed) = refs
    k = pl.program_id(0)
    rows = act_ref.shape[2]
    pitch = 16
    chunk = 2 * pitch
    half = pitch // 2

    @pl.when(k == 0)
    def _():
        placed[...] = jnp.zeros_like(placed)
        totals = received_sum(received)
        clips, classes = logits_ref.shape
        wide = totals.shape[1] // 2
        for i in range(clips):
            row = totals[2 + i // 2 : 3 + i // 2, i % 2 * wide : i % 2 * wide + classes]
            logits_ref[pl.ds(i, 1)] = row + bias_ref[...]
        totals = totals[0:2] / cell_total(counts_ref, False, cells)
        center, scale = stats_ref[0:1], stats_ref[1:2]
        lead = gain_ref[...] * scale
        slope = -(lead * scale * totals[1:2])
        offset = -(lead * (totals[0:1] - center * scale * totals[1:2]))
        grad = (entry_grad_ref[...] * lead).astype(bf16)
        back_even[...] = dot_t(grad, up_ref[...])
        product = sum(dot_t(part, up_ref[...]) for part in split(up_ref[...].astype(f32) * slope, 2))
        mix[0], mix[1] = split(product, 2)
        offsets = [part.astype(f32) for part in split(offset, 2)]
        sums = [part.astype(f32) for part in split(act_sum_ref[...], 2)]
        none = jnp.zeros((4, offset.shape[1]), f32)
        offset_rows = jnp.concatenate(offsets + offsets + [none], axis=0).astype(bf16)
        none = jnp.zeros((4, act_sum_ref.shape[1]), f32)
        sum_rows = jnp.concatenate([sums[0], sums[0], sums[1], sums[1], none], axis=0).astype(bf16)
        shift[...] = jnp.sum(dot_t(offset_rows, up_ref[...])[0:2], axis=0, keepdims=True)
        terms = t_dot(act_even_ref[...], grad) + t_dot(sum_rows, offset_rows) + gram_up_ref[...] * slope
        terms_ref[...] = terms.astype(bf16)

    for j in range(rows // chunk):
        at = pl.multiple_of(k * (rows // 4) + half * j, half)
        put_even(placed, frame_of(0) * rows + chunk * j, back_even[pl.ds(at, half), :])
    for slot, out in ((0, gz_ref), (1, gc_ref)):
        mask = frame_mask(counts_ref, k, frame_of(slot))
        act = act_ref[0, slot]
        back = (dot(act, mix[0]) + dot(act, mix[1]) + shift[...]) * mask + get_lanes(placed, slot * rows, rows)
        back = back * gelu_slope(mid_ref[0, slot])
        out[0] = jnp.where(valid_rows(back.shape, pitch, width), back, 0.0).astype(bf16)


def first_grad_kernel(
    width, orders, counts_ref, rz_ref, gz_ref, gc_ref, rc_ref, taps_ref, first_ref, x_ref,
    grad_ref, *refs
):
    outs, (frames, xpad, product) = refs[:-3], refs[-3:]
    k = pl.program_id(0)
    rows = gz_ref.shape[1]
    height, width = x_ref.shape[2], x_ref.shape[3]
    pitch = 16
    chunk = 2 * pitch

    @pl.when(k == 0)
    def _():
        clear_edges(frames, pitch, rows)
        xpad[...] = jnp.zeros_like(xpad)
        product[...] = jnp.zeros_like(product)

    fill_frames(frames, (rz_ref, gz_ref, gc_ref, rc_ref), pitch, rows)
    for slot in range(2):
        frame = frame_of(slot)
        for h in range(height):
            xpad[pl.ds(slot * rows + h * pitch, width), :] = x_ref[0, frame, h]
        scale = frame_mask(counts_ref, k, frame)

        def step(c, _):
            start = pl.multiple_of(c * chunk, chunk)
            grad = conv_rows(
                lambda i: taps_ref[pl.ds(26 - i, 1), :],
                lambda a, b: frames[slot + a, pl.ds(pl.multiple_of(start + pitch * b, pitch), chunk), :],
                chunk,
            )
            grad = grad * scale * gelu_slope(first_ref[0, slot, pl.ds(start, chunk), :])
            grad = jnp.where(valid_rows(grad.shape, pitch, width), grad, 0.0)
            grad_ref[0, pl.ds(pl.multiple_of(slot * rows + start, chunk), chunk), :] = grad.astype(bf16)
            return 0

        lax.fori_loop(0, rows // chunk, step, 0, unroll=True)
    product[...] += t_dot(grad_ref[0], xpad[...])

    @pl.when(k == pl.num_programs(0) - 1)
    def _():
        terms = jnp.transpose(product[...])
        if orders is None:
            outs[0][...] = terms.astype(bf16)
        else:
            clips, chips, block = orders
            xpad_rows = terms.reshape(clips * chips * 2, block, terms.shape[1])
            space, clip = lax.axis_index("space"), lax.axis_index("clip")
            keep_ref, send_ref, full = outs[0], outs[1], outs[2]
            full[...] = xpad_rows
            for b in range(clips):
                for z in range(chips):
                    at = ((clip ^ b) * chips + z) * 2
                    keep_ref[b, z] = full[at + (space & 1)]
                    send_ref[b, z] = full[at + 1 - (space & 1)].astype(bf16)


def pair_sum_kernel(keep_ref, got_ref, keep_terms_ref, got_terms_ref, *out_refs):
    wide, inner = keep_terms_ref.shape[-1], keep_ref.shape[-1]
    deep = keep_terms_ref.shape[-2]
    for b, out_ref in enumerate(out_refs):
        out_ref[:, :, pl.ds(0, wide)] = (keep_terms_ref[b] + got_terms_ref[b].astype(f32)).astype(bf16)
        total = keep_ref[b] + got_ref[b].astype(f32)
        for i in range(keep_ref.shape[-2] // deep):
            out_ref[:, :, pl.ds(wide + i * inner, inner)] = total[:, i * deep : (i + 1) * deep].astype(bf16)


def chip_totals_kernel(count, *refs):
    terms, outs = refs[:count], refs[count:]
    for z, out_ref in enumerate(outs):
        at = (lax.axis_index("space") // 2) ^ z
        total = terms[0][at].astype(f32)
        for term in terms[1:]:
            total = total + term[at].astype(f32)
        out_ref[...] = total.astype(bf16)


def finish_kernel(count, *refs):
    skip, up = refs[:count], refs[count : 2 * count]
    skip_ref, up_ref, fourth_down_ref = refs[2 * count :]

    def total(terms):
        return sum(term[...].astype(f32) for term in terms)

    skip_ref[...] = total(skip)
    both = total(up)
    block, lanes = up_ref.shape[0], fourth_down_ref.shape[1]
    up_ref[...] = both[:block]
    part = both.shape[0] - block
    for i in range(both.shape[1] // lanes):
        fourth_down_ref[pl.ds(i * part, part), :] = both[block:, i * lanes : (i + 1) * lanes]


def terms_kernel(
    count, clips, wide, small_rows, *refs
):
    received, refs = refs[:count], refs[count:]
    (grad_ref, up_ref, depth_ref, gain_ref, shift_ref, late_gain_ref, late_shift_ref, late_depth_ref, head_ref,
     *down_refs) = refs
    lanes = 128
    total = None
    for ref in received:
        for i in range(ref.shape[0]):
            total = ref[i].astype(f32) if total is None else total + ref[i].astype(f32)
    deep = total.shape[0]
    up_ref[...] = total[:, :wide]
    depth_ref[...] = total[:, wide : wide + 27]
    device = lax.axis_index("clip") * lax.axis_size("space") + lax.axis_index("space")
    end = wide + lanes * (1 + small_rows // deep)
    small = jnp.concatenate([total[:, i : i + lanes] for i in range(wide + lanes, end, lanes)], axis=0)

    def own_lanes(values, width):
        moved = pltpu.roll(values, (lanes - device * width % lanes) % lanes, 1)
        return moved[:, :width]

    late = own_lanes(small, late_gain_ref.shape[1])
    third = own_lanes(small, gain_ref.shape[1])
    late_gain_ref[...] = late[1:2]
    late_shift_ref[...] = late[0:1]
    gain_ref[...] = third[3:4]
    shift_ref[...] = third[2:3]
    everyone = clips * lax.axis_size("clip")
    late_depth_ref[...] = small[8 + everyone :, :27]
    pooled = late[8 : 8 + everyone].astype(bf16)
    head_ref[...] = sum(t_dot(pooled, part) for part in split(grad_ref[...], 3))
    for down_ref in down_refs:
        inner = down_ref.shape[1]
        for i in range(down_ref.shape[0] // deep):
            down_ref[pl.ds(i * deep, deep), :] = total[:, end + i * inner : end + (i + 1) * inner]


def clip_grad_kernel(grad_ref, down_ref, entry_grad_ref, out_ref, wide):
    _, _, height, width, _ = out_ref.shape
    pitch = 16
    half = pitch // 2
    rows = height * pitch
    for slot in range(2):
        put_lanes(wide, slot * rows, dot_t(grad_ref[0, pl.ds(slot * rows, rows), :], down_ref[...]))
    for j in range(height // 2):
        at = frame_of(0) * rows + 2 * pitch * j
        put_even(wide, at, get_even(wide, at, half) + entry_grad_ref[0, pl.ds(half * j, half), :])
    for slot in range(2):
        frame = frame_of(slot)
        for h in range(height):
            out_ref[0, frame, h] = get_lanes(wide, slot * rows + h * pitch, width).astype(bf16)


kernel_micros = {
    "first": 5.3, "mid_own": 5.0, "mid": 8.6, "entry": 3.4, "late_mid": 4.7, "post": 6.0, "skip_sums": 7.0,
    "sum_grad": 4.6, "late_taps": 3.6, "late_back": 5.0, "up_down_sums": 5.5, "third_grad": 6.7, "third_taps": 7.7,
    "up_down_total": 2.3, "skip_total": 3.0, "skip_phase": 1.0, "up_down_phase": 1.0, "finish": 2.0, "terms": 1.5, "taps": 0.6, "pooled_grad": 1.5, "head": 1.0, "add": 0.6, "skipped": 2.5, "first_grad": 10.7, "pair_sum": 1.9, "clip_sum": 1.6, "clip_grad": 5.5,
}
smem = pl.BlockSpec(memory_space=pltpu.SMEM)


def whole(shape):
    return pl.BlockSpec(shape, lambda k: (0,) * len(shape))


def by_clip(shape):
    return pl.BlockSpec((1,) + shape[1:], lambda k: (k,) + (0,) * (len(shape) - 1))


def cost(micros):
    return pl.CostEstimate(flops=0, bytes_accessed=int(micros * 3.4e6), transcendentals=0)


def call(kernel, name, inputs, outputs, scratch, clips=None, limit=LIMIT):
    if clips is None:
        def spec(kind, shape):
            return smem if kind == "s" else pl.BlockSpec(memory_space=pltpu.VMEM)
    else:
        def spec(kind, shape):
            return smem if kind == "s" else whole(shape) if kind == "w" else by_clip(shape)
    options = {} if clips is None else {"grid": (clips,)}
    return pl.pallas_call(
        kernel,
        name=name,
        out_shape=[jax.ShapeDtypeStruct(s, d) for s, d, _ in outputs],
        in_specs=[spec(kind, a.shape) for a, kind in inputs],
        out_specs=[spec(kind, s) for s, _, kind in outputs],
        scratch_shapes=scratch,
        compiler_params=pltpu.CompilerParams(vmem_limit_bytes=limit * mib),
        cost_estimate=cost(kernel_micros[name]),
        **options,
    )(*[a for a, _ in inputs])


def group_parts(values):
    size = lax.axis_size("space")
    if size != 8:
        copies = jnp.broadcast_to(values[None], (size,) + values.shape)
        return [lax.all_to_all(copies, "space", split_axis=0, concat_axis=0, tiled=True)]
    (pair,) = call(add_kernel, "add", [(values, "w"), (core_swap(values), "w")], [(values.shape, f32, "w")], [])
    return [part[None] for part in over_chips([pair] * 4)]


def w(arrays):
    return [(array, "w") for array in arrays]


def swap_neighbours(to_z, to_core):
    size = lax.axis_size("space")
    core = [(i, i ^ 1) for i in range(size)]
    z = [(i, j) for m in range(1, size - 1, 2) for i, j in ((m, m + 1), (m + 1, m))]
    return lax.ppermute(to_z, "space", z), lax.ppermute(to_core, "space", core)


def reduce_rows(term):
    return add_rows(send_rows(term))


def add_rows(received):
    return jnp.sum(received.astype(f32), axis=0)


def send_rows(term):
    parts = lax.axis_size("clip") * lax.axis_size("space")
    pieces = term.astype(bf16).reshape((parts, term.shape[0] // parts) + term.shape[1:])
    return lax.all_to_all(pieces, ("clip", "space"), split_axis=0, concat_axis=0, tiled=True)


def core_swap(values):
    return lax.ppermute(values, "space", [(i, i ^ 1) for i in range(lax.axis_size("space"))])


def own_rows(left_ref, out, starts):
    out[0] = jnp.transpose(left_ref[...])
    block = out.shape[1] // 2 // len(starts)
    for j, start in enumerate(starts):
        out[1, pl.ds(j * block, block), :] = out[0, pl.ds(pl.multiple_of(start * block, block), block), :]


def own_blocks(orders):
    space, clip = lax.axis_index("space"), lax.axis_index("clip")
    clips, chips = orders
    return [((clip ^ b) * chips + z) * 2 + (space & 1) for b in range(clips) for z in range(chips)]


def place(outs, chips, j, values):
    b, z = j // chips, j % chips
    if z < chips // 2:
        outs[b % 2][b // 2, z] = values.astype(bf16)
    else:
        outs[2 + b // 2][b % 2, z - chips // 2] = values.astype(bf16)


def first_phase(pieces):
    keep_low, send_low, keep_high, send_high = pieces
    return [keep_low, clip_swap(send_low, 1), keep_high, clip_swap(send_high, 2)]


def clip_swap(values, bit):
    return lax.ppermute(values, "clip", [(i, i ^ bit) for i in range(lax.axis_size("clip"))])


def phase_kernel(keep_low_ref, got_low_ref, keep_high_ref, got_high_ref, low_ref, low_send_ref, high_ref, high_send_ref):
    for keep, got, out, send in (
        (keep_low_ref, got_low_ref, low_ref, low_send_ref), (keep_high_ref, got_high_ref, high_ref, high_send_ref)
    ):
        out[...] = (keep[0].astype(f32) + got[0].astype(f32)).astype(bf16)
        send[...] = (keep[1].astype(f32) + got[1].astype(f32)).astype(bf16)


def second_phase(name, pieces):
    shape = pieces[0].shape[1:]
    low, low_send, high, high_send = call(phase_kernel, name, w(pieces), [(shape, bf16, "w")] * 4, [])
    return [low, clip_swap(low_send, 2), high, clip_swap(high_send, 1)]


def halves_total_kernel(low_ref, got_low_ref, high_ref, got_high_ref, *outs):
    half = low_ref.shape[0]
    for z, out_ref in enumerate(outs):
        at = (lax.axis_index("space") // 2) ^ z
        low = low_ref[at % half].astype(f32) + got_low_ref[at % half].astype(f32)
        high = high_ref[at % half].astype(f32) + got_high_ref[at % half].astype(f32)
        out_ref[...] = jnp.where(at < half, low, high).astype(bf16)


def skip_kernel(
    orders, left_ref, left_other_ref, right_ref, right_other_ref, weight_ref, back_ref, *refs
):
    clips, chips = orders
    outs, (left, left_other) = refs[:4], refs[4:]

    @pl.when(pl.program_id(0) == 0)
    def _():
        own_rows(left_ref, left, own_blocks(orders))
        own_rows(left_other_ref, left_other, own_blocks(orders))
        back_ref[...] = jnp.zeros_like(back_ref)

    half = left.shape[1] // 2
    total = dot(left[1, pl.ds(0, half)], right_ref[...]) + dot(left_other[1, pl.ds(0, half)], right_other_ref[...])
    block = half // (clips * chips)
    for j in range(clips * chips):
        place(outs, chips, j, total[j * block : (j + 1) * block])
    back_ref[...] += dot_t(right_ref[...], weight_ref[...])


def skip_sums(left, left_other, right, right_other, weight, parts, orders):
    block = left.shape[1] // parts
    wide = right.shape[1]
    lanes = 512
    rows, deep = left.shape
    return pl.pallas_call(
        functools.partial(skip_kernel, orders),
        name="skip_sums",
        grid=(wide // lanes,),
        out_shape=[
            jax.ShapeDtypeStruct((rows, deep), f32),
            *[jax.ShapeDtypeStruct((2, orders[1] // 2, block, wide), bf16)] * 4,
        ],
        in_specs=[pl.BlockSpec((rows, deep), lambda n: (0, 0))] * 2
        + [pl.BlockSpec((rows, lanes), lambda n: (0, n))] * 2
        + [pl.BlockSpec((deep, lanes), lambda n: (0, n))],
        out_specs=[
            pl.BlockSpec((rows, deep), lambda n: (0, 0)),
            *[pl.BlockSpec((2, orders[1] // 2, block, lanes), lambda n: (0, 0, 0, n))] * 4,
        ],
        scratch_shapes=[pltpu.VMEM((2, deep, rows), bf16)] * 2,
        compiler_params=pltpu.CompilerParams(vmem_limit_bytes=LIMIT * mib),
        cost_estimate=cost(kernel_micros["skip_sums"]),
    )(left, left_other, right, right_other, weight)


def products_kernel(
    orders, act_ref, act_other_ref, entry_ref, entry_other_ref, first_ref, first_other_ref, sum_ref, sum_other_ref,
    *refs
):
    clips, chips = orders
    outs, (act, act_other, entry, entry_other, down) = refs[:4], refs[4:]
    n = pl.program_id(0)

    @pl.when(n == 0)
    def _():
        blocks = own_blocks(orders)
        own_rows(act_ref, act, blocks)
        own_rows(act_other_ref, act_other, blocks)
        own_rows(entry_ref, entry, blocks)
        own_rows(entry_other_ref, entry_other, blocks)
        half = entry.shape[1] // 2
        down[...] = (
            dot(entry[1, pl.ds(0, half)], first_ref[...]) + dot(entry_other[1, pl.ds(0, half)], first_other_ref[...])
        ).reshape(down.shape)

    half = act.shape[1] // 2
    up = dot(act[1, pl.ds(0, half)], sum_ref[...]) + dot(act_other[1, pl.ds(0, half)], sum_other_ref[...])
    block = half // (clips * chips)
    part = outs[0].shape[2] - block
    for j in range(clips * chips):
        under = down[j, pl.ds(pl.multiple_of(n * part, part), part), :]
        place(outs, chips, j, jnp.concatenate([up[j * block : (j + 1) * block], under], axis=0))


def up_down_sums(act, act_other, entry, entry_other, first, first_other, sums, sums_other, parts, orders):
    rows, deep = entry.shape
    inner, wide = act.shape[1], sums.shape[1]
    lanes = inner
    clips, chips = orders
    up_block, down_block = inner // parts, deep // parts
    block = up_block + down_block * inner // wide
    same = lambda n: (0, 0)
    return pl.pallas_call(
        functools.partial(products_kernel, orders),
        name="up_down_sums",
        grid=(wide // lanes,),
        out_shape=[jax.ShapeDtypeStruct((2, chips // 2, block, wide), bf16)] * 4,
        in_specs=[pl.BlockSpec((rows, inner), same)] * 2
        + [pl.BlockSpec((rows, deep), same)] * 2
        + [pl.BlockSpec((rows, inner), same)] * 2
        + [pl.BlockSpec((rows, lanes), lambda n: (0, n))] * 2,
        out_specs=[pl.BlockSpec((2, chips // 2, block, lanes), lambda n: (0, 0, 0, n))] * 4,
        scratch_shapes=[pltpu.VMEM((2, inner, rows), bf16)] * 2
        + [pltpu.VMEM((2, deep, rows), bf16)] * 2
        + [pltpu.VMEM((clips * chips, down_block, inner), f32)],
        compiler_params=pltpu.CompilerParams(vmem_limit_bytes=LIMIT * mib),
        cost_estimate=cost(kernel_micros["up_down_sums"]),
    )(act, act_other, entry, entry_other, first, first_other, sums, sums_other)


def over_clip(pieces):
    size = len(pieces)
    return [pieces[0]] + [lax.ppermute(pieces[b], "clip", [(i, i ^ b) for i in range(size)]) for b in range(1, size)]


def over_chips(pieces):
    size = len(pieces)
    return [pieces[0]] + [
        lax.ppermute(pieces[z], "space", [(i, i ^ (2 * z)) for i in range(2 * size)]) for z in range(1, size)
    ]


def skipped_sums(entry, weight):
    rows, deep = entry.shape
    wide = weight.shape[1]
    lanes = 512
    return pl.pallas_call(
        skipped_kernel,
        name="skipped",
        grid=(wide // lanes,),
        out_shape=jax.ShapeDtypeStruct((rows, wide), bf16),
        in_specs=[pl.BlockSpec((rows, deep), lambda n: (0, 0)), pl.BlockSpec((deep, lanes), lambda n: (0, n))],
        out_specs=pl.BlockSpec((rows, lanes), lambda n: (0, n)),
        compiler_params=pltpu.CompilerParams(vmem_limit_bytes=LIMIT * mib),
        cost_estimate=cost(kernel_micros["skipped"]),
    )(entry, weight)


def after(values, token):
    return lax.optimization_barrier((values, token))[0]


def per_device(
    clip_input, frame_counts, third_down, third_depth, third_up, third_gain, third_shift,
    fourth_down, fourth_skip, fourth_depth, fourth_up, fourth_gain, fourth_shift,
    classifier, class_bias, logit_grad,
):
    clips, frames, height, width, channels = clip_input.shape
    inner = third_down.shape[1]
    late_inner = fourth_down.shape[1]
    late_wide = fourth_up.shape[1]
    half_width = width // 2
    rows = height * 16
    late_rows = height // 2 * 8
    late_all = clips * late_rows
    cells = height * width
    late_cells = (height // 2) * half_width
    parts = lax.axis_size("clip") * lax.axis_size("space")
    clip_axis, chips = lax.axis_size("clip"), lax.axis_size("space") // 2
    by_pairs = clip_axis == 4 and chips == 4 and channels // parts % 32 == 0 and late_inner // parts % 16 == 0
    orders = (clip_axis, chips) if by_pairs else None
    third_gain, third_shift = third_gain[None], third_shift[None]
    fourth_gain, fourth_shift = fourth_gain[None], fourth_shift[None]
    head = jnp.transpose(classifier)

    first, act_z, act_c, even_x = call(
        first_kernel, "first",
        [(frame_counts, "s"), (clip_input, "c"), (third_down, "w")],
        [
            ((clips, 2, rows, inner), f32, "c"),
            ((clips, rows, inner), bf16, "c"),
            ((clips, rows, inner), bf16, "c"),
            ((clips, late_rows, channels), f32, "c"),
        ],
        [pltpu.VMEM((rows, channels), bf16), pltpu.VMEM((channels // 128, 16, 128), f32)],
        clips=clips,
    )
    got_z, got_c = swap_neighbours(act_z, act_c)
    third_taps, late_taps = call(
        taps_kernel, "taps", w([jnp.transpose(third_depth), jnp.transpose(fourth_depth)]),
        [((27, inner), f32, "w"), ((27, late_inner), f32, "w")], [],
    )
    (mid_part,) = call(
        mid_own_kernel, "mid_own",
        [(act_z, "c"), (act_c, "c"), (third_taps, "w")],
        [((clips, 2, rows, inner), f32, "c")],
        [pltpu.VMEM((2, rows + 32, inner), f32)],
        clips=clips,
    )
    mid, mid_act, act_even, even_sum, moments, gram_up, act_sum = call(
        functools.partial(mid_kernel, width), "mid",
        [(frame_counts, "s"), (got_z, "c"), (got_c, "c"), (mid_part, "c"), (third_taps, "w"), (third_up, "w")],
        [
            ((clips, 2, rows, inner), f32, "c"),
            ((clips, 2, rows, inner), bf16, "c"),
            ((late_all, inner), bf16, "w"),
            ((late_all, channels), f32, "w"),
            ((2, channels), f32, "w"),
            ((inner, channels), f32, "w"),
            ((1, inner), f32, "w"),
        ],
        [
            pltpu.VMEM((2, rows + 32, inner), f32),
            pltpu.VMEM((inner // 128, 2 * rows, 128), f32),
            pltpu.VMEM((late_all, inner), f32),
            pltpu.VMEM((inner, inner), f32),
            pltpu.VMEM((8, inner), f32),
        ],
        clips=clips,
    )
    even_sum = even_sum.reshape(clips, late_rows, channels)
    moments = group_parts(moments)
    stats, even_hat, entry, late_first, late_act = call(
        functools.partial(entry_kernel, half_width, cells, len(moments)), "entry",
        [(frame_counts, "s"), *w(moments), (even_x, "w"), (even_sum, "w"),
         (third_gain, "w"), (third_shift, "w"), (fourth_down, "w")],
        [
            ((2, channels), f32, "w"),
            ((clips, late_rows, channels), f32, "w"),
            ((late_all, channels), bf16, "w"),
            ((late_all, late_inner), f32, "w"),
            ((clips, late_rows, late_inner), bf16, "w"),
        ],
        [],
    )
    late_first = late_first.reshape(clips, late_rows, late_inner)
    late_z, late_c = swap_neighbours(late_act, late_act)
    (pooled_grad,) = call(pooled_grad_kernel, "pooled_grad", w([logit_grad, head]), [((clips, late_wide), f32, "w")], [])
    skipped = skipped_sums(entry, fourth_skip).reshape(clips, late_rows, late_wide)
    late_mid, late_mid_act, late_sum, late_moments = call(
        functools.partial(late_kernel, half_width), "late_mid",
        [(frame_counts, "s"), (late_z, "w"), (late_act, "w"), (late_c, "w"), (late_taps, "w"), (fourth_up, "w")],
        [
            ((clips, late_rows, late_inner), f32, "w"),
            ((late_all, late_inner), bf16, "w"),
            ((late_all, late_wide), bf16, "w"),
            ((2, late_wide), f32, "w"),
        ],
        [
            pltpu.VMEM((3, late_rows + 16, late_inner), f32),
            pltpu.VMEM((clips, late_rows, late_inner), f32),
        ],
    )
    late_sum = late_sum.reshape(clips, late_rows, late_wide)
    late_moments = group_parts(late_moments)
    late_stats, late_back, pooled, pre_grad, skip_grad = call(
        functools.partial(post_kernel, half_width, late_cells, len(late_moments)), "post",
        [(frame_counts, "s"), *w(late_moments), (late_sum, "w"), (skipped, "w"),
         (fourth_gain, "w"), (fourth_shift, "w"), (pooled_grad, "w")],
        [
            ((2, late_wide), f32, "w"),
            ((2, late_wide), f32, "w"),
            ((clips, late_wide), f32, "w"),
            ((clips, late_rows, late_wide), f32, "w"),
            ((clips, late_rows, late_wide), bf16, "w"),
        ],
        [],
    )
    received = group_parts(late_back)
    skip_rows = skip_grad.reshape(late_all, late_wide)
    if by_pairs:
        entry_other = core_swap(entry)
        skip_back, *skip_pieces = skip_sums(
            entry, entry_other, skip_rows, core_swap(after(skip_rows, received[0])), fourth_skip, parts, (clip_axis, chips)
        )
    else:
        skip_back = dot_t(skip_rows, fourth_skip)
        fourth_skip_grad = reduce_rows(t_dot(entry, skip_rows))
    late_stats = after(late_stats, skip_back)
    late_sum_grad, late_mid_grad = call(
        functools.partial(sum_grad_kernel, half_width, late_cells, len(received)), "sum_grad",
        [(frame_counts, "s"), *w(received), (late_stats, "w"), (late_sum, "w"), (pre_grad, "w"),
         (fourth_gain, "w"), (fourth_up, "w"), (late_mid, "w")],
        [
            ((late_all, late_wide), bf16, "w"),
            ((clips, late_rows, late_inner), bf16, "w"),
        ],
        [],
    )
    late_gz, late_gc = swap_neighbours(late_mid_grad, late_mid_grad)
    if by_pairs:
        skip_pieces = first_phase(after(skip_pieces, late_mid_grad))
    logit_terms, bias_grad = call(
        head_kernel, "head", w([after(pooled, late_mid_grad), head, logit_grad]),
        [((clips // 2, channels), f32, "w"), ((1, logit_grad.shape[1]), f32, "w")], [],
    )
    late_first = after(late_first, logit_terms)
    (late_taps_table,) = call(
        late_taps_kernel, "late_taps",
        [(late_z, "w"), (late_act, "w"), (late_c, "w"), (late_mid_grad, "w")],
        [((late_inner, 128), f32, "w")],
        [pltpu.VMEM((3, clips, late_rows + 16, late_inner), f32)],
    )
    late_first = after(late_first, late_taps_table)
    late_first_grad, entry_grad, third_back = call(
        functools.partial(late_back_kernel, half_width), "late_back",
        [(frame_counts, "s"), (late_gz, "w"), (late_mid_grad, "w"), (late_gc, "w"), (late_taps, "w"),
         (late_first, "w"), (fourth_down, "w"), (skip_back, "w"), (even_hat, "w"), (logit_terms, "w")],
        [
            ((late_all, late_inner), bf16, "w"),
            ((clips, late_rows, channels), f32, "w"),
            ((2 + clips // 2, channels), f32, "w"),
        ],
        [
            pltpu.VMEM((3, late_rows + 16, late_inner), f32),
            pltpu.VMEM((clips, late_rows, late_inner), f32),
        ],
    )
    received = group_parts(third_back)
    if by_pairs:
        up_pieces = up_down_sums(
            late_mid_act, core_swap(late_mid_act), entry, entry_other, late_first_grad, core_swap(late_first_grad),
            late_sum_grad, core_swap(late_sum_grad), parts, (clip_axis, chips),
        )
        skip_pieces = second_phase("skip_phase", after(skip_pieces, up_pieces[0]))
        stats = after(stats, skip_pieces[0])
    else:
        fourth_up_grad = reduce_rows(t_dot(late_mid_act, late_sum_grad))
        fourth_down_grad = reduce_rows(t_dot(entry, late_first_grad))
    grad_z, grad_c, up_terms, logits = call(
        functools.partial(third_grad_kernel, width, cells, len(received)), "third_grad",
        [(frame_counts, "s"), *w(received), (stats, "w"), (third_gain, "w"),
         (entry_grad.reshape(late_all, channels), "w"), (third_up, "w"), (act_even, "w"), (act_sum, "w"),
         (gram_up, "w"), (class_bias[None], "w"), (mid_act, "c"), (mid, "c")],
        [
            ((clips, rows, inner), bf16, "c"),
            ((clips, rows, inner), bf16, "c"),
            ((inner, channels), bf16, "w"),
            ((clips, logit_grad.shape[1]), f32, "w"),
        ],
        [
            pltpu.VMEM((late_all, inner), f32),
            pltpu.VMEM((2, inner, inner), bf16),
            pltpu.VMEM((1, inner), f32),
            pltpu.VMEM((inner // 128, 2 * rows, 128), f32),
        ],
        clips=clips,
    )
    third_gz, third_gc = swap_neighbours(grad_z, grad_c)
    small_rows = 8 + clips * clip_axis + late_inner // parts
    deep = inner // parts
    extra = 128 * (1 + small_rows // deep)
    if by_pairs:
        term_outputs = [
            ((clip_axis, chips, deep, channels + extra), f32, "w"),
            ((clip_axis, chips, deep, channels + extra), bf16, "w"),
        ]
    else:
        term_outputs = [((inner, channels + extra), bf16, "w")]
    third_terms = call(
        functools.partial(third_taps_kernel, orders, parts), "third_taps",
        [(got_z, "c"), (act_z, "c"), (act_c, "c"), (got_c, "c"), (grad_z, "c"), (grad_c, "c"),
         (up_terms, "w"), (late_back, "w"), (third_back, "w"), (pooled, "w"), (late_taps_table, "w")],
        term_outputs,
        [
            pltpu.VMEM((4, rows + 32, inner), f32),
            pltpu.VMEM((2, rows, inner), f32),
            pltpu.VMEM((27, 8, inner), f32),
            pltpu.VMEM((inner, channels + extra), f32),
        ],
        clips=clips,
    )
    first = after(first, third_terms[0])
    if by_pairs:
        skip_pieces = call(
            halves_total_kernel, "skip_total", w(after(skip_pieces, third_terms[0])),
            [(skip_pieces[0].shape[1:], bf16, "w")] * chips, [],
        )
        first = after(first, skip_pieces[0])
        up_pieces = first_phase(after(up_pieces, third_terms[0]))
        skip_pieces = over_chips(after(skip_pieces, third_terms[0]))
    block = channels // parts
    if by_pairs:
        down_outputs = [
            ((clip_axis, chips, block, inner), f32, "w"),
            ((clip_axis, chips, block, inner), bf16, "w"),
        ]
        down_scratch = [pltpu.VMEM((parts, block, inner), f32)]
    else:
        down_outputs, down_scratch = [((channels, inner), bf16, "w")], []
    first_grad, *down_terms = call(
        functools.partial(first_grad_kernel, width, (clip_axis, chips, block) if by_pairs else None), "first_grad",
        [(frame_counts, "s"), (third_gz, "c"), (grad_z, "c"), (grad_c, "c"), (third_gc, "c"),
         (third_taps, "w"), (first, "c"), (clip_input, "c")],
        [((clips, 2 * rows, inner), bf16, "c"), *down_outputs],
        [
            *down_scratch,
            pltpu.VMEM((4, rows + 32, inner), f32),
            pltpu.VMEM((2 * rows, channels), bf16),
            pltpu.VMEM((inner, channels), f32),
        ],
        clips=clips,
    )
    (clip_grad,) = call(
        clip_grad_kernel, "clip_grad",
        [(first_grad, "c"), (third_down, "w"), (entry_grad, "c")],
        [(clip_input.shape, bf16, "c")],
        [pltpu.VMEM((channels // 128, 2 * rows, 128), f32)],
        clips=clips,
    )
    if by_pairs:
        keep, send = down_terms
        keep_terms, send_terms = third_terms
        up_pieces = second_phase("up_down_phase", after(up_pieces, first_grad))
        clip_parts = call(
            pair_sum_kernel, "pair_sum",
            w([after(keep, clip_grad), core_swap(send), keep_terms, core_swap(after(send_terms, third_gz))]),
            [((chips, deep, channels + extra + block // deep * inner), bf16, "w")] * clip_axis,
            [],
        )
        up_pieces = call(
            halves_total_kernel, "up_down_total", w(after(up_pieces, (clip_parts[0], skip_pieces))),
            [(up_pieces[0].shape[1:], bf16, "w")] * chips, [],
        )
        clip_parts = over_clip(clip_parts)
        up_pieces = over_chips(up_pieces)
        chip_parts = call(
            functools.partial(chip_totals_kernel, clip_axis), "clip_sum", w(after(clip_parts, up_pieces[0])),
            [(clip_parts[0].shape[1:], bf16, "w")] * chips, [],
        )
        third_terms = [part[None] for part in over_chips(chip_parts)]
        up_block = late_inner // parts
        fourth_skip_grad, fourth_up_grad, fourth_down_grad = call(
            functools.partial(finish_kernel, chips), "finish", w(skip_pieces + up_pieces),
            [
                ((block, late_wide), f32, "w"),
                ((up_block, late_wide), f32, "w"),
                ((block, late_inner), f32, "w"),
            ],
            [],
        )
    else:
        third_down_grad = add_rows(send_rows(down_terms[0]))
        third_terms = [send_rows(third_terms[0])]
    own, own_third, own_taps = late_wide // parts, channels // parts, late_inner // parts
    third_up_grad, third_depth_grad, gain, shift, late_gain, late_shift, fourth_depth_grad, classifier_grad, *down = call(
        functools.partial(terms_kernel, len(third_terms), clips, channels, small_rows), "terms",
        w(third_terms + [logit_grad]),
        [
            ((deep, channels), f32, "w"),
            ((deep, 27), f32, "w"),
            ((1, own_third), f32, "w"),
            ((1, own_third), f32, "w"),
            ((1, own), f32, "w"),
            ((1, own), f32, "w"),
            ((own_taps, 27), f32, "w"),
            ((own, logit_grad.shape[1]), f32, "w"),
            *([((block, inner), f32, "w")] if by_pairs else []),
        ],
        [],
    )
    if by_pairs:
        (third_down_grad,) = down
    return (
        logits,
        clip_grad,
        third_down_grad,
        third_depth_grad,
        third_up_grad,
        gain.reshape(-1),
        shift.reshape(-1),
        fourth_down_grad,
        fourth_skip_grad,
        fourth_depth_grad,
        fourth_up_grad,
        late_gain.reshape(-1),
        late_shift.reshape(-1),
        classifier_grad,
        bias_grad.reshape(-1),
    )


def solution(mesh):
    both = ("clip", "space")
    return jax.shard_map(
        per_device,
        mesh=mesh,
        in_specs=(P("clip", "space", None, None, None), P("clip")) + (P(),) * 14,
        out_specs=(
            P("clip", None),
            P("clip", "space", None, None, None),
            P(both, None),
            P(both, None),
            P(both, None),
            P(both),
            P(both),
            P(both, None),
            P(both, None),
            P(both, None),
            P(both, None),
            P(both),
            P(both),
            P(both, None),
            P(),
        ),
        check_vma=False,
    )
```
